256 devices in a mesh: batch: 32 (over x, z), feat: 8 (over y, core).
Axes of the slice: x: 4, y: 4, z: 8, core: 2. Of those that a mesh axis runs over, the one named last changes fastest.
Arguments:
- queries: bfloat16 [4096, 4096], P('batch', 'feat'), may hold values from -8 to 8
- passages: bfloat16 [4096, 4096], P('batch', 'feat'), may hold values from -8 to 8
- positives: int32 [4096], P('batch'), may hold values from 0 to 4095, each once
- level_weight: float32 [7], replicated, may hold values from 0.5 to 2
Outputs:
- loss: float32 [], replicated
- grad_queries: bfloat16 [4096, 4096], P('batch', 'feat')
- grad_passages: bfloat16 [4096, 4096], P('batch', 'feat')
The draws below stay inside these ranges and needn't reach their ends.
Inputs may be any that keep to these rules, and one draw needn't show every extreme that they name: `positives`: each passage is the positive of exactly one query.
All inputs are finite; a program needn't handle non-finite values.
Results may differ from the reference program's by a relative error of at most 0.022.
Values may be sent and summed in bfloat16 or wider, within the bound.
No kernel may reach another device: no remote copies, remote signals or barrier semaphores. Data moves between devices by JAX's collectives and lax.ppermute only.
A program may use at most 128 MiB of HBM per device.

```python
import math
import jax
import jax.numpy as jnp
from jax import lax

D = 4096
SMALLEST = 64
LEVELS = 7
TOTAL = 4096


def draw_queries(key, part):
    key = jax.random.fold_in(key, 7)
    values = jax.random.truncated_normal(key, -8.0, 8.0, (TOTAL, D), jnp.float32)
    return values.astype(jnp.bfloat16)


def draw_passages(key, part):
    key = jax.random.fold_in(key, 13)
    values = jax.random.truncated_normal(key, -8.0, 8.0, (TOTAL, D), jnp.float32)
    return values.astype(jnp.bfloat16)


def setup_inputs(seed: int = 0) -> dict:
    key_list = jax.random.split(jax.random.key(seed), 5)
    queries = draw_queries(jax.random.fold_in(key_list[4], 71), 0)
    passages = draw_passages(jax.random.fold_in(key_list[4], 71), 0)
    positives = jax.random.permutation(key_list[2], TOTAL).astype(jnp.int32)
    level_weight = jnp.clip(jnp.exp(jax.random.uniform(key_list[3], (LEVELS,), jnp.float32, math.log(0.5), math.log(2.0))), 0.5, 2.0)
    return {"queries": queries, "passages": passages, "positives": positives, "level_weight": level_weight}


SHARPNESS = 3.0

def reference(queries, passages, positives, level_weight):
    pair_total = queries.shape[0]
    block_size = math.gcd(pair_total, 512)
    block_count = pair_total // block_size
    widths = [SMALLEST * 2 ** level_id for level_id in range(LEVELS)]
    columns = jnp.arange(pair_total, dtype=jnp.int32)
    contract = (((1,), (1,)), ((), ()))

    def one_block(carried, block_id):
        loss_sum, passage_acc = carried
        first_row = (block_id * block_size).astype(jnp.int32)
        query_block = lax.dynamic_slice_in_dim(queries, first_row, block_size, 0)
        chosen = lax.dynamic_slice_in_dim(positives, first_row, block_size, 0)
        onehot = (columns[None, :] == chosen[:, None]).astype(jnp.float32)
        running = jnp.zeros((block_size, pair_total), jnp.float32)
        level_grads = []
        seg_begin = 0
        for level_id, level_width in enumerate(widths):
            running = running + lax.dot_general(query_block[:, seg_begin:level_width], passages[:, seg_begin:level_width], contract, preferred_element_type=jnp.float32)
            factor = SHARPNESS / math.sqrt(level_width)
            scores = running * factor
            row_max = lax.optimization_barrier(jnp.max(scores, axis=1, keepdims=True))
            log_total = row_max + jnp.log(lax.optimization_barrier(jnp.sum(jnp.exp(scores - row_max), axis=1, keepdims=True)))
            picked = lax.optimization_barrier(jnp.sum(scores * onehot, axis=1, keepdims=True))
            loss_sum = loss_sum + level_weight[level_id] * jnp.sum(log_total - picked)
            level_grads.append(level_weight[level_id] * factor * (jnp.exp(scores - log_total) - onehot))
            seg_begin = level_width
        tail_sum = jnp.zeros((block_size, pair_total), jnp.float32)
        query_parts = []
        passage_parts = []
        for level_id in reversed(range(LEVELS)):
            tail_sum = tail_sum + level_grads[level_id]
            rounded = tail_sum.astype(jnp.bfloat16)
            seg_begin = 0 if level_id == 0 else widths[level_id - 1]
            seg_end = widths[level_id]
            query_parts.insert(0, jnp.dot(rounded, passages[:, seg_begin:seg_end], preferred_element_type=jnp.float32))
            passage_parts.insert(0, jnp.dot(rounded.T, query_block[:, seg_begin:seg_end], preferred_element_type=jnp.float32))
        grad_block = jnp.concatenate(query_parts, axis=1).astype(jnp.bfloat16)
        passage_acc = passage_acc + jnp.concatenate(passage_parts, axis=1)
        return ((loss_sum, passage_acc), grad_block)
    initial = (jnp.zeros((), jnp.float32), jnp.zeros((pair_total, D), jnp.float32))
    finals, grad_blocks = lax.scan(one_block, initial, jnp.arange(block_count, dtype=jnp.int32))
    loss_sum, passage_acc = finals
    return (loss_sum / pair_total, grad_blocks.reshape(pair_total, D), passage_acc.astype(jnp.bfloat16))
```

```python
import math

import jax
import jax.numpy as jnp
from jax import lax
from jax.sharding import PartitionSpec as P

SMALLEST = 64
LEVELS = 7
SHARPNESS = 3.0
WIDTHS = [SMALLEST * 2**k for k in range(LEVELS)]
FACTORS = [SHARPNESS / math.sqrt(w) for w in WIDTHS]

BATCH = 32
FEAT = 8


def shift_x(a, s):
    return lax.ppermute(a, "batch", [(b, (b + 8 * s) % BATCH) for b in range(BATCH)])


def shift_zl(a, s):
    return lax.ppermute(
        a, "batch", [(b, b // 8 * 8 + (b + 2 * s) % 8) for b in range(BATCH)]
    )


def swap_zh(a):
    return lax.ppermute(a, "batch", [(b, b ^ 1) for b in range(BATCH)])


def shift_y(a, s):
    return lax.ppermute(a, "feat", [(f, (f + 2 * s) % FEAT) for f in range(FEAT)])


def swap_core(a):
    return lax.ppermute(a, "feat", [(f, f ^ 1) for f in range(FEAT)])


def dot(a, b, ca, cb):
    return lax.dot_general(
        a, b, (((ca,), (cb,)), ((), ())), preferred_element_type=jnp.float32
    )


def merge(ours, theirs):
    m1, s1, p1 = ours
    m2, s2, p2 = theirs
    m = jnp.maximum(m1, m2)
    return m, s1 * jnp.exp(m1 - m) + s2 * jnp.exp(m2 - m), p1 + p2


def merge_packed(a, b):
    n = a.shape[0] // 3
    cut = lambda v: (v[:n], v[n : 2 * n], v[2 * n :])
    return jnp.concatenate(merge(cut(a), cut(b)), axis=0)


def group_stats(packed):
    packed = merge_packed(packed, swap_zh(packed))
    others = [shift_x(packed, s) for s in (1, 2, 3)]
    packed = merge_packed(
        merge_packed(packed, others[0]), merge_packed(others[1], others[2])
    )
    n = packed.shape[0] // 3
    return packed[:n] + jnp.log(packed[n : 2 * n]), packed[2 * n :]


def level_stats(scores, onehot):
    top = jnp.max(scores, axis=0, keepdims=True)
    e = jnp.exp(scores - top)
    return e, (
        top,
        jnp.sum(e, axis=0, keepdims=True),
        jnp.sum(jnp.where(onehot, scores, 0.0), axis=0, keepdims=True),
    )


def pack(stats):
    return jnp.concatenate([s[i] for i in range(3) for s in stats], axis=0)


def per_device(queries, passages, positives, level_weight):
    n, width = queries.shape
    bi = lax.axis_index("batch")
    fi = lax.axis_index("feat")
    x, zl, zh = bi // 8, bi % 8 // 2, bi % 2
    y, core = fi // 2, fi % 2
    same = zh == core
    d = (x - y + 4) % 4

    def turn(a):
        a = a.reshape(a.shape[0], 2, 4, n)
        blocks = [
            lax.dynamic_index_in_dim(a, (x - i + 4) % 4, 2, True) for i in range(4)
        ]
        return jnp.concatenate(blocks, axis=2).reshape(a.shape[0], 8 * n)

    p_all = jnp.concatenate([passages] + [shift_zl(passages, s) for s in (1, 2, 3)], axis=0)
    q_other = swap_zh(queries)
    q_pair = jnp.stack(
        [jnp.where(same, queries, q_other), jnp.where(same, q_other, queries)]
    )
    pos_other = swap_zh(positives)
    pos_pair = jnp.stack(
        [jnp.where(same, positives, pos_other), jnp.where(same, pos_other, positives)]
    )
    q_all = jnp.stack([q_pair] + [shift_x(q_pair, s) for s in (1, 2, 3)], axis=1)
    q_all = q_all.reshape(8 * n, width)
    pos_all = jnp.stack([pos_pair] + [shift_x(pos_pair, s) for s in (1, 2, 3)], axis=1)
    pos_all = pos_all.reshape(1, 8 * n)
    half = 4 * n

    p_index = jnp.arange(4 * n, dtype=jnp.int32)
    p_ids = (x * 8 + (zl - p_index // n + 4) % 4 * 2 + zh) * n + p_index % n
    onehot = p_ids[:, None] == pos_all

    ends = WIDTHS[:4]
    running = None
    low_scores = []
    for begin, end in zip([0] + ends[:-1], ends):
        part = dot(p_all[:, begin:end], q_all[:, begin:end], 1, 1)
        running = part if running is None else running + part
        low_scores.append(running)

    kept = running[:, :half] + swap_core(running[:, half:])

    def block(a, slot):
        return lax.dynamic_slice_in_dim(a, slot * n, n, axis=1)

    pieces = [block(kept, d)] + [shift_y(block(kept, (d - t + 4) % 4), t) for t in (1, 2, 3)]
    from_y = [(y - t + 4) % 4 for t in range(4)]
    sum4 = sum(jnp.where(src == 0, v, 0.0) for src, v in zip(from_y, pieces))
    sum5 = sum(jnp.where(src <= 1, v, 0.0) for src, v in zip(from_y, pieces))
    sum6 = pieces[0] + pieces[1] + (pieces[2] + pieces[3])
    own_onehot = p_ids[:, None] == lax.dynamic_slice_in_dim(pos_all, d * n, n, axis=1)
    high = [level_stats(s * FACTORS[4 + i], own_onehot) for i, s in enumerate((sum4, sum5, sum6))]
    high_lse, high_picked = group_stats(pack([st for _, st in high]))
    coef = [level_weight[k] * FACTORS[k] for k in range(LEVELS)]
    tails = [None] * 3
    acc = 0.0
    for i in (2, 1, 0):
        e, (top, _, _) = high[i]
        rate = coef[4 + i] * jnp.exp(top - high_lse[i : i + 1])
        acc = acc + (e * rate - jnp.where(own_onehot, coef[4 + i], 0.0))
        tails[i] = acc.astype(jnp.bfloat16)

    low = [level_stats(s * FACTORS[i], onehot) for i, s in enumerate(low_scores)]
    low_lse, low_picked = (
        turn(v) for v in group_stats(turn(pack([st for _, st in low])))
    )
    low_grads = []
    for i in range(4):
        e, (top, _, _) = low[i]
        rate = coef[i] * jnp.exp(top - low_lse[i : i + 1])
        low_grads.append(e * rate - jnp.where(onehot, coef[i], 0.0))

    low_loss = sum(level_weight[i] * jnp.sum(low_lse[i] - low_picked[i]) for i in range(4))
    high_loss = sum(
        level_weight[4 + i] * jnp.sum(high_lse[i] - high_picked[i]) for i in range(3)
    )
    loss = high_loss + jnp.where(fi == 0, low_loss, 0.0)
    loss = jnp.where((x == 0) & (zh == 0), loss, 0.0)
    for axis, size, bits in (("feat", FEAT, (1, 2, 4)), ("batch", BATCH, (1, 2, 4, 8, 16))):
        for bit in bits:
            loss = loss + lax.ppermute(loss, axis, [(i, i ^ bit) for i in range(size)])
    loss = loss / (n * BATCH)

    def tail_for(dst):
        return jnp.where(dst == 0, tails[0], jnp.where(dst == 1, tails[1], tails[2]))

    got = jnp.stack(
        [tail_for(y)] + [shift_y(tail_for((y + t) % 4), t) for t in (1, 2, 3)]
    )
    mine = jnp.concatenate(
        [lax.dynamic_index_in_dim(got, (s - d + 4) % 4, 0, False) for s in range(4)], axis=1
    )
    tail = jnp.concatenate([mine, swap_core(mine)], axis=1)
    grad_tails = [None] * 4
    acc = tail.astype(jnp.float32)
    for i in (3, 2, 1, 0):
        acc = acc + jnp.where(fi == 0, low_grads[i], 0.0)
        grad_tails[i] = acc.astype(jnp.bfloat16)

    spans = list(zip([0] + ends[:-1], ends))
    gq = jnp.concatenate(
        [dot(g, p_all[:, a:b], 0, 0) for g, (a, b) in zip(grad_tails, spans)], axis=1
    ).astype(jnp.bfloat16)
    gp = jnp.concatenate(
        [dot(g, q_all[:, a:b], 1, 0) for g, (a, b) in zip(grad_tails, spans)], axis=1
    ).astype(jnp.bfloat16)

    gq = gq.reshape(2, 4, n, width)
    gq_sum = gq[:, 0].astype(jnp.float32)
    for s in (1, 2, 3):
        gq_sum = gq_sum + shift_x(gq[:, s], -s).astype(jnp.float32)
    theirs = swap_zh(jnp.where(same, gq_sum[1], gq_sum[0]).astype(jnp.bfloat16))
    grad_queries = jnp.where(same, gq_sum[0], gq_sum[1]) + theirs.astype(jnp.float32)

    gp = gp.reshape(4, n, width)
    grad_passages = gp[0].astype(jnp.float32)
    for s in (1, 2, 3):
        grad_passages = grad_passages + shift_zl(gp[s], -s).astype(jnp.float32)
    return loss, grad_queries.astype(jnp.bfloat16), grad_passages.astype(jnp.bfloat16)


def solution(mesh):
    in_specs = (P("batch", "feat"), P("batch", "feat"), P("batch"), P())
    out_specs = (P(), P("batch", "feat"), P("batch", "feat"))
    return jax.shard_map(
        per_device, mesh=mesh, in_specs=in_specs, out_specs=out_specs, check_vma=False
    )
```

```python
import math

import jax
import jax.numpy as jnp
from jax import lax
from jax.sharding import PartitionSpec as P

SMALLEST = 64
LEVELS = 7
LOW = 5
SHARPNESS = 3.0
WIDTHS = [SMALLEST * 2**k for k in range(LEVELS)]
FACTORS = [SHARPNESS / math.sqrt(w) for w in WIDTHS]
SPANS = list(zip([0] + WIDTHS[: LOW - 1], WIDTHS[:LOW]))
EXTRA = 16

BATCH = 32
FEAT = 8
BOTH = ("batch", "feat")
X_GROUPS = [[x * 8 + z for x in range(4)] for z in range(8)]
XZH_GROUPS = [[x * 8 + zl * 2 + zh for x in range(4) for zh in range(2)] for zl in range(4)]
Y_GROUPS = [[y * 2 + c for y in range(4)] for c in range(2)]


def shift_x(a, s):
    return lax.ppermute(a, "batch", [(b, (b + 8 * s) % BATCH) for b in range(BATCH)])


def shift_zl(a, s):
    return lax.ppermute(
        a, "batch", [(b, b // 8 * 8 + (b + 2 * s) % 8) for b in range(BATCH)]
    )


def swap_core(a):
    return lax.ppermute(a, "feat", [(f, f ^ 1) for f in range(FEAT)])


def move_zh(a, first):
    pairs = []
    for b in range(BATCH):
        for f in range(FEAT):
            if (b % 2 == f % 2) == first:
                pairs.append((b * FEAT + f, (b ^ 1) * FEAT + f))
    return lax.ppermute(a, BOTH, pairs)


def dot(a, b, ca, cb):
    return lax.dot_general(
        a, b, (((ca,), (cb,)), ((), ())), preferred_element_type=jnp.float32
    )


def level_stats(scores, onehot):
    top = jnp.max(scores, axis=0, keepdims=True)
    e = jnp.exp(scores - top)
    return e, (
        top,
        jnp.sum(e, axis=0, keepdims=True),
        jnp.sum(jnp.where(onehot, scores, 0.0), axis=0, keepdims=True),
    )


def pack(stats):
    return jnp.concatenate([s[i] for i in range(3) for s in stats], axis=0)


def split_terms(v):
    hi = v.astype(jnp.bfloat16)
    rest = v - hi.astype(jnp.float32)
    mid = rest.astype(jnp.bfloat16)
    lo = (rest - mid.astype(jnp.float32)).astype(jnp.bfloat16)
    return hi, mid, lo


def extra_rows(rows, width):
    out = jnp.concatenate(rows, axis=0)
    return jnp.pad(out, ((0, EXTRA - out.shape[0]), (0, width - out.shape[1])))


def sum_terms(rows):
    rows = rows[:3].astype(jnp.float32)
    return rows[0:1] + rows[1:2] + rows[2:3]


def per_device(queries, passages, positives, level_weight):
    n, width = queries.shape
    bi = lax.axis_index("batch")
    fi = lax.axis_index("feat")
    x, zl, zh = bi // 8, bi % 8 // 2, bi % 2
    y, core = fi // 2, fi % 2
    same = zh == core

    def both_halves(own, other):
        first = jnp.where(core == 0, own, other)
        second = jnp.where(core == 0, other, own)
        return jnp.concatenate([first, second], axis=-1)

    def halves(a):
        first, second = a[..., :width], a[..., width:]
        return jnp.where(core == 0, first, second), jnp.where(core == 0, second, first)

    def place(own, others, index):
        out = jnp.zeros((4,) + own.shape, own.dtype)
        for s, block in enumerate([own] + others):
            out = lax.dynamic_update_slice_in_dim(out, block[None], (index - s + 4) % 4, 0)
        return out

    rows = jnp.stack([positives // 64, positives % 64]).astype(jnp.bfloat16)
    q_chip = jnp.concatenate(
        [both_halves(queries, swap_core(queries)), extra_rows([rows], 2 * width)], axis=0
    )
    q_msg = jnp.where(same, q_chip, move_zh(q_chip, True))
    q_msgs = place(q_msg, [shift_x(q_msg, s) for s in (1, 2, 3)], x)
    q = q_msgs[:, :n]
    pos = q_msgs[:, n : n + 2, :n].astype(jnp.int32)
    pos = pos[:, 0] * 64 + pos[:, 1]

    p_half = place(passages, [shift_zl(passages, s) for s in (1, 2, 3)], zl)
    p_half = p_half.reshape(4 * n, width)
    p = both_halves(p_half, swap_core(p_half))

    p_index = jnp.arange(4 * n, dtype=jnp.int32)
    p_ids = (x * 8 + p_index // n * 2 + zh) * n + p_index % n
    onehot = p_ids[:, None] == pos.reshape(1, 4 * n)

    partial = jnp.stack([dot(p, q[j], 1, 1) for j in range(4)])
    pieces = lax.all_to_all(partial, "feat", 0, 0, axis_index_groups=Y_GROUPS)

    sum5 = pieces[0] + pieces[1]
    sum6 = sum5 + (pieces[2] + pieces[3])
    own_onehot = p_ids[:, None] == lax.dynamic_slice_in_dim(pos, y, 1, axis=0)
    high = [level_stats(s * FACTORS[LOW + i], own_onehot) for i, s in enumerate((sum5, sum6))]

    q_rows = q.reshape(4 * n, 2 * width)
    running = None
    low = []
    for i, (begin, end) in enumerate(SPANS):
        part = dot(p[:, begin:end], q_rows[:, begin:end], 1, 1)
        running = part if running is None else running + part
        low.append(level_stats(running * FACTORS[i], onehot))

    low_stats = pack([st for _, st in low]).reshape(3 * LOW * 4, n)
    stats = jnp.concatenate([low_stats, pack([st for _, st in high])], axis=0)
    stats = jnp.pad(stats, ((0, -stats.shape[0] % 8), (0, 0)))
    stats = lax.all_to_all(
        jnp.broadcast_to(stats[None], (8,) + stats.shape),
        "batch", 0, 0, axis_index_groups=XZH_GROUPS,
    )

    def merge(v, levels):
        v = v.reshape(8, 3, levels, -1)
        top = jnp.max(v[:, 0], axis=0)
        total = jnp.sum(v[:, 1] * jnp.exp(v[:, 0] - top), axis=0)
        return top + jnp.log(total), jnp.sum(v[:, 2], axis=0)

    cut = 3 * LOW * 4
    low_lse, low_picked = merge(stats[:, :cut], LOW)
    high_lse, high_picked = merge(stats[:, cut : cut + 6], 2)
    coef = [level_weight[k] * FACTORS[k] for k in range(LEVELS)]

    def grad(e, top, lse, k, hot):
        return e * (coef[k] * jnp.exp(top - lse)) - jnp.where(hot, coef[k], 0.0)

    tail6 = grad(high[1][0], high[1][1][0], high_lse[1:2], 6, own_onehot)
    tail5 = tail6 + grad(high[0][0], high[0][1][0], high_lse[0:1], 5, own_onehot)

    low_loss = sum(level_weight[i] * jnp.sum(low_lse[i] - low_picked[i]) for i in range(LOW))
    high_loss = sum(
        level_weight[LOW + i] * jnp.sum(high_lse[i] - high_picked[i]) for i in range(2)
    )
    loss = high_loss + jnp.where(y == 0, low_loss, 0.0)
    lane = jnp.arange(n, dtype=jnp.int32)[None, :]
    loss_rows = extra_rows(split_terms(jnp.where(lane == zl * FEAT + fi, loss, 0.0)), n)

    t5 = jnp.concatenate([tail5.astype(jnp.bfloat16), loss_rows], axis=0)
    t6 = jnp.concatenate([tail6.astype(jnp.bfloat16), loss_rows], axis=0)
    got = lax.all_to_all(
        jnp.stack([t5, t5, t6, t6]), "feat", 0, 0, axis_index_groups=Y_GROUPS
    )
    loss_vec = sum(sum_terms(got[j, 4 * n :]) for j in range(4))
    tail = jnp.concatenate([got[j, : 4 * n] for j in range(4)], axis=1)

    acc = tail.astype(jnp.float32)
    tails = [None] * LOW
    for i in reversed(range(LOW)):
        e, (top, _, _) = low[i]
        g = grad(e, top, low_lse[i : i + 1], i, onehot)
        acc = acc + jnp.where(y == 0, g, 0.0)
        tails[i] = acc.astype(jnp.bfloat16)

    gp = jnp.concatenate(
        [dot(t, q_rows[:, a:b], 1, 0) for t, (a, b) in zip(tails, SPANS)], axis=1
    )
    gp_own, gp_other = halves(gp)
    gp = gp_own + swap_core(gp_other.astype(jnp.bfloat16)).astype(jnp.float32)
    gp = gp.reshape(4, n, width).astype(jnp.bfloat16)
    gp_loss = swap_core(loss_vec) + loss_vec
    gp_rows = extra_rows(split_terms(gp_loss), width)

    def passage_message(index):
        block = lax.dynamic_index_in_dim(gp, index, 0, False)
        return jnp.concatenate([block, gp_rows], axis=0)

    others = [shift_zl(passage_message((zl - s + 4) % 4), -s) for s in (1, 2, 3)]
    grad_passages = lax.dynamic_index_in_dim(gp, zl, 0, False).astype(jnp.float32)
    for other in others:
        grad_passages = grad_passages + other[:n].astype(jnp.float32)
    loss_vec = gp_loss + sum(sum_terms(other[n:, :n]) for other in others)
    loss = jnp.sum(loss_vec) / (n * BATCH)

    gq = jnp.concatenate(
        [dot(t, p[:, a:b], 0, 0) for t, (a, b) in zip(tails, SPANS)], axis=1
    )
    gq = gq.astype(jnp.bfloat16).reshape(4, n, 2 * width)
    block = lambda i: lax.dynamic_index_in_dim(gq, i, 0, False)
    gq_sum = block(x).astype(jnp.float32)
    for s in (1, 2, 3):
        gq_sum = gq_sum + shift_x(block((x - s + 4) % 4), -s).astype(jnp.float32)
    gq_sum = gq_sum + move_zh(gq_sum.astype(jnp.bfloat16), False).astype(jnp.float32)
    gq_own, gq_other = halves(gq_sum.astype(jnp.bfloat16))
    grad_queries = jnp.where(same, gq_own, swap_core(gq_other))
    return loss, grad_queries, grad_passages.astype(jnp.bfloat16)


def solution(mesh):
    in_specs = (P("batch", "feat"), P("batch", "feat"), P("batch"), P())
    out_specs = (P(), P("batch", "feat"), P("batch", "feat"))
    return jax.shard_map(
        per_device, mesh=mesh, in_specs=in_specs, out_specs=out_specs, check_vma=False
    )
```

```python
import math

import jax
import jax.numpy as jnp
from jax import lax
from jax.experimental import pallas as pl
from jax.experimental.pallas import tpu as pltpu
from jax.sharding import PartitionSpec as P

SMALLEST = 64
LEVELS = 7
LOW = 5
SHARPNESS = 3.0
WIDTHS = [SMALLEST * 2**k for k in range(LEVELS)]
FACTORS = [SHARPNESS / math.sqrt(w) for w in WIDTHS]
SPANS = list(zip([0] + WIDTHS[: LOW - 1], WIDTHS[:LOW]))
EXTRA = 16
PAIR = 2 * SMALLEST

BATCH = 32
FEAT = 8
BOTH = ("batch", "feat")
XZH_GROUPS = [[x * 8 + zl * 2 + zh for x in range(4) for zh in range(2)] for zl in range(4)]
Y_GROUPS = [[y * 2 + c for y in range(4)] for c in range(2)]
X, Y, ZL, ZH, CORE = range(5)

f32 = jnp.float32
bf16 = jnp.bfloat16


def shift_x(a, s):
    return lax.ppermute(a, "batch", [(b, (b + 8 * s) % BATCH) for b in range(BATCH)])


def shift_zl(a, s):
    return lax.ppermute(
        a, "batch", [(b, b // 8 * 8 + (b + 2 * s) % 8) for b in range(BATCH)]
    )


def shift_y(a, s):
    return lax.ppermute(a, "feat", [(f, (f + 2 * s) % FEAT) for f in range(FEAT)])


def swap_core(a):
    return lax.ppermute(a, "feat", [(f, f ^ 1) for f in range(FEAT)])


def move_zh(a, first):
    pairs = []
    for b in range(BATCH):
        for f in range(FEAT):
            if (b % 2 == f % 2) == first:
                pairs.append((b * FEAT + f, (b ^ 1) * FEAT + f))
    return lax.ppermute(a, BOTH, pairs)


def dot(a, b, ca, cb):
    return lax.dot_general(
        a, b, (((ca,), (cb,)), ((), ())), preferred_element_type=f32
    )


def shape(*dims_dtype):
    return jax.ShapeDtypeStruct(dims_dtype[:-1], dims_dtype[-1])


def call(body, smem, args, outs, scratch=(), flops=0):
    vmem = pl.BlockSpec(memory_space=pltpu.VMEM)
    scalar = pl.BlockSpec(memory_space=pltpu.SMEM)
    moved = sum(a.size * a.dtype.itemsize for a in (*args, *outs))
    return pl.pallas_call(
        body,
        out_shape=outs,
        in_specs=[scalar] * len(smem) + [vmem] * len(args),
        out_specs=[vmem] * len(outs),
        scratch_shapes=list(scratch),
        cost_estimate=pl.CostEstimate(
            flops=flops, bytes_accessed=moved, transcendentals=0
        ),
        compiler_params=pltpu.CompilerParams(vmem_limit_bytes=40 << 20),
    )(*smem, *args)


def find_positives(ids, pos, n):
    rows = lax.broadcasted_iota(jnp.int32, (4 * n, n), 0)
    bits = n.bit_length() - 1
    block = ids[X] * 8 + ids[ZH] + 2 * ((ids[ZL] + 4 - (rows >> bits)) & 3)
    return (block << bits) + (rows & (n - 1)) == pos


def score_kernel(ids, p_own, p_other, q0, q1, q2, q3, partial, p, q_all, pos):
    n = q_all.shape[1]
    width = p_own.shape[1]

    @pl.when(ids[CORE] == 0)
    def _():
        p[:, :width] = p_own[...]
        p[:, width:] = p_other[...]

    @pl.when(ids[CORE] != 0)
    def _():
        p[:, :width] = p_other[...]
        p[:, width:] = p_own[...]

    for s, q in enumerate((q0, q1, q2, q3)):
        j = (ids[X] + 4 - s) & 3
        q_all[j] = q[:n]
        digits = q[n:, :n].astype(f32)
        pos[j] = (digits[0:1] * 64.0 + digits[1:2]).astype(jnp.int32)
        partial[j] = dot(p[...], q[:n], 1, 1)


def low_kernel(ids, p, q_all, pos, e_low, stats):
    n = q_all.shape[1]
    first = lax.broadcasted_iota(jnp.int32, (n, PAIR), 1) < SMALLEST
    for j in range(4):
        hot = find_positives(ids, pos[j], n)
        tops, sums, picks = [], [], []
        running = None
        for k, (begin, end) in enumerate(SPANS):
            if k == 0:
                q_part = q_all[j, :, :PAIR]
                q_part = jnp.where(first, q_part, jnp.zeros_like(q_part))
                running = dot(p[:, :PAIR], q_part, 1, 1)
            elif k == 1:
                running = dot(p[:, :PAIR], q_all[j, :, :PAIR], 1, 1)
            else:
                running = running + dot(p[:, begin:end], q_all[j, :, begin:end], 1, 1)
            scores = running * FACTORS[k]
            top = jnp.max(scores, axis=0, keepdims=True)
            e = jnp.exp(scores - top)
            e_low[k, j] = e
            tops.append(top)
            sums.append(jnp.sum(e, axis=0, keepdims=True))
            picks.append(jnp.sum(jnp.where(hot, scores, 0.0), axis=0, keepdims=True))
        stats[j] = jnp.concatenate(tops + sums + picks + [tops[0]], axis=0)


def owner_kernel(ids, pieces, pos, low_stats, e_high, message):
    n = pos.shape[2]
    hot = find_positives(ids, pos[ids[Y]], n)
    sum5 = pieces[0] + pieces[1]
    sum6 = sum5 + (pieces[2] + pieces[3])
    rows = []
    for i, total in enumerate((sum5, sum6)):
        scores = total * FACTORS[LOW + i]
        top = jnp.max(scores, axis=0, keepdims=True)
        e = jnp.exp(scores - top)
        e_high[i] = e
        rows += [
            top,
            jnp.sum(e, axis=0, keepdims=True),
            jnp.sum(jnp.where(hot, scores, 0.0), axis=0, keepdims=True),
        ]
    high = jnp.concatenate(rows + rows[:2], axis=0)
    for i in range(8):
        for j in range(4):
            message[i, 16 * j : 16 * j + 16] = low_stats[j]
        message[i, 64:72] = high


def put_terms(ref, row, v):
    hi = v.astype(bf16).astype(f32)
    mid = (v - hi).astype(bf16).astype(f32)
    lo = v - hi - mid
    zero = jnp.zeros((EXTRA - 3, v.shape[1]), f32)
    ref[row:, : v.shape[1]] = jnp.concatenate([hi, mid, lo, zero], axis=0).astype(bf16)


def tail_kernel(ids, weight, stats, local, e_high, pos, m0, m1, m2, m3, rates):
    n = pos.shape[2]

    def merged(top, total, picked):
        best = jnp.max(top, axis=0)
        mass = jnp.sum(total * jnp.exp(top - best[None]), axis=0)
        return best + jnp.log(mass), jnp.sum(picked, axis=0)

    on = ids[Y] == 0
    low_loss = jnp.zeros((1, n), f32)
    for j in range(4):
        at = 16 * j
        lse, picked = merged(
            stats[:, at : at + 5], stats[:, at + 5 : at + 10], stats[:, at + 10 : at + 15]
        )
        rows = []
        for k in range(LOW):
            low_loss += weight[k] * (lse[k : k + 1] - picked[k : k + 1])
            scale = jnp.where(on, weight[k] * FACTORS[k], 0.0)
            rows.append(scale * jnp.exp(local[at + k : at + k + 1] - lse[k : k + 1]))
        rates[j] = jnp.concatenate(rows + rows[:3], axis=0)

    hot = find_positives(ids, pos[ids[Y]], n)
    loss = jnp.where(on, low_loss, 0.0)
    tail = None
    tails = []
    for i in (1, 0):
        at = 64 + 3 * i
        lse, picked = merged(
            stats[:, at : at + 1], stats[:, at + 1 : at + 2], stats[:, at + 2 : at + 3]
        )
        loss += weight[LOW + i] * (lse - picked)
        scale = weight[LOW + i] * FACTORS[LOW + i]
        rate = scale * jnp.exp(local[at : at + 1] - lse)
        g = e_high[i] * rate - jnp.where(hot, scale, 0.0)
        tail = g if tail is None else tail + g
        tails.append(tail.astype(bf16))
    lane = lax.broadcasted_iota(jnp.int32, (1, n), 1)
    mine = ids[ZL] * FEAT + ids[Y] * 2 + ids[CORE]
    loss = jnp.where(lane == mine, jnp.sum(loss, axis=1, keepdims=True), 0.0)
    for t, m in enumerate((m0, m1, m2, m3)):
        narrow = ((ids[Y] + t) & 3) <= 1

        @pl.when(narrow)
        def _():
            m[: 4 * n] = tails[1]

        @pl.when(jnp.logical_not(narrow))
        def _():
            m[: 4 * n] = tails[0]

        put_terms(m, 4 * n, loss)


def get_terms(ref, row, lanes):
    v = ref[row:, :lanes].astype(f32)
    return v[0:1] + v[1:2] + v[2:3]


def grad_kernel(
    ids, weight, t0, t1, t2, t3, e_low, rates, pos, p, q_all,
    gq0, gq1, gq2, gq3, gp_own, gp_message, tails, gq,
):
    n = pos.shape[2]
    width = gp_own.shape[1]
    on = ids[Y] == 0
    loss = jnp.zeros((1, n), f32)
    for t, ref in enumerate((t0, t1, t2, t3)):
        j = (ids[Y] + 4 - t) & 3
        lanes = pl.ds(pl.multiple_of(j * n, n), n)
        loss += get_terms(ref, 4 * n, n)
        hot = find_positives(ids, pos[j], n)
        acc = ref[: 4 * n].astype(f32)
        for k in reversed(range(LOW)):
            scale = jnp.where(on, weight[k] * FACTORS[k], 0.0)
            acc = acc + (e_low[k, j] * rates[j, k : k + 1] - jnp.where(hot, scale, 0.0))
            tails[k, :, lanes] = acc.astype(bf16)

    q = q_all[...].reshape(4 * n, 2 * width)
    first = lax.broadcasted_iota(jnp.int32, (4 * n, PAIR), 1) < SMALLEST

    def by_span(fn):
        yield 0, PAIR, jnp.where(first, fn(0, 0, PAIR), fn(1, 0, PAIR))
        for k in range(2, LOW):
            begin, end = SPANS[k]
            yield begin, end, fn(k, begin, end)

    for begin, end, v in by_span(lambda k, a, b: dot(tails[k], q[:, a:b], 1, 0)):
        mine = (begin < width) == (ids[CORE] == 0)
        at = begin % width

        @pl.when(mine)
        def _():
            gp_own[:, at : at + end - begin] = v

        @pl.when(jnp.logical_not(mine))
        def _():
            gp_message[: 4 * n, at : at + end - begin] = v.astype(bf16)

    gp_message[4 * n :] = jnp.zeros((EXTRA, width), bf16)
    put_terms(gp_message, 4 * n, loss)
    for begin, end, v in by_span(lambda k, a, b: dot(tails[k], p[:, a:b], 0, 0)):
        gq[:, begin:end] = v
    for s, out in enumerate((gq0, gq1, gq2, gq3)):
        j = (ids[X] + 4 - s) & 3
        out[...] = gq[pl.ds(pl.multiple_of(j * n, n), n), :].astype(out.dtype)


def core_sum_kernel(gp_own, own_message, other_message, own, m1, m2, m3, loss):
    n, width = own.shape
    total = get_terms(own_message, 4 * n, n) + get_terms(other_message, 4 * n, n)
    loss[...] = jnp.broadcast_to(total, loss.shape)
    for s, out in enumerate((own, m1, m2, m3)):
        rows = slice(s * n, s * n + n)
        v = gp_own[rows] + other_message[rows].astype(f32)
        out[:n] = v.astype(out.dtype)
        if s:
            out[n:] = jnp.zeros((EXTRA, width), bf16)
            put_terms(out, n, total)


def per_device(queries, passages, positives, level_weight):
    n, width = queries.shape
    wide = 2 * width
    bi = lax.axis_index("batch")
    fi = lax.axis_index("feat")
    core = fi % 2
    same = bi % 2 == core
    ids = jnp.stack([bi // 8, fi // 2, bi % 8 // 2, bi % 2, core]).astype(jnp.int32)

    q_core = swap_core(queries)
    rows = jnp.stack([positives // 64, positives % 64]).astype(bf16)
    q_chip = jnp.concatenate(
        [
            jnp.concatenate(
                [jnp.where(core == 0, queries, q_core), jnp.where(core == 0, q_core, queries)],
                axis=1,
            ),
            jnp.pad(rows, ((0, EXTRA - 2), (0, wide - n))),
        ],
        axis=0,
    )
    q_msg = jnp.where(same, q_chip, move_zh(q_chip, True))
    q_msgs = [q_msg] + [shift_x(q_msg, s) for s in (1, 2, 3)]

    p_half = jnp.concatenate([passages] + [shift_zl(passages, s) for s in (1, 2, 3)], axis=0)
    p_other = swap_core(p_half)

    tile = 4 * n * 4 * n
    partial, p, q, pos = call(
        score_kernel, [ids], [p_half, p_other, *q_msgs],
        [
            shape(4, 4 * n, n, f32),
            shape(4 * n, wide, bf16),
            shape(4, n, wide, bf16),
            shape(4, 1, n, jnp.int32),
        ],
        flops=2 * tile * wide,
    )
    pieces = lax.all_to_all(partial, "feat", 0, 0, axis_index_groups=Y_GROUPS)
    e_low, low_stats = call(
        low_kernel, [ids], [p, q, pos],
        [shape(LOW, 4, 4 * n, n, f32), shape(4, 16, n, f32)],
        flops=2 * tile * wide,
    )
    e_high, message = call(
        owner_kernel, [ids], [pieces, pos, low_stats],
        [shape(2, 4 * n, n, f32), shape(8, 72, n, f32)],
    )
    stats = lax.all_to_all(message, "batch", 0, 0, axis_index_groups=XZH_GROUPS)
    *tails, rates = call(
        tail_kernel, [ids, level_weight], [stats, message[0], e_high, pos],
        [shape(4 * n + EXTRA, n, bf16)] * 4 + [shape(4, 8, n, f32)],
    )
    tails = [tails[0]] + [shift_y(tails[t], t) for t in (1, 2, 3)]
    *gq, gp_own, gp_message = call(
        grad_kernel, [ids, level_weight], [*tails, e_low, rates, pos, p, q],
        [shape(n, wide, f32)]
        + [shape(n, wide, bf16)] * 3
        + [shape(4 * n, width, f32), shape(4 * n + EXTRA, width, bf16)],
        scratch=[pltpu.VMEM((LOW, 4 * n, 4 * n), bf16), pltpu.VMEM((4 * n, wide), f32)],
        flops=4 * tile * wide,
    )

    own, *messages, loss_row = call(
        core_sum_kernel, [], [gp_own, gp_message, swap_core(gp_message)],
        [shape(n, width, f32)] + [shape(n + EXTRA, width, bf16)] * 3 + [shape(8, n, f32)],
    )
    grad_passages = own
    loss_row = loss_row[0]
    for s, message in zip((1, 2, 3), messages):
        other = shift_zl(message, -s).astype(f32)
        grad_passages = grad_passages + other[:n]
        loss_row = loss_row + (other[n, :n] + other[n + 1, :n] + other[n + 2, :n])
    loss = jnp.sum(loss_row) / (n * BATCH)

    gq_sum = gq[0]
    for s in (1, 2, 3):
        gq_sum = gq_sum + shift_x(gq[s], -s).astype(f32)
    gq_sum = gq_sum + move_zh(gq_sum.astype(bf16), False).astype(f32)
    gq_sum = gq_sum.astype(bf16)
    left, right = gq_sum[:, :width], gq_sum[:, width:]
    other = swap_core(jnp.where(core == 0, right, left))
    grad_queries = jnp.where(same, jnp.where(core == 0, left, right), other)
    return loss, grad_queries, grad_passages.astype(bf16)


def solution(mesh):
    in_specs = (P("batch", "feat"), P("batch", "feat"), P("batch"), P())
    out_specs = (P(), P("batch", "feat"), P("batch", "feat"))
    return jax.shard_map(
        per_device, mesh=mesh, in_specs=in_specs, out_specs=out_specs, check_vma=False
    )
```

```python
import math

import jax
import jax.numpy as jnp
from jax import lax
from jax.experimental import pallas as pl
from jax.experimental.pallas import tpu as pltpu
from jax.sharding import PartitionSpec as P

SMALLEST = 64
LEVELS = 7
LOW = 5
SHARPNESS = 3.0
WIDTHS = [SMALLEST * 2**k for k in range(LEVELS)]
FACTORS = [SHARPNESS / math.sqrt(w) for w in WIDTHS]
SPANS = list(zip([0] + WIDTHS[: LOW - 1], WIDTHS[:LOW]))
EXTRA = 16
PAIR = 2 * SMALLEST

BATCH = 32
FEAT = 8
BOTH = ("batch", "feat")
XZH_GROUPS = [[x * 8 + zl * 2 + zh for x in range(4) for zh in range(2)] for zl in range(4)]
Y_GROUPS = [[y * 2 + c for y in range(4)] for c in range(2)]
X, Y, ZL, ZH, CORE = range(5)

f32 = jnp.float32
bf16 = jnp.bfloat16


def shift_x(a, s):
    return lax.ppermute(a, "batch", [(b, (b + 8 * s) % BATCH) for b in range(BATCH)])


def shift_zl(a, s):
    return lax.ppermute(
        a, "batch", [(b, b // 8 * 8 + (b + 2 * s) % 8) for b in range(BATCH)]
    )


def shift_y(a, s):
    return lax.ppermute(a, "feat", [(f, (f + 2 * s) % FEAT) for f in range(FEAT)])


def swap_core(a):
    return lax.ppermute(a, "feat", [(f, f ^ 1) for f in range(FEAT)])


def move_square(a, rule):
    pairs = []
    for b in range(BATCH):
        for f in range(FEAT):
            to = rule(b % 2, f % 2)
            if to is not None:
                pairs.append((b * FEAT + f, (b - b % 2 + to[0]) * FEAT + f - f % 2 + to[1]))
    return lax.ppermute(a, BOTH, pairs)


def dot(a, b, ca, cb):
    return lax.dot_general(
        a, b, (((ca,), (cb,)), ((), ())), preferred_element_type=f32
    )


def shape(*dims_dtype):
    return jax.ShapeDtypeStruct(dims_dtype[:-1], dims_dtype[-1])


def call(body, smem, args, outs, scratch=(), flops=0, grant=8):
    vmem = pl.BlockSpec(memory_space=pltpu.VMEM)
    scalar = pl.BlockSpec(memory_space=pltpu.SMEM)
    moved = sum(a.size * a.dtype.itemsize for a in (*args, *outs))
    return pl.pallas_call(
        body,
        out_shape=outs,
        in_specs=[scalar] * len(smem) + [vmem] * len(args),
        out_specs=[vmem] * len(outs),
        scratch_shapes=list(scratch),
        cost_estimate=pl.CostEstimate(
            flops=flops, bytes_accessed=moved, transcendentals=0
        ),
        compiler_params=pltpu.CompilerParams(vmem_limit_bytes=grant << 20),
    )(*smem, *args)


def find_positives(ids, pos, n):
    rows = lax.broadcasted_iota(jnp.int32, (4 * n, n), 0)
    bits = n.bit_length() - 1
    block = ids[X] * 8 + ids[ZH] + 2 * ((ids[ZL] + 4 - (rows >> bits)) & 3)
    return (block << bits) + (rows & (n - 1)) == pos


def pack_kernel(ids, own, near, far, out):
    n, width = near.shape
    same = ids[ZH] == ids[CORE]

    def put(first, second, rows):
        out[:n, :width] = first[:n]
        out[:n, width:] = second[:n]
        out[n:, :width] = rows[n:]

    out[n:, width:] = jnp.zeros((EXTRA, width), bf16)
    for core in (0, 1):
        for matches in (True, False):
            a, b = (own, near) if matches else (near, far)
            if core:
                a, b = b, a

            @pl.when((ids[CORE] == core) & (same == matches))
            def _():
                put(a, b, own if matches else far)


def score_kernel(
    ids, p0, p1, p2, p3, o0, o1, o2, o3, q0, q1, q2, q3, partial, p, q_all, pos
):
    n, width = p0.shape
    for s, (own, other) in enumerate(zip((p0, p1, p2, p3), (o0, o1, o2, o3))):
        rows = slice(s * n, s * n + n)

        @pl.when(ids[CORE] == 0)
        def _():
            p[rows, :width] = own[...]
            p[rows, width:] = other[...]

        @pl.when(ids[CORE] != 0)
        def _():
            p[rows, :width] = other[...]
            p[rows, width:] = own[...]

    for s, q in enumerate((q0, q1, q2, q3)):
        j = (ids[X] + 4 - s) & 3
        q_all[j] = q[:n]
        digits = q[n:, :n].astype(f32)
        pos[j] = (digits[0:1] * 64.0 + digits[1:2]).astype(jnp.int32)
        partial[j] = dot(p[...], q[:n], 1, 1)


def low_kernel(ids, p, q_all, pos, e_low, stats):
    n = q_all.shape[1]
    first = lax.broadcasted_iota(jnp.int32, (n, PAIR), 1) < SMALLEST
    for j in range(4):
        hot = find_positives(ids, pos[j], n)
        tops, sums, picks = [], [], []
        running = None
        for k, (begin, end) in enumerate(SPANS):
            if k == 0:
                q_part = q_all[j, :, :PAIR]
                q_part = jnp.where(first, q_part, jnp.zeros_like(q_part))
                running = dot(p[:, :PAIR], q_part, 1, 1)
            elif k == 1:
                running = dot(p[:, :PAIR], q_all[j, :, :PAIR], 1, 1)
            else:
                running = running + dot(p[:, begin:end], q_all[j, :, begin:end], 1, 1)
            scores = running * FACTORS[k]
            top = jnp.max(scores, axis=0, keepdims=True)
            e = jnp.exp(scores - top)
            e_low[k, j] = e
            tops.append(top)
            sums.append(jnp.sum(e, axis=0, keepdims=True))
            picks.append(jnp.sum(jnp.where(hot, scores, 0.0), axis=0, keepdims=True))
        stats[j] = jnp.concatenate(tops + sums + picks + [tops[0]], axis=0)


def owner_kernel(ids, pieces, pos, low_stats, e_high, message, local):
    n = pos.shape[2]
    hot = find_positives(ids, pos[ids[Y]], n)
    sum5 = pieces[0] + pieces[1]
    sum6 = sum5 + (pieces[2] + pieces[3])
    rows = []
    for i, total in enumerate((sum5, sum6)):
        scores = total * FACTORS[LOW + i]
        top = jnp.max(scores, axis=0, keepdims=True)
        e = jnp.exp(scores - top)
        e_high[i] = e
        rows += [
            top,
            jnp.sum(e, axis=0, keepdims=True),
            jnp.sum(jnp.where(hot, scores, 0.0), axis=0, keepdims=True),
        ]
    high = jnp.concatenate(rows + rows[:2], axis=0)
    for i in range(8):
        for j in range(4):
            message[i, 16 * j : 16 * j + 16] = low_stats[j]
        message[i, 64:72] = high
    local[...] = message[0]


def put_terms(ref, row, v):
    hi = v.astype(bf16).astype(f32)
    mid = (v - hi).astype(bf16).astype(f32)
    lo = v - hi - mid
    zero = jnp.zeros((EXTRA - 3, v.shape[1]), f32)
    ref[row:, : v.shape[1]] = jnp.concatenate([hi, mid, lo, zero], axis=0).astype(bf16)


def tail_kernel(ids, weight, stats, local, e_high, pos, m0, m1, m2, m3, rates):
    n = pos.shape[2]

    def merged(top, total, picked):
        best = jnp.max(top, axis=0)
        mass = jnp.sum(total * jnp.exp(top - best[None]), axis=0)
        return best + jnp.log(mass), jnp.sum(picked, axis=0)

    on = ids[Y] == 0
    low_loss = jnp.zeros((1, n), f32)
    for j in range(4):
        at = 16 * j
        lse, picked = merged(
            stats[:, at : at + 5], stats[:, at + 5 : at + 10], stats[:, at + 10 : at + 15]
        )
        rows = []
        for k in range(LOW):
            low_loss += weight[k] * (lse[k : k + 1] - picked[k : k + 1])
            scale = jnp.where(on, weight[k] * FACTORS[k], 0.0)
            rows.append(scale * jnp.exp(local[at + k : at + k + 1] - lse[k : k + 1]))
        rates[j] = jnp.concatenate(rows + rows[:3], axis=0)

    hot = find_positives(ids, pos[ids[Y]], n)
    loss = jnp.where(on, low_loss, 0.0)
    tail = None
    tails = []
    for i in (1, 0):
        at = 64 + 3 * i
        lse, picked = merged(
            stats[:, at : at + 1], stats[:, at + 1 : at + 2], stats[:, at + 2 : at + 3]
        )
        loss += weight[LOW + i] * (lse - picked)
        scale = weight[LOW + i] * FACTORS[LOW + i]
        rate = scale * jnp.exp(local[at : at + 1] - lse)
        g = e_high[i] * rate - jnp.where(hot, scale, 0.0)
        tail = g if tail is None else tail + g
        tails.append(tail.astype(bf16))
    lane = lax.broadcasted_iota(jnp.int32, (1, n), 1)
    mine = ids[ZL] * FEAT + ids[Y] * 2 + ids[CORE]
    loss = jnp.where(lane == mine, jnp.sum(loss, axis=1, keepdims=True), 0.0)
    for t, m in enumerate((m0, m1, m2, m3)):
        narrow = ((ids[Y] + t) & 3) <= 1

        @pl.when(narrow)
        def _():
            m[: 4 * n] = tails[1]

        @pl.when(jnp.logical_not(narrow))
        def _():
            m[: 4 * n] = tails[0]

        put_terms(m, 4 * n, loss)


def get_terms(ref, row, lanes):
    v = ref[row:, :lanes].astype(f32)
    return v[0:1] + v[1:2] + v[2:3]


def grad_kernel(
    ids, weight, t0, t1, t2, t3, e_low, rates, pos, p, q_all,
    gq0, gq1, gq2, gq3, gp0, gp1, gp2, gp3, row, tails, gq, gp,
):
    n = pos.shape[2]
    wide = gp0.shape[1]
    on = ids[Y] == 0
    loss = jnp.zeros((1, n), f32)
    for t, ref in enumerate((t0, t1, t2, t3)):
        j = (ids[Y] + 4 - t) & 3
        lanes = pl.ds(pl.multiple_of(j * n, n), n)
        loss += get_terms(ref, 4 * n, n)
        hot = find_positives(ids, pos[j], n)
        acc = ref[: 4 * n].astype(f32)
        for k in reversed(range(LOW)):
            scale = jnp.where(on, weight[k] * FACTORS[k], 0.0)
            acc = acc + (e_low[k, j] * rates[j, k : k + 1] - jnp.where(hot, scale, 0.0))
            tails[k, :, lanes] = acc.astype(bf16)
    row[...] = jnp.broadcast_to(loss, row.shape)

    q = q_all[...].reshape(4 * n, wide)
    first = lax.broadcasted_iota(jnp.int32, (4 * n, PAIR), 1) < SMALLEST

    def fill(out, fn):
        out[:, :PAIR] = jnp.where(first, fn(0, 0, PAIR), fn(1, 0, PAIR))
        for k in range(2, LOW):
            begin, end = SPANS[k]
            out[:, begin:end] = fn(k, begin, end)

    fill(gq, lambda k, a, b: dot(tails[k], p[:, a:b], 0, 0))
    for s, out in enumerate((gq0, gq1, gq2, gq3)):
        j = (ids[X] + 4 - s) & 3
        out[...] = gq[pl.ds(pl.multiple_of(j * n, n), n), :].astype(out.dtype)
    fill(gp, lambda k, a, b: dot(tails[k], q[:, a:b], 1, 0))
    for s, out in enumerate((gp0, gp1, gp2, gp3)):
        out[:n] = gp[s * n : s * n + n].astype(out.dtype)
        if s:
            out[n:] = jnp.zeros((EXTRA, wide), bf16)
            put_terms(out, n, loss)


def passage_kernel(ids, gp0, g1, g2, g3, row, own, message, loss):
    n, width = own.shape
    total = row[0:1]
    for g in (g1, g2, g3):
        total += get_terms(g, n, n)
    loss[...] = jnp.broadcast_to(total, loss.shape)
    message[n:] = jnp.zeros((EXTRA, width), bf16)
    put_terms(message, n, total)

    def half(c):
        lanes = slice(c * width, c * width + width)
        return gp0[:, lanes] + (
            g1[:n, lanes].astype(f32) + g2[:n, lanes].astype(f32) + g3[:n, lanes].astype(f32)
        )

    @pl.when(ids[CORE] == 0)
    def _():
        own[...] = half(0)
        message[:n] = half(1).astype(bf16)

    @pl.when(ids[CORE] != 0)
    def _():
        own[...] = half(1)
        message[:n] = half(0).astype(bf16)


def per_device(queries, passages, positives, level_weight):
    n, width = queries.shape
    wide = 2 * width
    bi = lax.axis_index("batch")
    fi = lax.axis_index("feat")
    core = fi % 2
    same = bi % 2 == core
    ids = jnp.stack([bi // 8, fi // 2, bi % 8 // 2, bi % 2, core]).astype(jnp.int32)

    rows = jnp.stack([positives // 64, positives % 64]).astype(bf16)
    rows = jnp.pad(rows, ((0, EXTRA - 2), (0, width - n)))
    q_row = jnp.concatenate([queries, rows], axis=0)
    near = move_square(queries, lambda h, c: (1 - h, c) if h == c else (h, 1 - c))
    far = move_square(q_row, lambda h, c: None if h == c else (1 - h, 1 - c))
    (q_msg,) = call(
        pack_kernel, [ids], [q_row, near, far], [shape(n + EXTRA, wide, bf16)]
    )
    q_msgs = [q_msg] + [shift_x(q_msg, s) for s in (1, 2, 3)]

    p_own = [passages] + [shift_zl(passages, s) for s in (1, 2, 3)]
    p_other = [swap_core(a) for a in p_own]

    tile = 4 * n * 4 * n
    partial, p, q, pos = call(
        score_kernel, [ids], [*p_own, *p_other, *q_msgs],
        [
            shape(4, 4 * n, n, f32),
            shape(4 * n, wide, bf16),
            shape(4, n, wide, bf16),
            shape(4, 1, n, jnp.int32),
        ],
        flops=2 * tile * wide,
    )
    pieces = lax.all_to_all(partial, "feat", 0, 0, axis_index_groups=Y_GROUPS)
    e_low, low_stats = call(
        low_kernel, [ids], [p, q, pos],
        [shape(LOW, 4, 4 * n, n, f32), shape(4, 16, n, f32)],
        flops=2 * tile * wide,
    )
    e_high, message, local = call(
        owner_kernel, [ids], [pieces, pos, low_stats],
        [shape(2, 4 * n, n, f32), shape(8, 72, n, f32), shape(72, n, f32)],
    )
    stats = lax.all_to_all(message, "batch", 0, 0, axis_index_groups=XZH_GROUPS)
    *tails, rates = call(
        tail_kernel, [ids, level_weight], [stats, local, e_high, pos],
        [shape(4 * n + EXTRA, n, bf16)] * 4 + [shape(4, 8, n, f32)],
    )
    tails = [tails[0]] + [shift_y(tails[t], t) for t in (1, 2, 3)]
    gq0, gq1, gq2, gq3, gp0, gp1, gp2, gp3, row = call(
        grad_kernel, [ids, level_weight], [*tails, e_low, rates, pos, p, q],
        [shape(n, wide, f32)]
        + [shape(n, wide, bf16)] * 3
        + [shape(n, wide, f32)]
        + [shape(n + EXTRA, wide, bf16)] * 3
        + [shape(8, n, f32)],
        scratch=[pltpu.VMEM((LOW, 4 * n, 4 * n), bf16)] + [pltpu.VMEM((4 * n, wide), f32)] * 2,
        flops=4 * tile * wide, grant=20,
    )
    gq = [shift_x(g, -s) for s, g in enumerate((gq1, gq2, gq3), 1)]
    gp = [shift_zl(g, -s) for s, g in enumerate((gp1, gp2, gp3), 1)]

    own, message, loss_row = call(
        passage_kernel, [ids], [gp0, *gp, row],
        [shape(n, width, f32), shape(n + EXTRA, width, bf16), shape(8, n, f32)],
    )
    other = swap_core(message).astype(f32)
    grad_passages = (own + other[:n]).astype(bf16)
    loss_row = loss_row[0] + (other[n, :n] + other[n + 1, :n] + other[n + 2, :n])
    loss = jnp.sum(loss_row) / (n * BATCH)

    gq_sum = gq0 + sum(g.astype(f32) for g in gq)
    far = move_square(gq_sum.astype(bf16), lambda h, c: None if h == c else (1 - h, c))
    gq_sum = (gq_sum + far.astype(f32)).astype(bf16)
    left, right = gq_sum[:, :width], gq_sum[:, width:]
    other = swap_core(jnp.where(core == 0, right, left))
    grad_queries = jnp.where(same, jnp.where(core == 0, left, right), other)
    return loss, grad_queries, grad_passages


def solution(mesh):
    in_specs = (P("batch", "feat"), P("batch", "feat"), P("batch"), P())
    out_specs = (P(), P("batch", "feat"), P("batch", "feat"))
    return jax.shard_map(
        per_device, mesh=mesh, in_specs=in_specs, out_specs=out_specs, check_vma=False
    )
```

```python
import math

import jax
import jax.numpy as jnp
from jax import lax
from jax.experimental import pallas as pl
from jax.experimental.pallas import tpu as pltpu
from jax.sharding import PartitionSpec as P

SMALLEST = 64
LEVELS = 7
LOW = 5
SHARPNESS = 3.0
WIDTHS = [SMALLEST * 2**k for k in range(LEVELS)]
FACTORS = [SHARPNESS / math.sqrt(w) for w in WIDTHS]
SPANS = list(zip([0] + WIDTHS[: LOW - 1], WIDTHS[:LOW]))
EXTRA = 16
PAIR = 2 * SMALLEST

BATCH = 32
FEAT = 8
BOTH = ("batch", "feat")
XZH_GROUPS = [[x * 8 + zl * 2 + zh for x in range(4) for zh in range(2)] for zl in range(4)]
X, Y, ZL, ZH, CORE = range(5)

f32 = jnp.float32
bf16 = jnp.bfloat16


def shift_x(a, s):
    return lax.ppermute(a, "batch", [(b, (b + 8 * s) % BATCH) for b in range(BATCH)])


def shift_zl(a, s):
    return lax.ppermute(
        a, "batch", [(b, b // 8 * 8 + (b + 2 * s) % 8) for b in range(BATCH)]
    )


def shift_y(a, s):
    return lax.ppermute(a, "feat", [(f, (f + 2 * s) % FEAT) for f in range(FEAT)])


def swap_core(a):
    return lax.ppermute(a, "feat", [(f, f ^ 1) for f in range(FEAT)])


def move_square(a, rule):
    pairs = []
    for b in range(BATCH):
        for f in range(FEAT):
            to = rule(b % 2, f % 2)
            if to is not None:
                pairs.append((b * FEAT + f, (b - b % 2 + to[0]) * FEAT + f - f % 2 + to[1]))
    return lax.ppermute(a, BOTH, pairs)


def dot(a, b, ca, cb):
    return lax.dot_general(
        a, b, (((ca,), (cb,)), ((), ())), preferred_element_type=f32
    )


def shape(*dims_dtype):
    return jax.ShapeDtypeStruct(dims_dtype[:-1], dims_dtype[-1])


def call(body, smem, args, outs, scratch=(), flops=0, grant=8, unread=0):
    vmem = pl.BlockSpec(memory_space=pltpu.VMEM)
    scalar = pl.BlockSpec(memory_space=pltpu.SMEM)
    moved = sum(a.size * a.dtype.itemsize for a in (*args, *outs))
    return pl.pallas_call(
        body,
        out_shape=outs,
        in_specs=[scalar] * len(smem)
        + [vmem] * (len(args) - unread)
        + [pl.BlockSpec(memory_space=pl.ANY)] * unread,
        out_specs=[vmem] * len(outs),
        scratch_shapes=list(scratch),
        cost_estimate=pl.CostEstimate(
            flops=flops, bytes_accessed=moved, transcendentals=0
        ),
        compiler_params=pltpu.CompilerParams(vmem_limit_bytes=grant << 20),
    )(*smem, *args)


def find_positives(ids, pos, n):
    rows = lax.broadcasted_iota(jnp.int32, (4 * n, n), 0)
    bits = n.bit_length() - 1
    block = ids[X] * 8 + ids[ZH] + 2 * ((ids[ZL] + 4 - (rows >> bits)) & 3)
    return (block << bits) + (rows & (n - 1)) == pos


def pack_kernel(ids, own, near, far, out):
    n, width = near.shape
    same = ids[ZH] == ids[CORE]

    def put(first, second, rows):
        out[:n, :width] = first[:n]
        out[:n, width:] = second[:n]
        out[n:, :width] = rows[n:]

    out[n:, width:] = jnp.zeros((EXTRA, width), bf16)
    for core in (0, 1):
        for matches in (True, False):
            a, b = (own, near) if matches else (near, far)
            if core:
                a, b = b, a

            @pl.when((ids[CORE] == core) & (same == matches))
            def _():
                put(a, b, own if matches else far)


def score_kernel(
    ids, p0, p1, p2, p3, o0, o1, o2, o3, q0, q1, q2, q3, s0, s1, s2, s3, p, q_all, pos
):
    n, width = p0.shape
    for s, (own, other) in enumerate(zip((p0, p1, p2, p3), (o0, o1, o2, o3))):
        rows = slice(s * n, s * n + n)

        @pl.when(ids[CORE] == 0)
        def _():
            p[rows, :width] = own[...]
            p[rows, width:] = other[...]

        @pl.when(ids[CORE] != 0)
        def _():
            p[rows, :width] = other[...]
            p[rows, width:] = own[...]

    for s, q in enumerate((q0, q1, q2, q3)):
        j = (ids[X] + 4 - s) & 3
        q_all[j] = q[:n]
        digits = q[n:, :n].astype(f32)
        pos[j] = (digits[0:1] * 64.0 + digits[1:2]).astype(jnp.int32)
    for t, out in enumerate((s0, s1, s2, s3)):
        out[...] = dot(p[...], q_all[(ids[Y] + t) & 3], 1, 1)


def low_kernel(ids, p, q_all, pos, e_low, stats):
    n = q_all.shape[1]
    first = lax.broadcasted_iota(jnp.int32, (n, PAIR), 1) < SMALLEST
    for j in range(4):
        hot = find_positives(ids, pos[j], n)
        tops, sums, picks = [], [], []
        running = None
        for k, (begin, end) in enumerate(SPANS):
            if k == 0:
                q_part = q_all[j, :, :PAIR]
                q_part = jnp.where(first, q_part, jnp.zeros_like(q_part))
                running = dot(p[:, :PAIR], q_part, 1, 1)
            elif k == 1:
                running = dot(p[:, :PAIR], q_all[j, :, :PAIR], 1, 1)
            else:
                running = running + dot(p[:, begin:end], q_all[j, :, begin:end], 1, 1)
            scores = running * FACTORS[k]
            top = jnp.max(scores, axis=0, keepdims=True)
            e = jnp.exp(scores - top)
            e_low[k, j] = e
            tops.append(top)
            sums.append(jnp.sum(e, axis=0, keepdims=True))
            picks.append(jnp.sum(jnp.where(hot, scores, 0.0), axis=0, keepdims=True))
        stats[j] = jnp.concatenate(tops + sums + picks + [tops[0]], axis=0)


def owner_kernel(ids, s0, s1, s2, s3, pos, low_stats, e_high, message, local):
    n = pos.shape[2]
    hot = find_positives(ids, pos[ids[Y]], n)
    sum5 = sum6 = None
    for t, ref in enumerate((s0, s1, s2, s3)):
        v = ref[...]
        part = jnp.where(((ids[Y] + 4 - t) & 3) <= 1, v, 0.0)
        sum5 = part if t == 0 else sum5 + part
        sum6 = v if t == 0 else sum6 + v
    rows = []
    for i, total in enumerate((sum5, sum6)):
        scores = total * FACTORS[LOW + i]
        top = jnp.max(scores, axis=0, keepdims=True)
        e = jnp.exp(scores - top)
        e_high[i] = e
        rows += [
            top,
            jnp.sum(e, axis=0, keepdims=True),
            jnp.sum(jnp.where(hot, scores, 0.0), axis=0, keepdims=True),
        ]
    high = jnp.concatenate(rows + rows[:2], axis=0)
    for i in range(8):
        for j in range(4):
            message[i, 16 * j : 16 * j + 16] = low_stats[j]
        message[i, 64:72] = high
    local[...] = message[0]


def put_terms(ref, row, v):
    hi = v.astype(bf16).astype(f32)
    mid = (v - hi).astype(bf16).astype(f32)
    lo = v - hi - mid
    zero = jnp.zeros((EXTRA - 3, v.shape[1]), f32)
    ref[row:, : v.shape[1]] = jnp.concatenate([hi, mid, lo, zero], axis=0).astype(bf16)


def tail_kernel(ids, weight, stats, local, e_high, pos, m0, m1, m2, m3, rates):
    n = pos.shape[2]

    def merged(top, total, picked):
        best = jnp.max(top, axis=0)
        mass = jnp.sum(total * jnp.exp(top - best[None]), axis=0)
        return best + jnp.log(mass), jnp.sum(picked, axis=0)

    on = ids[Y] == 0
    low_loss = jnp.zeros((1, n), f32)
    for j in range(4):
        at = 16 * j
        lse, picked = merged(
            stats[:, at : at + 5], stats[:, at + 5 : at + 10], stats[:, at + 10 : at + 15]
        )
        rows = []
        for k in range(LOW):
            low_loss += weight[k] * (lse[k : k + 1] - picked[k : k + 1])
            scale = jnp.where(on, weight[k] * FACTORS[k], 0.0)
            rows.append(scale * jnp.exp(local[at + k : at + k + 1] - lse[k : k + 1]))
        rates[j] = jnp.concatenate(rows + rows[:3], axis=0)

    hot = find_positives(ids, pos[ids[Y]], n)
    loss = jnp.where(on, low_loss, 0.0)
    tail = None
    tails = []
    for i in (1, 0):
        at = 64 + 3 * i
        lse, picked = merged(
            stats[:, at : at + 1], stats[:, at + 1 : at + 2], stats[:, at + 2 : at + 3]
        )
        loss += weight[LOW + i] * (lse - picked)
        scale = weight[LOW + i] * FACTORS[LOW + i]
        rate = scale * jnp.exp(local[at : at + 1] - lse)
        g = e_high[i] * rate - jnp.where(hot, scale, 0.0)
        tail = g if tail is None else tail + g
        tails.append(tail.astype(bf16))
    lane = lax.broadcasted_iota(jnp.int32, (1, n), 1)
    mine = ids[ZL] * FEAT + ids[Y] * 2 + ids[CORE]
    loss = jnp.where(lane == mine, jnp.sum(loss, axis=1, keepdims=True), 0.0)
    for t, m in enumerate((m0, m1, m2, m3)):
        narrow = ((ids[Y] + t) & 3) <= 1

        @pl.when(narrow)
        def _():
            m[: 4 * n] = tails[1]

        @pl.when(jnp.logical_not(narrow))
        def _():
            m[: 4 * n] = tails[0]

        put_terms(m, 4 * n, loss)


def get_terms(ref, row, lanes):
    v = ref[row:, :lanes].astype(f32)
    return v[0:1] + v[1:2] + v[2:3]


def low_grad_kernel(ids, weight, e_low, rates, pos, p, q_all, gq, gp, tails):
    n = pos.shape[2]
    on = ids[Y] == 0
    for j in range(4):
        hot = find_positives(ids, pos[j], n)
        acc = None
        for k in reversed(range(LOW)):
            scale = jnp.where(on, weight[k] * FACTORS[k], 0.0)
            g = e_low[k, j] * rates[j, k : k + 1] - jnp.where(hot, scale, 0.0)
            acc = g if acc is None else acc + g
            tails[k, :, j * n : j * n + n] = acc.astype(bf16)

    q = q_all[...].reshape(4 * n, q_all.shape[2])
    first = lax.broadcasted_iota(jnp.int32, (4 * n, PAIR), 1) < SMALLEST

    def fill(out, fn):
        out[:, :PAIR] = jnp.where(first, fn(0, 0, PAIR), fn(1, 0, PAIR))
        for k in range(2, LOW):
            begin, end = SPANS[k]
            out[:, begin:end] = fn(k, begin, end)

    fill(gq, lambda k, a, b: dot(tails[k], p[:, a:b], 0, 0))
    fill(gp, lambda k, a, b: dot(tails[k], q[:, a:b], 1, 0))


def grad_kernel(
    ids, t0, t1, t2, t3, gq_low, gp_low, p, q_all,
    gq0, gq1, gq2, gq3, own, message, row, tail, gq,
):
    n, wide = gq0.shape
    width = own.shape[1]
    loss = jnp.zeros((1, n), f32)
    for t, ref in enumerate((t0, t1, t2, t3)):
        j = (ids[Y] + 4 - t) & 3
        tail[:, pl.ds(pl.multiple_of(j * n, n), n)] = ref[: 4 * n]
        loss += get_terms(ref, 4 * n, n)
    row[...] = jnp.broadcast_to(loss, row.shape)

    q = q_all[...].reshape(4 * n, wide)
    message[4 * n :] = jnp.zeros((EXTRA, width), bf16)
    put_terms(message, 4 * n, loss)
    for c in (0, 1):
        lanes = slice(c * width, c * width + width)
        gp = dot(tail[...], q[:, lanes], 1, 0) + gp_low[:, lanes]

        @pl.when(ids[CORE] == c)
        def _():
            own[...] = gp

        @pl.when(ids[CORE] != c)
        def _():
            message[: 4 * n] = gp.astype(bf16)

    gq[...] = dot(tail[...], p[...], 0, 0) + gq_low[...]
    for s, out in enumerate((gq0, gq1, gq2, gq3)):
        j = (ids[X] + 4 - s) & 3
        out[...] = gq[pl.ds(pl.multiple_of(j * n, n), n), :].astype(out.dtype)


def core_sum_kernel(gp_own, row, other, own, m1, m2, m3, loss):
    n, width = own.shape
    total = row[0:1] + get_terms(other, 4 * n, n)
    loss[...] = jnp.broadcast_to(total, loss.shape)
    for s, out in enumerate((own, m1, m2, m3)):
        rows = slice(s * n, s * n + n)
        v = gp_own[rows] + other[rows].astype(f32)
        out[:n] = v.astype(out.dtype)
        if s:
            out[n:] = jnp.zeros((EXTRA, width), bf16)
            put_terms(out, n, total)


def query_sum_kernel(gq0, g1, g2, g3, *refs):
    total, message = refs[-2:]
    v = gq0[...] + (g1[...].astype(f32) + g2[...].astype(f32) + g3[...].astype(f32))
    total[...] = v
    message[...] = v.astype(bf16)


def per_device(queries, passages, positives, level_weight):
    n, width = queries.shape
    wide = 2 * width
    bi = lax.axis_index("batch")
    fi = lax.axis_index("feat")
    core = fi % 2
    same = bi % 2 == core
    ids = jnp.stack([bi // 8, fi // 2, bi % 8 // 2, bi % 2, core]).astype(jnp.int32)

    rows = jnp.stack([positives // 64, positives % 64]).astype(bf16)
    rows = jnp.pad(rows, ((0, EXTRA - 2), (0, width - n)))
    q_row = jnp.concatenate([queries, rows], axis=0)
    near = move_square(queries, lambda h, c: (1 - h, c) if h == c else (h, 1 - c))
    far = move_square(q_row, lambda h, c: None if h == c else (1 - h, 1 - c))
    (q_msg,) = call(
        pack_kernel, [ids], [q_row, near, far], [shape(n + EXTRA, wide, bf16)]
    )
    q_msgs = [q_msg] + [shift_x(q_msg, s) for s in (1, 2, 3)]

    p_own = [passages] + [shift_zl(passages, s) for s in (1, 2, 3)]
    p_other = [swap_core(a) for a in p_own]

    tile = 4 * n * 4 * n
    *partial, p, q, pos = call(
        score_kernel, [ids], [*p_own, *p_other, *q_msgs],
        [shape(4 * n, n, f32)] * 4
        + [
            shape(4 * n, wide, bf16),
            shape(4, n, wide, bf16),
            shape(4, 1, n, jnp.int32),
        ],
        flops=2 * tile * wide,
    )
    pieces = [partial[0]] + [shift_y(partial[t], t) for t in (1, 2, 3)]
    e_low, low_stats = call(
        low_kernel, [ids], [p, q, pos],
        [shape(LOW, 4, 4 * n, n, f32), shape(4, 16, n, f32)],
        flops=2 * tile * wide,
    )
    e_high, message, local = call(
        owner_kernel, [ids], [*pieces, pos, low_stats],
        [shape(2, 4 * n, n, f32), shape(8, 72, n, f32), shape(72, n, f32)],
    )
    stats = lax.all_to_all(message, "batch", 0, 0, axis_index_groups=XZH_GROUPS)
    *tails, rates = call(
        tail_kernel, [ids, level_weight], [stats, local, e_high, pos],
        [shape(4 * n + EXTRA, n, bf16)] * 4 + [shape(4, 8, n, f32)],
    )
    tails = [tails[0]] + [shift_y(tails[t], t) for t in (1, 2, 3)]
    gq_low, gp_low = call(
        low_grad_kernel, [ids, level_weight], [e_low, rates, pos, p, q],
        [shape(4 * n, wide, f32)] * 2,
        scratch=[pltpu.VMEM((LOW, 4 * n, 4 * n), bf16)],
        flops=4 * tile * wide, grant=12,
    )
    gq0, gq1, gq2, gq3, gp_own, message, row = call(
        grad_kernel, [ids], [*tails, gq_low, gp_low, p, q],
        [shape(n, wide, f32)]
        + [shape(n, wide, bf16)] * 3
        + [
            shape(4 * n, width, f32),
            shape(4 * n + EXTRA, width, bf16),
            shape(8, n, f32),
        ],
        scratch=[pltpu.VMEM((4 * n, 4 * n), bf16), pltpu.VMEM((4 * n, wide), f32)],
        flops=4 * tile * wide, grant=12,
    )
    gq = [shift_x(g, -s) for s, g in enumerate((gq1, gq2, gq3), 1)]

    own, *messages, loss_row = call(
        core_sum_kernel, [], [gp_own, row, swap_core(message)],
        [shape(n, width, f32)] + [shape(n + EXTRA, width, bf16)] * 3 + [shape(8, n, f32)],
    )
    gp = [shift_zl(m, -s) for s, m in enumerate(messages, 1)]
    gq_sum, gq_message = call(
        query_sum_kernel, [], [gq0, *gq, *messages],
        [shape(n, wide, f32), shape(n, wide, bf16)], unread=3,
    )
    far = move_square(gq_message, lambda h, c: None if h == c else (1 - h, c))
    gq_sum = (gq_sum + far.astype(f32)).astype(bf16)
    left, right = gq_sum[:, :width], gq_sum[:, width:]
    other = swap_core(jnp.where(core == 0, right, left))
    grad_queries = jnp.where(same, jnp.where(core == 0, left, right), other)

    grad_passages = own + sum(g[:n].astype(f32) for g in gp)
    loss_row = loss_row[0] + sum(jnp.sum(g[n : n + 3, :n].astype(f32), axis=0) for g in gp)
    loss = jnp.sum(loss_row) / (n * BATCH)
    return loss, grad_queries, grad_passages.astype(bf16)


def solution(mesh):
    in_specs = (P("batch", "feat"), P("batch", "feat"), P("batch"), P())
    out_specs = (P(), P("batch", "feat"), P("batch", "feat"))
    return jax.shard_map(
        per_device, mesh=mesh, in_specs=in_specs, out_specs=out_specs, check_vma=False
    )
```

```python
import math

import jax
import jax.numpy as jnp
from jax import lax
from jax.experimental import pallas as pl
from jax.experimental.pallas import tpu as pltpu
from jax.sharding import PartitionSpec as P

SMALLEST = 64
LEVELS = 7
LOW = 5
SHARPNESS = 3.0
WIDTHS = [SMALLEST * 2**k for k in range(LEVELS)]
FACTORS = [SHARPNESS / math.sqrt(w) for w in WIDTHS]
SPANS = list(zip([0] + WIDTHS[: LOW - 1], WIDTHS[:LOW]))
EXTRA = 16
PAIR = 2 * SMALLEST

BATCH = 32
FEAT = 8
BOTH = ("batch", "feat")
STAT_GROUPS = [
    [(x * 8 + zl * 2 + zh) * FEAT + y * 2 + c for zl in range(4) for c in range(2)]
    for x in range(4) for zh in range(2) for y in range(4)
]
X, Y, ZL, ZH, CORE = range(5)

f32 = jnp.float32
bf16 = jnp.bfloat16


def shift_x(a, s):
    return lax.ppermute(a, "batch", [(b, (b + 8 * s) % BATCH) for b in range(BATCH)])


def shift_zl(a, s):
    return lax.ppermute(
        a, "batch", [(b, b // 8 * 8 + (b + 2 * s) % 8) for b in range(BATCH)]
    )


def shift_y(a, s):
    return lax.ppermute(a, "feat", [(f, (f + 2 * s) % FEAT) for f in range(FEAT)])


def swap_core(a):
    return lax.ppermute(a, "feat", [(f, f ^ 1) for f in range(FEAT)])


def move_square(a, rule):
    pairs = []
    for b in range(BATCH):
        for f in range(FEAT):
            to = rule(b % 2, f % 2)
            if to is not None:
                pairs.append((b * FEAT + f, (b - b % 2 + to[0]) * FEAT + f - f % 2 + to[1]))
    return lax.ppermute(a, BOTH, pairs)


def dot(a, b, ca, cb):
    return lax.dot_general(
        a, b, (((ca,), (cb,)), ((), ())), preferred_element_type=f32
    )


def shape(*dims_dtype):
    return jax.ShapeDtypeStruct(dims_dtype[:-1], dims_dtype[-1])


def call(body, smem, args, outs, scratch=(), flops=0, grant=8, unread=0):
    vmem = pl.BlockSpec(memory_space=pltpu.VMEM)
    scalar = pl.BlockSpec(memory_space=pltpu.SMEM)
    moved = sum(a.size * a.dtype.itemsize for a in (*args, *outs))
    return pl.pallas_call(
        body,
        out_shape=outs,
        in_specs=[scalar] * len(smem)
        + [vmem] * (len(args) - unread)
        + [pl.BlockSpec(memory_space=pl.ANY)] * unread,
        out_specs=[vmem] * len(outs),
        scratch_shapes=list(scratch),
        cost_estimate=pl.CostEstimate(
            flops=flops, bytes_accessed=moved, transcendentals=0
        ),
        compiler_params=pltpu.CompilerParams(vmem_limit_bytes=grant << 20),
    )(*smem, *args)


def find_positives(ids, pos, n):
    rows = lax.broadcasted_iota(jnp.int32, (4 * n, n), 0)
    bits = n.bit_length() - 1
    block = ((ids[X] + 4 - (rows >> bits)) & 3) * 8 + ids[ZL] * 2 + ids[CORE]
    return (block << bits) + (rows & (n - 1)) == pos


def pack_kernel(ids, own, near, far, q_row, out, late):
    n, width = near.shape
    same = ids[ZH] == ids[CORE]
    late[...] = q_row[...]
    for core in (0, 1):
        for matches in (True, False):
            a, b = (own, near) if matches else (near, far)
            if core:
                a, b = b, a

            @pl.when((ids[CORE] == core) & (same == matches))
            def _():
                out[:, :width] = a[...]
                out[:, width:] = b[...]


def score_kernel(
    ids, p0, p1, p2, p3, q0, q1, q2, q3, o0, o1, o2, o3, s0, s1, s2, s3, p, q_all, pos
):
    n, wide = p0.shape
    width = wide // 2
    for s, block in enumerate((p0, p1, p2, p3)):
        p[s * n : s * n + n] = block[...]
    for s, (own, other) in enumerate(zip((q0, q1, q2, q3), (o0, o1, o2, o3))):
        j = (ids[ZL] + 4 - s) & 3
        digits = own[n:, :n].astype(f32)
        pos[j] = (digits[0:1] * 64.0 + digits[1:2]).astype(jnp.int32)

        @pl.when(ids[CORE] == 0)
        def _():
            q_all[j, :, :width] = own[:n]
            q_all[j, :, width:] = other[:n]

        @pl.when(ids[CORE] != 0)
        def _():
            q_all[j, :, :width] = other[:n]
            q_all[j, :, width:] = own[:n]

    for t, out in enumerate((s0, s1, s2, s3)):
        out[...] = dot(p[...], q_all[(ids[Y] + t) & 3], 1, 1)


def level(scores, hot, weight):
    top = jnp.max(scores, axis=0, keepdims=True)
    e = jnp.exp(scores - top)
    lse = top + jnp.log(jnp.sum(e, axis=0, keepdims=True))
    picked = weight * jnp.sum(jnp.where(hot, scores, 0.0), axis=0, keepdims=True)
    return e, top, lse, picked


def low_kernel(ids, weight, p, q_all, pos, e_low, stats, tops):
    n = q_all.shape[1]
    first = lax.broadcasted_iota(jnp.int32, (n, PAIR), 1) < SMALLEST
    for j in range(4):
        hot = find_positives(ids, pos[j], n)
        rows, lses, total = [], [], jnp.zeros((1, n), f32)
        running = None
        for k, (begin, end) in enumerate(SPANS):
            if k == 0:
                q_part = q_all[j, :, :PAIR]
                q_part = jnp.where(first, q_part, jnp.zeros_like(q_part))
                running = dot(p[:, :PAIR], q_part, 1, 1)
            elif k == 1:
                running = dot(p[:, :PAIR], q_all[j, :, :PAIR], 1, 1)
            else:
                running = running + dot(p[:, begin:end], q_all[j, :, begin:end], 1, 1)
            e_low[k, j], top, lse, picked = level(running * FACTORS[k], hot, weight[k])
            rows.append(top)
            lses.append(lse)
            total += picked
        tops[j] = jnp.concatenate(rows + rows[:3], axis=0)
        stats[j] = jnp.concatenate(lses + [total, total, total], axis=0)


def owner_kernel(ids, weight, s0, s1, s2, s3, pos, low_stats, e_high, message, tops):
    n = pos.shape[2]
    hot = find_positives(ids, pos[ids[Y]], n)
    sum5 = sum6 = None
    for t, ref in enumerate((s0, s1, s2, s3)):
        v = ref[...]
        part = jnp.where(((ids[Y] + 4 - t) & 3) <= 1, v, 0.0)
        sum5 = part if t == 0 else sum5 + part
        sum6 = v if t == 0 else sum6 + v
    e_high[0], top5, lse5, picked5 = level(sum5 * FACTORS[5], hot, weight[5])
    e_high[1], top6, lse6, picked6 = level(sum6 * FACTORS[6], hot, weight[6])
    tops[...] = jnp.concatenate([top5, top6] * 4, axis=0)
    high = jnp.concatenate([lse5, lse6] + [picked5 + picked6] * 6, axis=0)
    for i in range(8):
        for j in range(4):
            message[i, 8 * j : 8 * j + 8] = low_stats[j]
        message[i, 32:] = high


def put_terms(ref, row, v):
    hi = v.astype(bf16).astype(f32)
    mid = (v - hi).astype(bf16).astype(f32)
    lo = v - hi - mid
    zero = jnp.zeros((EXTRA - 3, v.shape[1]), f32)
    ref[row:, : v.shape[1]] = jnp.concatenate([hi, mid, lo, zero], axis=0).astype(bf16)


def tail_kernel(ids, weight, stats, low_tops, tops, e_high, pos, m0, m1, m2, m3, rates):
    n = pos.shape[2]

    def merged(at, levels):
        lse = stats[:, at : at + levels]
        best = jnp.max(lse, axis=0)
        mass = jnp.sum(jnp.exp(lse - best[None]), axis=0)
        return best + jnp.log(mass), jnp.sum(stats[:, at + levels : at + levels + 1], axis=0)

    on = ids[Y] == 0
    loss = jnp.zeros((1, n), f32)
    for j in range(4):
        lse, picked = merged(8 * j, LOW)
        loss -= picked
        rows = []
        for k in range(LOW):
            loss += weight[k] * lse[k : k + 1]
            scale = jnp.where(on, weight[k] * FACTORS[k], 0.0)
            rows.append(scale * jnp.exp(low_tops[j, k : k + 1] - lse[k : k + 1]))
        rates[j] = jnp.concatenate(rows + rows[:3], axis=0)

    hot = find_positives(ids, pos[ids[Y]], n)
    lse, picked = merged(32, 2)
    loss = jnp.where(on, loss, 0.0) - picked
    tail = None
    tails = []
    for i in (1, 0):
        loss += weight[LOW + i] * lse[i : i + 1]
        scale = weight[LOW + i] * FACTORS[LOW + i]
        rate = scale * jnp.exp(tops[i : i + 1] - lse[i : i + 1])
        g = e_high[i] * rate - jnp.where(hot, scale, 0.0)
        tail = g if tail is None else tail + g
        tails.append(tail.astype(bf16))
    lane = lax.broadcasted_iota(jnp.int32, (1, n), 1)
    mine = ids[X] * 8 + ids[ZH] * 4 + ids[Y]
    loss = jnp.where(lane == mine, jnp.sum(loss, axis=1, keepdims=True), 0.0)
    for t, m in enumerate((m0, m1, m2, m3)):
        narrow = ((ids[Y] + t) & 3) <= 1

        @pl.when(narrow)
        def _():
            m[: 4 * n] = tails[1]

        @pl.when(jnp.logical_not(narrow))
        def _():
            m[: 4 * n] = tails[0]

        put_terms(m, 4 * n, loss)


def get_terms(ref, row, lanes):
    v = ref[row:, :lanes].astype(f32)
    return v[0:1] + v[1:2] + v[2:3]


def low_grad_kernel(ids, weight, e_low, rates, pos, p, q_all, gq, gp, tails):
    n = pos.shape[2]
    on = ids[Y] == 0
    for j in range(4):
        hot = find_positives(ids, pos[j], n)
        acc = None
        for k in reversed(range(LOW)):
            scale = jnp.where(on, weight[k] * FACTORS[k], 0.0)
            g = e_low[k, j] * rates[j, k : k + 1] - jnp.where(hot, scale, 0.0)
            acc = g if acc is None else acc + g
            tails[k, :, j * n : j * n + n] = acc.astype(bf16)

    q = q_all[...].reshape(4 * n, q_all.shape[2])
    first = lax.broadcasted_iota(jnp.int32, (4 * n, PAIR), 1) < SMALLEST

    def fill(out, fn):
        out[:, :PAIR] = jnp.where(first, fn(0, 0, PAIR), fn(1, 0, PAIR))
        for k in range(2, LOW):
            begin, end = SPANS[k]
            out[:, begin:end] = fn(k, begin, end)

    fill(gq, lambda k, a, b: dot(tails[k], p[:, a:b], 0, 0))
    fill(gp, lambda k, a, b: dot(tails[k], q[:, a:b], 1, 0))


def grad_kernel(
    ids, t0, t1, t2, t3, gq_low, gp_low, p, q_all,
    gp0, gp1, gp2, gp3, own, message, row, tail,
):
    n, wide = gp0.shape
    width = own.shape[1]
    loss = jnp.zeros((1, n), f32)
    for t, ref in enumerate((t0, t1, t2, t3)):
        j = (ids[Y] + 4 - t) & 3
        tail[:, pl.ds(pl.multiple_of(j * n, n), n)] = ref[: 4 * n]
        loss += get_terms(ref, 4 * n, n)
    row[...] = jnp.broadcast_to(loss, row.shape)

    q = q_all[...].reshape(4 * n, wide)
    for s, out in enumerate((gp0, gp1, gp2, gp3)):
        rows = slice(s * n, s * n + n)
        out[:n] = (dot(tail[rows], q, 1, 0) + gp_low[rows]).astype(out.dtype)
        if s:
            out[n:] = jnp.zeros((EXTRA, wide), bf16)
            put_terms(out, n, loss)

    for c in (0, 1):
        lanes = slice(c * width, c * width + width)
        gq = dot(tail[...], p[:, lanes], 0, 0) + gq_low[:, lanes]

        @pl.when(ids[CORE] == c)
        def _():
            own[...] = gq

        @pl.when(ids[CORE] != c)
        def _():
            message[...] = gq.astype(bf16)


def core_sum_kernel(ids, gq_own, other, own, m1, m2, m3):
    n = own.shape[0]
    for s, out in enumerate((own, m1, m2, m3)):
        j = (ids[ZL] + 4 - s) & 3
        rows = pl.ds(pl.multiple_of(j * n, n), n)
        out[...] = (gq_own[rows, :] + other[rows, :].astype(f32)).astype(out.dtype)


def passage_sum_kernel(ids, gp0, g1, g2, g3, row, m1, m2, m3, own, near, far, loss):
    n, width = own.shape
    total = row[0:1]
    for g in (g1, g2, g3):
        total += get_terms(g, n, n)
    loss[...] = jnp.broadcast_to(total, loss.shape)
    same = ids[ZH] == ids[CORE]
    for c in (0, 1):
        lanes = slice(c * width, c * width + width)
        v = gp0[:, lanes] + (
            g1[:n, lanes].astype(f32) + g2[:n, lanes].astype(f32) + g3[:n, lanes].astype(f32)
        )

        @pl.when(ids[CORE] == c)
        def _():
            own[...] = v

        @pl.when((ids[CORE] == c) != same)
        def _():
            near[:n] = v.astype(bf16)

        @pl.when(ids[CORE] != c)
        def _():
            far[:n] = v.astype(bf16)

    for out in (near, far):
        out[n:] = jnp.zeros((EXTRA, width), bf16)
        put_terms(out, n, total)


def per_device(queries, passages, positives, level_weight):
    n, width = queries.shape
    wide = 2 * width
    bi = lax.axis_index("batch")
    fi = lax.axis_index("feat")
    core = fi % 2
    same = bi % 2 == core
    ids = jnp.stack([bi // 8, fi // 2, bi % 8 // 2, bi % 2, core]).astype(jnp.int32)

    near = move_square(passages, lambda h, c: (1 - h, c) if h == c else (h, 1 - c))
    far = move_square(passages, lambda h, c: None if h == c else (1 - h, 1 - c))
    rows = jnp.stack([positives // 64, positives % 64]).astype(bf16)
    rows = jnp.pad(rows, ((0, EXTRA - 2), (0, width - n)))
    q_row = jnp.concatenate([queries, rows], axis=0)
    p_block, q_late = call(
        pack_kernel, [ids], [passages, near, far, q_row],
        [shape(n, wide, bf16), shape(n + EXTRA, width, bf16)],
    )
    p_blocks = [p_block] + [shift_x(p_block, s) for s in (1, 2, 3)]

    q_own = [q_row, shift_zl(q_row, 1), shift_zl(q_late, 2), shift_zl(q_row, 3)]
    q_other = [swap_core(a) for a in q_own]

    tile = 4 * n * 4 * n
    *partial, p, q, pos = call(
        score_kernel, [ids], [*p_blocks, *q_own, *q_other],
        [shape(4 * n, n, f32)] * 4
        + [
            shape(4 * n, wide, bf16),
            shape(4, n, wide, bf16),
            shape(4, 1, n, jnp.int32),
        ],
        flops=2 * tile * wide,
    )
    pieces = [partial[0]] + [shift_y(partial[t], t) for t in (1, 2, 3)]
    e_low, low_stats, low_tops = call(
        low_kernel, [ids, level_weight], [p, q, pos],
        [shape(LOW, 4, 4 * n, n, f32), shape(4, 8, n, f32), shape(4, 8, n, f32)],
        flops=2 * tile * wide,
    )
    e_high, message, tops = call(
        owner_kernel, [ids, level_weight], [*pieces, pos, low_stats],
        [shape(2, 4 * n, n, f32), shape(8, 40, n, f32), shape(8, n, f32)],
    )
    stats = lax.all_to_all(message, BOTH, 0, 0, axis_index_groups=STAT_GROUPS)
    *tails, rates = call(
        tail_kernel, [ids, level_weight], [stats, low_tops, tops, e_high, pos],
        [shape(4 * n + EXTRA, n, bf16)] * 4 + [shape(4, 8, n, f32)],
    )
    tails = [tails[0]] + [shift_y(tails[t], t) for t in (1, 2, 3)]
    gq_low, gp_low = call(
        low_grad_kernel, [ids, level_weight], [e_low, rates, pos, p, q],
        [shape(4 * n, wide, f32)] * 2,
        scratch=[pltpu.VMEM((LOW, 4 * n, 4 * n), bf16)],
        flops=4 * tile * wide, grant=12,
    )
    gp0, gp1, gp2, gp3, gq_own, message, row = call(
        grad_kernel, [ids], [*tails, gq_low, gp_low, p, q],
        [shape(n, wide, f32)]
        + [shape(n + EXTRA, wide, bf16)] * 3
        + [
            shape(4 * n, width, f32),
            shape(4 * n, width, bf16),
            shape(8, n, f32),
        ],
        scratch=[pltpu.VMEM((4 * n, 4 * n), bf16)],
        flops=4 * tile * wide, grant=12,
    )
    gp = [shift_x(g, -s) for s, g in enumerate((gp1, gp2, gp3), 1)]
    own, *messages = call(
        core_sum_kernel, [ids], [gq_own, swap_core(message)],
        [shape(n, width, f32)] + [shape(n, width, bf16)] * 3,
    )
    gq = [shift_zl(m, -s) for s, m in enumerate(messages, 1)]
    gp_own, near, far, loss_row = call(
        passage_sum_kernel, [ids], [gp0, *gp, row, *messages],
        [shape(n, width, f32)] + [shape(n + EXTRA, width, bf16)] * 2 + [shape(8, n, f32)],
        unread=3,
    )
    near = move_square(near, lambda h, c: (h, 1 - c) if h == c else (1 - h, c)).astype(f32)
    far = move_square(far, lambda h, c: None if h == c else (1 - h, 1 - c)).astype(f32)
    grad_queries = own + sum(g.astype(f32) for g in gq)
    grad_passages = near[:n] + jnp.where(same, gp_own, far[:n])
    loss_other = jnp.where(same, near[n : n + 3, :n], far[n : n + 3, :n])
    loss = jnp.sum(loss_row[0] + jnp.sum(loss_other, axis=0)) / (n * BATCH)
    return loss, grad_queries.astype(bf16), grad_passages.astype(bf16)
def solution(mesh):
    in_specs = (P("batch", "feat"), P("batch", "feat"), P("batch"), P())
    out_specs = (P(), P("batch", "feat"), P("batch", "feat"))
    return jax.shard_map(
        per_device, mesh=mesh, in_specs=in_specs, out_specs=out_specs, check_vma=False
    )
```

```python
import math

import jax
import jax.numpy as jnp
from jax import lax
from jax.experimental import pallas as pl
from jax.experimental.pallas import tpu as pltpu
from jax.sharding import PartitionSpec as P

SMALLEST = 64
LEVELS = 7
LOW = 5
SHARPNESS = 3.0
WIDTHS = [SMALLEST * 2**k for k in range(LEVELS)]
FACTORS = [SHARPNESS / math.sqrt(w) for w in WIDTHS]
SPANS = list(zip([0] + WIDTHS[: LOW - 1], WIDTHS[:LOW]))
EXTRA = 16
PAIR = 2 * SMALLEST

BATCH = 32
FEAT = 8
BOTH = ("batch", "feat")
XZH_GROUPS = [[x * 8 + zl * 2 + zh for x in range(4) for zh in range(2)] for zl in range(4)]
X, Y, ZL, ZH, CORE = range(5)

f32 = jnp.float32
bf16 = jnp.bfloat16


def shift_x(a, s):
    return lax.ppermute(a, "batch", [(b, (b + 8 * s) % BATCH) for b in range(BATCH)])


def shift_zl(a, s):
    return lax.ppermute(
        a, "batch", [(b, b // 8 * 8 + (b + 2 * s) % 8) for b in range(BATCH)]
    )


def shift_y(a, s):
    return lax.ppermute(a, "feat", [(f, (f + 2 * s) % FEAT) for f in range(FEAT)])


def swap_core(a):
    return lax.ppermute(a, "feat", [(f, f ^ 1) for f in range(FEAT)])


def move_square(a, rule):
    pairs = []
    for b in range(BATCH):
        for f in range(FEAT):
            to = rule(b % 2, f % 2)
            if to is not None:
                pairs.append((b * FEAT + f, (b - b % 2 + to[0]) * FEAT + f - f % 2 + to[1]))
    return lax.ppermute(a, BOTH, pairs)


def dot(a, b, ca, cb):
    return lax.dot_general(
        a, b, (((ca,), (cb,)), ((), ())), preferred_element_type=f32
    )


def shape(*dims_dtype):
    return jax.ShapeDtypeStruct(dims_dtype[:-1], dims_dtype[-1])


def call(body, smem, args, outs, scratch=(), flops=0, grant=8, in_place=0):
    vmem = pl.BlockSpec(memory_space=pltpu.VMEM)
    scalar = pl.BlockSpec(memory_space=pltpu.SMEM)
    moved = sum(a.size * a.dtype.itemsize for a in (*args, *outs))
    return pl.pallas_call(
        body,
        out_shape=outs,
        in_specs=[scalar] * len(smem)
        + [vmem] * (len(args) - in_place)
        + [pl.BlockSpec(memory_space=pl.ANY)] * in_place,
        out_specs=[vmem] * len(outs),
        scratch_shapes=list(scratch),
        cost_estimate=pl.CostEstimate(
            flops=flops, bytes_accessed=moved, transcendentals=0
        ),
        compiler_params=pltpu.CompilerParams(vmem_limit_bytes=grant << 20),
    )(*smem, *args)


def find_positives(ids, pos, n):
    rows = lax.broadcasted_iota(jnp.int32, (4 * n, n), 0)
    bits = n.bit_length() - 1
    block = ids[X] * 8 + ids[ZH] + 2 * ((ids[ZL] + 4 - (rows >> bits)) & 3)
    return (block << bits) + (rows & (n - 1)) == pos


def pack_kernel(ids, own, near, far, out):
    n, width = near.shape
    same = ids[ZH] == ids[CORE]

    def put(first, second, rows):
        out[:n, :width] = first[:n]
        out[:n, width:] = second[:n]
        out[n:, :width] = rows[n:]

    out[n:, width:] = jnp.zeros((EXTRA, width), bf16)
    for core in (0, 1):
        for matches in (True, False):
            a, b = (own, near) if matches else (near, far)
            if core:
                a, b = b, a

            @pl.when((ids[CORE] == core) & (same == matches))
            def _():
                put(a, b, own if matches else far)


def score_kernel(
    ids, p1, p2, p3, o0, o1, o2, o3, q0, q1, q2, q3, p0_hbm,
    s0, s1, s2, s3, p, q_all, pos, p0, arrived,
):
    n, width = p1.shape
    copy = pltpu.make_async_copy(p0_hbm, p0, arrived)
    copy.start()
    for s, (own, other) in enumerate(zip((p1, p2, p3, p0), (o1, o2, o3, o0))):
        rows = slice((s + 1) % 4 * n, (s + 1) % 4 * n + n)
        if s == 3:
            copy.wait()

        @pl.when(ids[CORE] == 0)
        def _():
            p[rows, :width] = own[...]
            p[rows, width:] = other[...]

        @pl.when(ids[CORE] != 0)
        def _():
            p[rows, :width] = other[...]
            p[rows, width:] = own[...]

    for s, q in enumerate((q0, q1, q2, q3)):
        j = (ids[X] + 4 - s) & 3
        q_all[j] = q[:n]
        digits = q[n:, :n].astype(f32)
        pos[j] = (digits[0:1] * 64.0 + digits[1:2]).astype(jnp.int32)
    for t, out in enumerate((s0, s1, s2, s3)):
        out[...] = dot(p[...], q_all[(ids[Y] + t) & 3], 1, 1)


def level(scores, hot, weight):
    top = jnp.max(scores, axis=0, keepdims=True)
    e = jnp.exp(scores - top)
    lse = top + jnp.log(jnp.sum(e, axis=0, keepdims=True))
    picked = weight * jnp.sum(jnp.where(hot, scores, 0.0), axis=0, keepdims=True)
    return e, top, lse, picked


def low_kernel(ids, weight, p, q_all, pos, e_low, stats, tops):
    n = q_all.shape[1]
    first = lax.broadcasted_iota(jnp.int32, (n, PAIR), 1) < SMALLEST
    for j in range(4):
        hot = find_positives(ids, pos[j], n)
        rows, lses, total = [], [], jnp.zeros((1, n), f32)
        running = None
        for k, (begin, end) in enumerate(SPANS):
            if k == 0:
                q_part = q_all[j, :, :PAIR]
                q_part = jnp.where(first, q_part, jnp.zeros_like(q_part))
                running = dot(p[:, :PAIR], q_part, 1, 1)
            elif k == 1:
                running = dot(p[:, :PAIR], q_all[j, :, :PAIR], 1, 1)
            else:
                running = running + dot(p[:, begin:end], q_all[j, :, begin:end], 1, 1)
            e_low[k, j], top, lse, picked = level(running * FACTORS[k], hot, weight[k])
            rows.append(top)
            lses.append(lse)
            total += picked
        tops[j] = jnp.concatenate(rows + rows[:3], axis=0)
        stats[j] = jnp.concatenate(lses + [total, total, total], axis=0)


def owner_kernel(ids, weight, s0, s1, s2, s3, pos, low_stats, e_high, message, tops):
    n = pos.shape[2]
    hot = find_positives(ids, pos[ids[Y]], n)
    sum5 = sum6 = None
    for t, ref in enumerate((s0, s1, s2, s3)):
        v = ref[...]
        part = jnp.where(((ids[Y] + 4 - t) & 3) <= 1, v, 0.0)
        sum5 = part if t == 0 else sum5 + part
        sum6 = v if t == 0 else sum6 + v
    e_high[0], top5, lse5, picked5 = level(sum5 * FACTORS[5], hot, weight[5])
    e_high[1], top6, lse6, picked6 = level(sum6 * FACTORS[6], hot, weight[6])
    tops[...] = jnp.concatenate([top5, top6] * 4, axis=0)
    high = jnp.concatenate([lse5, lse6] + [picked5 + picked6] * 6, axis=0)
    for i in range(8):
        for j in range(4):
            message[i, 8 * j : 8 * j + 8] = low_stats[j]
        message[i, 32:] = high


def put_terms(ref, row, v):
    hi = v.astype(bf16).astype(f32)
    mid = (v - hi).astype(bf16).astype(f32)
    lo = v - hi - mid
    zero = jnp.zeros((EXTRA - 3, v.shape[1]), f32)
    ref[row:, : v.shape[1]] = jnp.concatenate([hi, mid, lo, zero], axis=0).astype(bf16)


def tail_kernel(ids, weight, stats, low_tops, tops, e_high, pos, m0, m1, m2, m3, rates):
    n = pos.shape[2]

    def merged(at, levels):
        lse = stats[:, at : at + levels]
        best = jnp.max(lse, axis=0)
        mass = jnp.sum(jnp.exp(lse - best[None]), axis=0)
        return best + jnp.log(mass), jnp.sum(stats[:, at + levels : at + levels + 1], axis=0)

    on = ids[Y] == 0
    loss = jnp.zeros((1, n), f32)
    for j in range(4):
        lse, picked = merged(8 * j, LOW)
        loss -= picked
        rows = []
        for k in range(LOW):
            loss += weight[k] * lse[k : k + 1]
            scale = jnp.where(on, weight[k] * FACTORS[k], 0.0)
            rows.append(scale * jnp.exp(low_tops[j, k : k + 1] - lse[k : k + 1]))
        rates[j] = jnp.concatenate(rows + rows[:3], axis=0)

    hot = find_positives(ids, pos[ids[Y]], n)
    lse, picked = merged(32, 2)
    loss = jnp.where(on, loss, 0.0) - picked
    tail = None
    tails = []
    for i in (1, 0):
        loss += weight[LOW + i] * lse[i : i + 1]
        scale = weight[LOW + i] * FACTORS[LOW + i]
        rate = scale * jnp.exp(tops[i : i + 1] - lse[i : i + 1])
        g = e_high[i] * rate - jnp.where(hot, scale, 0.0)
        tail = g if tail is None else tail + g
        tails.append(tail.astype(bf16))
    lane = lax.broadcasted_iota(jnp.int32, (1, n), 1)
    mine = ids[ZL] * FEAT + ids[Y] * 2 + ids[CORE]
    loss = jnp.where(lane == mine, jnp.sum(loss, axis=1, keepdims=True), 0.0)
    for t, m in enumerate((m0, m1, m2, m3)):
        narrow = ((ids[Y] + t) & 3) <= 1

        @pl.when(narrow)
        def _():
            m[: 4 * n] = tails[1]

        @pl.when(jnp.logical_not(narrow))
        def _():
            m[: 4 * n] = tails[0]

        put_terms(m, 4 * n, loss)


def get_terms(ref, row, lanes):
    v = ref[row:, :lanes].astype(f32)
    return v[0:1] + v[1:2] + v[2:3]


def low_grad_kernel(ids, weight, e_low, rates, pos, p, q_all, gq, gp, tails):
    n = pos.shape[2]
    on = ids[Y] == 0
    for j in range(4):
        hot = find_positives(ids, pos[j], n)
        acc = None
        for k in reversed(range(LOW)):
            scale = jnp.where(on, weight[k] * FACTORS[k], 0.0)
            g = e_low[k, j] * rates[j, k : k + 1] - jnp.where(hot, scale, 0.0)
            acc = g if acc is None else acc + g
            tails[k, :, j * n : j * n + n] = acc.astype(bf16)

    q = q_all[...].reshape(4 * n, q_all.shape[2])
    first = lax.broadcasted_iota(jnp.int32, (4 * n, PAIR), 1) < SMALLEST

    def fill(out, fn):
        out[:, :PAIR] = jnp.where(first, fn(0, 0, PAIR), fn(1, 0, PAIR))
        for k in range(2, LOW):
            begin, end = SPANS[k]
            out[:, begin:end] = fn(k, begin, end)

    fill(gq, lambda k, a, b: dot(tails[k], p[:, a:b], 0, 0))
    fill(gp, lambda k, a, b: dot(tails[k], q[:, a:b], 1, 0))


def query_grad_kernel(ids, t0, t1, t2, t3, gq_low, p, gq0, gq1, gq2, gq3, tail, row, gq):
    n, wide = gq0.shape
    loss = jnp.zeros((1, n), f32)
    for t, ref in enumerate((t0, t1, t2, t3)):
        j = (ids[Y] + 4 - t) & 3
        tail[:, pl.ds(pl.multiple_of(j * n, n), n)] = ref[: 4 * n]
        loss += get_terms(ref, 4 * n, n)
    row[...] = jnp.broadcast_to(loss, row.shape)
    gq[...] = dot(tail[...], p[...], 0, 0) + gq_low[...]
    for s, out in enumerate((gq0, gq1, gq2, gq3)):
        j = (ids[X] + 4 - s) & 3
        out[...] = gq[pl.ds(pl.multiple_of(j * n, n), n), :].astype(out.dtype)


def passage_grad_kernel(ids, tail, row, gp_low, q_all, own, message):
    n = q_all.shape[1]
    width = own.shape[1]
    q = q_all[...].reshape(4 * n, 2 * width)
    message[4 * n :] = jnp.zeros((EXTRA, width), bf16)
    put_terms(message, 4 * n, row[0:1])
    for c in (0, 1):
        lanes = slice(c * width, c * width + width)
        gp = dot(tail[...], q[:, lanes], 1, 0) + gp_low[:, lanes]

        @pl.when(ids[CORE] == c)
        def _():
            own[...] = gp

        @pl.when(ids[CORE] != c)
        def _():
            message[: 4 * n] = gp.astype(bf16)


def core_sum_kernel(gp_own, row, other, own, m1, m2, m3, loss):
    n, width = own.shape
    total = row[0:1] + get_terms(other, 4 * n, n)
    loss[...] = jnp.broadcast_to(total, loss.shape)
    for s, out in enumerate((own, m1, m2, m3)):
        rows = slice(s * n, s * n + n)
        v = gp_own[rows] + other[rows].astype(f32)
        out[:n] = v.astype(out.dtype)
        if s:
            out[n:] = jnp.zeros((EXTRA, width), bf16)
            put_terms(out, n, total)


def query_sum_kernel(ids, gq0, g1, g2, g3, m1, m2, m3, own, near, far):
    width = own.shape[1]
    same = ids[ZH] == ids[CORE]
    for c in (0, 1):
        lanes = slice(c * width, c * width + width)
        v = gq0[:, lanes] + (
            g1[:, lanes].astype(f32) + g2[:, lanes].astype(f32) + g3[:, lanes].astype(f32)
        )

        @pl.when(ids[CORE] == c)
        def _():
            own[...] = v

        @pl.when((ids[CORE] == c) != same)
        def _():
            near[...] = v.astype(bf16)

        @pl.when(ids[CORE] != c)
        def _():
            far[...] = v.astype(bf16)


def per_device(queries, passages, positives, level_weight):
    n, width = queries.shape
    wide = 2 * width
    bi = lax.axis_index("batch")
    fi = lax.axis_index("feat")
    core = fi % 2
    same = bi % 2 == core
    ids = jnp.stack([bi // 8, fi // 2, bi % 8 // 2, bi % 2, core]).astype(jnp.int32)

    rows = jnp.stack([positives // 64, positives % 64]).astype(bf16)
    rows = jnp.pad(rows, ((0, EXTRA - 2), (0, width - n)))
    q_row = jnp.concatenate([queries, rows], axis=0)
    near = move_square(queries, lambda h, c: (1 - h, c) if h == c else (h, 1 - c))
    far = move_square(q_row, lambda h, c: None if h == c else (1 - h, 1 - c))
    (q_msg,) = call(
        pack_kernel, [ids], [q_row, near, far], [shape(n + EXTRA, wide, bf16)]
    )
    q_msgs = [q_msg] + [shift_x(q_msg, s) for s in (1, 2, 3)]

    p_next, p_before = shift_zl(passages, 1), shift_zl(passages, 3)
    p_own = [passages, p_next, shift_zl(p_next, 1), p_before]
    p_other = [swap_core(a) for a in p_own]

    tile = 4 * n * 4 * n
    *partial, p, q, pos = call(
        score_kernel, [ids], [*p_own[1:], *p_other, *q_msgs, passages],
        [shape(4 * n, n, f32)] * 4
        + [
            shape(4 * n, wide, bf16),
            shape(4, n, wide, bf16),
            shape(4, 1, n, jnp.int32),
        ],
        scratch=[pltpu.VMEM((n, width), bf16), pltpu.SemaphoreType.DMA],
        flops=2 * tile * wide, in_place=1,
    )
    pieces = [partial[0]] + [shift_y(partial[t], t) for t in (1, 2, 3)]
    e_low, low_stats, low_tops = call(
        low_kernel, [ids, level_weight], [p, q, pos],
        [shape(LOW, 4, 4 * n, n, f32), shape(4, 8, n, f32), shape(4, 8, n, f32)],
        flops=2 * tile * wide,
    )
    e_high, message, tops = call(
        owner_kernel, [ids, level_weight], [*pieces, pos, low_stats],
        [shape(2, 4 * n, n, f32), shape(8, 40, n, f32), shape(8, n, f32)],
    )
    stats = lax.all_to_all(message, "batch", 0, 0, axis_index_groups=XZH_GROUPS)
    *tails, rates = call(
        tail_kernel, [ids, level_weight], [stats, low_tops, tops, e_high, pos],
        [shape(4 * n + EXTRA, n, bf16)] * 4 + [shape(4, 8, n, f32)],
    )
    tails = [tails[0]] + [shift_y(tails[t], t) for t in (1, 2, 3)]
    gq_low, gp_low = call(
        low_grad_kernel, [ids, level_weight], [e_low, rates, pos, p, q],
        [shape(4 * n, wide, f32)] * 2,
        scratch=[pltpu.VMEM((LOW, 4 * n, 4 * n), bf16)],
        flops=4 * tile * wide, grant=12,
    )
    gq0, gq1, gq2, gq3, tail, row = call(
        query_grad_kernel, [ids], [*tails, gq_low, p],
        [shape(n, wide, f32)]
        + [shape(n, wide, bf16)] * 3
        + [shape(4 * n, 4 * n, bf16), shape(8, n, f32)],
        scratch=[pltpu.VMEM((4 * n, wide), f32)],
        flops=2 * tile * wide,
    )
    gp_own, message = call(
        passage_grad_kernel, [ids], [tail, row, gp_low, q],
        [shape(4 * n, width, f32), shape(4 * n + EXTRA, width, bf16)],
        flops=2 * tile * wide,
    )
    gq = [shift_x(g, -s) for s, g in enumerate((gq1, gq2, gq3), 1)]

    own, *messages, loss_row = call(
        core_sum_kernel, [], [gp_own, row, swap_core(message)],
        [shape(n, width, f32)] + [shape(n + EXTRA, width, bf16)] * 3 + [shape(8, n, f32)],
    )
    gp = [shift_zl(m, -s) for s, m in enumerate(messages, 1)]
    gq_own, near, far = call(
        query_sum_kernel, [ids], [gq0, *gq, *messages],
        [shape(n, width, f32)] + [shape(n, width, bf16)] * 2, in_place=3,
    )
    near = move_square(near, lambda h, c: (h, 1 - c) if h == c else (1 - h, c)).astype(f32)
    far = move_square(far, lambda h, c: None if h == c else (1 - h, 1 - c)).astype(f32)
    grad_queries = (near + jnp.where(same, gq_own, far)).astype(bf16)

    grad_passages = own + sum(g[:n].astype(f32) for g in gp)
    loss_row = loss_row[0] + sum(jnp.sum(g[n : n + 3, :n].astype(f32), axis=0) for g in gp)
    loss = jnp.sum(loss_row) / (n * BATCH)
    return loss, grad_queries, grad_passages.astype(bf16)


def solution(mesh):
    in_specs = (P("batch", "feat"), P("batch", "feat"), P("batch"), P())
    out_specs = (P(), P("batch", "feat"), P("batch", "feat"))
    return jax.shard_map(
        per_device, mesh=mesh, in_specs=in_specs, out_specs=out_specs, check_vma=False
    )
```

```python
import math

import jax
import jax.numpy as jnp
from jax import lax
from jax.experimental import pallas as pl
from jax.experimental.pallas import tpu as pltpu
from jax.sharding import PartitionSpec as P

SMALLEST = 64
LEVELS = 7
LOW = 5
SHARPNESS = 3.0
WIDTHS = [SMALLEST * 2**k for k in range(LEVELS)]
FACTORS = [SHARPNESS / math.sqrt(w) for w in WIDTHS]
SPANS = list(zip([0] + WIDTHS[: LOW - 1], WIDTHS[:LOW]))
EXTRA = 16
PAIR = 2 * SMALLEST

BATCH = 32
FEAT = 8
BOTH = ("batch", "feat")
XZH_GROUPS = [[x * 8 + zl * 2 + zh for x in range(4) for zh in range(2)] for zl in range(4)]
X, Y, ZL, ZH, CORE = range(5)

f32 = jnp.float32
bf16 = jnp.bfloat16


def shift_x(a, s):
    return lax.ppermute(a, "batch", [(b, (b + 8 * s) % BATCH) for b in range(BATCH)])


def shift_zl(a, s):
    return lax.ppermute(
        a, "batch", [(b, b // 8 * 8 + (b + 2 * s) % 8) for b in range(BATCH)]
    )


def shift_y(a, s):
    return lax.ppermute(a, "feat", [(f, (f + 2 * s) % FEAT) for f in range(FEAT)])


def swap_core(a):
    return lax.ppermute(a, "feat", [(f, f ^ 1) for f in range(FEAT)])


def move_square(a, rule):
    pairs = []
    for b in range(BATCH):
        for f in range(FEAT):
            to = rule(b % 2, f % 2)
            if to is not None:
                pairs.append((b * FEAT + f, (b - b % 2 + to[0]) * FEAT + f - f % 2 + to[1]))
    return lax.ppermute(a, BOTH, pairs)


def dot(a, b, ca, cb):
    return lax.dot_general(
        a, b, (((ca,), (cb,)), ((), ())), preferred_element_type=f32
    )


def shape(*dims_dtype):
    return jax.ShapeDtypeStruct(dims_dtype[:-1], dims_dtype[-1])


def call(body, smem, args, outs, scratch=(), flops=0, grant=8, in_place=0, fixed=False):
    vmem = pl.BlockSpec(memory_space=pltpu.VMEM)
    scalar = pl.BlockSpec(memory_space=pltpu.SMEM)
    moved = sum(a.size * a.dtype.itemsize for a in (*args, *outs))
    return pl.pallas_call(
        body,
        out_shape=outs,
        in_specs=[scalar] * len(smem)
        + [vmem] * (len(args) - in_place)
        + [pl.BlockSpec(memory_space=pltpu.HBM if fixed else pl.ANY)] * in_place,
        out_specs=[vmem] * len(outs),
        scratch_shapes=list(scratch),
        cost_estimate=pl.CostEstimate(
            flops=flops, bytes_accessed=moved, transcendentals=0
        ),
        compiler_params=pltpu.CompilerParams(vmem_limit_bytes=grant << 20),
    )(*smem, *args)


def find_positives(ids, pos, n):
    rows = lax.broadcasted_iota(jnp.int32, (4 * n, n), 0)
    bits = n.bit_length() - 1
    block = ids[X] * 8 + ids[ZH] + 2 * ((ids[ZL] + 4 - (rows >> bits)) & 3)
    return (block << bits) + (rows & (n - 1)) == pos


def pack_kernel(ids, own, near, far, out):
    n, width = near.shape
    same = ids[ZH] == ids[CORE]

    def put(first, second, rows):
        out[:n, :width] = first[:n]
        out[:n, width:] = second[:n]
        out[n:, :width] = rows[n:]

    out[n:, width:] = jnp.zeros((EXTRA, width), bf16)
    for core in (0, 1):
        for matches in (True, False):
            a, b = (own, near) if matches else (near, far)
            if core:
                a, b = b, a

            @pl.when((ids[CORE] == core) & (same == matches))
            def _():
                put(a, b, own if matches else far)


def digit_kernel(ids, positives, queries, out, arrived):
    n, width = queries.shape
    copy = pltpu.make_async_copy(queries, out.at[pl.ds(0, n)], arrived)
    copy.start()
    p = positives[...]
    digits = jnp.concatenate([p >> 6, p & 63], axis=0).astype(f32)
    out[n:] = jnp.zeros((EXTRA, width), bf16)
    rows = jnp.concatenate([digits, jnp.zeros((EXTRA - 2, n), f32)], axis=0)
    out[n:, :n] = rows.astype(bf16)
    copy.wait()


def gather_kernel(ids, after, before, own, out, arrived):
    n = after.shape[0]
    copy = pltpu.make_async_copy(own, out.at[pl.ds(0, n)], arrived)
    copy.start()
    out[n : 2 * n] = after[...]
    out[2 * n :] = before[...]
    copy.wait()


def score_kernel(
    ids, near, other_near, far, other_far, q0, q1, q2, q3, s0, s1, s2, s3, p, q_all, pos
):
    n, width = far.shape
    for core in (0, 1):
        for own, other, take, put in (
            (near, other_near, slice(0, 2 * n), slice(0, 2 * n)),
            (far, other_far, slice(0, n), slice(2 * n, 3 * n)),
            (near, other_near, slice(2 * n, 3 * n), slice(3 * n, 4 * n)),
        ):

            @pl.when(ids[CORE] == core)
            def _():
                first, second = (other, own) if core else (own, other)
                p[put, :width] = first[take]
                p[put, width:] = second[take]

    for s, q in enumerate((q0, q1, q2, q3)):
        j = (ids[X] + 4 - s) & 3
        q_all[j] = q[:n]
        digits = q[n:, :n].astype(f32)
        pos[j] = (digits[0:1] * 64.0 + digits[1:2]).astype(jnp.int32)
    for t, out in enumerate((s0, s1, s2, s3)):
        out[...] = dot(p[...], q_all[(ids[Y] + t) & 3], 1, 1)


def level(scores, hot, weight):
    top = jnp.max(scores, axis=0, keepdims=True)
    e = jnp.exp(scores - top)
    lse = top + jnp.log(jnp.sum(e, axis=0, keepdims=True))
    picked = weight * jnp.sum(jnp.where(hot, scores, 0.0), axis=0, keepdims=True)
    return e, top, lse, picked


def low_kernel(ids, weight, p, q_all, pos, e_low, stats, tops):
    n = q_all.shape[1]
    first = lax.broadcasted_iota(jnp.int32, (n, PAIR), 1) < SMALLEST
    for j in range(4):
        hot = find_positives(ids, pos[j], n)
        rows, lses, total = [], [], jnp.zeros((1, n), f32)
        running = None
        for k, (begin, end) in enumerate(SPANS):
            if k == 0:
                q_part = q_all[j, :, :PAIR]
                q_part = jnp.where(first, q_part, jnp.zeros_like(q_part))
                running = dot(p[:, :PAIR], q_part, 1, 1)
            elif k == 1:
                running = dot(p[:, :PAIR], q_all[j, :, :PAIR], 1, 1)
            else:
                running = running + dot(p[:, begin:end], q_all[j, :, begin:end], 1, 1)
            e_low[k, j], top, lse, picked = level(running * FACTORS[k], hot, weight[k])
            rows.append(top)
            lses.append(lse)
            total += picked
        tops[j] = jnp.concatenate(rows + rows[:3], axis=0)
        stats[j] = jnp.concatenate(lses + [total, total, total], axis=0)


def owner_kernel(ids, weight, s0, s1, s2, s3, pos, low_stats, e_high, message, tops):
    n = pos.shape[2]
    hot = find_positives(ids, pos[ids[Y]], n)
    sum5 = sum6 = None
    for t, ref in enumerate((s0, s1, s2, s3)):
        v = ref[...]
        part = jnp.where(((ids[Y] + 4 - t) & 3) <= 1, v, 0.0)
        sum5 = part if t == 0 else sum5 + part
        sum6 = v if t == 0 else sum6 + v
    e_high[0], top5, lse5, picked5 = level(sum5 * FACTORS[5], hot, weight[5])
    e_high[1], top6, lse6, picked6 = level(sum6 * FACTORS[6], hot, weight[6])
    tops[...] = jnp.concatenate([top5, top6] * 4, axis=0)
    high = jnp.concatenate([lse5, lse6] + [picked5 + picked6] * 6, axis=0)
    for i in range(8):
        for j in range(4):
            message[i, 8 * j : 8 * j + 8] = low_stats[j]
        message[i, 32:] = high


def put_terms(ref, row, v):
    hi = v.astype(bf16).astype(f32)
    mid = (v - hi).astype(bf16).astype(f32)
    lo = v - hi - mid
    zero = jnp.zeros((EXTRA - 3, v.shape[1]), f32)
    ref[row:, : v.shape[1]] = jnp.concatenate([hi, mid, lo, zero], axis=0).astype(bf16)


def tail_kernel(ids, weight, stats, low_tops, tops, e_high, pos, m0, m1, m2, m3, rates):
    n = pos.shape[2]

    def merged(at, levels):
        lse = stats[:, at : at + levels]
        best = jnp.max(lse, axis=0)
        mass = jnp.sum(jnp.exp(lse - best[None]), axis=0)
        return best + jnp.log(mass), jnp.sum(stats[:, at + levels : at + levels + 1], axis=0)

    on = ids[Y] == 0
    loss = jnp.zeros((1, n), f32)
    for j in range(4):
        lse, picked = merged(8 * j, LOW)
        loss -= picked
        rows = []
        for k in range(LOW):
            loss += weight[k] * lse[k : k + 1]
            scale = jnp.where(on, weight[k] * FACTORS[k], 0.0)
            rows.append(scale * jnp.exp(low_tops[j, k : k + 1] - lse[k : k + 1]))
        rates[j] = jnp.concatenate(rows + rows[:3], axis=0)

    hot = find_positives(ids, pos[ids[Y]], n)
    lse, picked = merged(32, 2)
    loss = jnp.where(on, loss, 0.0) - picked
    tail = None
    tails = []
    for i in (1, 0):
        loss += weight[LOW + i] * lse[i : i + 1]
        scale = weight[LOW + i] * FACTORS[LOW + i]
        rate = scale * jnp.exp(tops[i : i + 1] - lse[i : i + 1])
        g = e_high[i] * rate - jnp.where(hot, scale, 0.0)
        tail = g if tail is None else tail + g
        tails.append(tail.astype(bf16))
    lane = lax.broadcasted_iota(jnp.int32, (1, n), 1)
    mine = ids[ZL] * FEAT + ids[Y] * 2 + ids[CORE]
    loss = jnp.where(lane == mine, jnp.sum(loss, axis=1, keepdims=True), 0.0)
    for t, m in enumerate((m0, m1, m2, m3)):
        narrow = ((ids[Y] + t) & 3) <= 1

        @pl.when(narrow)
        def _():
            m[: 4 * n] = tails[1]

        @pl.when(jnp.logical_not(narrow))
        def _():
            m[: 4 * n] = tails[0]

        put_terms(m, 4 * n, loss)


def get_terms(ref, row, lanes):
    v = ref[row:, :lanes].astype(f32)
    return v[0:1] + v[1:2] + v[2:3]


def low_grad_kernel(ids, weight, e_low, rates, pos, p, q_all, gq, gp, tails):
    n = pos.shape[2]
    on = ids[Y] == 0
    for j in range(4):
        hot = find_positives(ids, pos[j], n)
        acc = None
        for k in reversed(range(LOW)):
            scale = jnp.where(on, weight[k] * FACTORS[k], 0.0)
            g = e_low[k, j] * rates[j, k : k + 1] - jnp.where(hot, scale, 0.0)
            acc = g if acc is None else acc + g
            tails[k, :, j * n : j * n + n] = acc.astype(bf16)

    q = q_all[...].reshape(4 * n, q_all.shape[2])
    first = lax.broadcasted_iota(jnp.int32, (4 * n, PAIR), 1) < SMALLEST

    def fill(out, fn):
        out[:, :PAIR] = jnp.where(first, fn(0, 0, PAIR), fn(1, 0, PAIR))
        for k in range(2, LOW):
            begin, end = SPANS[k]
            out[:, begin:end] = fn(k, begin, end)

    fill(gq, lambda k, a, b: dot(tails[k], p[:, a:b], 0, 0))
    fill(gp, lambda k, a, b: dot(tails[k], q[:, a:b], 1, 0))


def passage_grad_kernel(ids, t0, t1, t2, t3, gp_low, q_all, own, message, tail, row):
    n = q_all.shape[1]
    width = own.shape[1]
    loss = jnp.zeros((1, n), f32)
    for t, ref in enumerate((t0, t1, t2, t3)):
        j = (ids[Y] + 4 - t) & 3
        tail[:, pl.ds(pl.multiple_of(j * n, n), n)] = ref[: 4 * n]
        loss += get_terms(ref, 4 * n, n)
    row[...] = jnp.broadcast_to(loss, row.shape)
    q = q_all[...].reshape(4 * n, 2 * width)
    message[4 * n :] = jnp.zeros((EXTRA, width), bf16)
    put_terms(message, 4 * n, loss)
    for c in (0, 1):
        lanes = slice(c * width, c * width + width)
        gp = dot(tail[...], q[:, lanes], 1, 0) + gp_low[:, lanes]

        @pl.when(ids[CORE] == c)
        def _():
            own[...] = gp

        @pl.when(ids[CORE] != c)
        def _():
            message[: 4 * n] = gp.astype(bf16)


def query_grad_kernel(ids, tail, gq_low, p, message, gq0, gq1, gq2, gq3, gq):
    n = gq0.shape[0]
    gq[...] = dot(tail[...], p[...], 0, 0) + gq_low[...]
    for s, out in enumerate((gq0, gq1, gq2, gq3)):
        j = (ids[X] + 4 - s) & 3
        out[...] = gq[pl.ds(pl.multiple_of(j * n, n), n), :].astype(out.dtype)


def core_sum_kernel(ids, gp_own, row, other, own, after, far, before, loss):
    n, width = own.shape
    total = row[0:1] + get_terms(other, 4 * n, n)
    loss[...] = jnp.broadcast_to(total, loss.shape)
    for s, out in enumerate((own, after, far, before)):
        rows = slice(s * n, s * n + n)
        v = gp_own[rows] + other[rows].astype(f32)
        out[:n] = v.astype(out.dtype)
        if s >= 2:
            out[n:] = jnp.zeros((EXTRA, width), bf16)
            put_terms(out, n, total)


def middle_kernel(
    ids, gq0, g1, g2, g3, gp_own, after, far_in, before_in, row,
    own, near, far, relay, gp_sum, loss,
):
    n, width = own.shape
    relay[n:] = jnp.zeros((EXTRA, width), bf16)
    put_terms(relay, n, row[0:1] + get_terms(far_in, n, n))
    relay[:n] = (after[...] + far_in[:n].astype(f32)).astype(bf16)
    gp_sum[...] = gp_own[...] + before_in[:n].astype(f32)
    loss[...] = jnp.broadcast_to(row[0:1] + get_terms(before_in, n, n), loss.shape)
    same = ids[ZH] == ids[CORE]
    for c in (0, 1):
        lanes = slice(c * width, c * width + width)
        v = gq0[:, lanes] + (
            g1[:, lanes].astype(f32) + g2[:, lanes].astype(f32) + g3[:, lanes].astype(f32)
        )

        @pl.when(ids[CORE] == c)
        def _():
            own[...] = v

        @pl.when((ids[CORE] == c) != same)
        def _():
            near[...] = v.astype(bf16)

        @pl.when(ids[CORE] != c)
        def _():
            far[...] = v.astype(bf16)


def last_kernel(ids, gq_own, near, far, gp_sum, relay, row, gq, gp, loss):
    n = gq.shape[0]

    @pl.when(ids[ZH] == ids[CORE])
    def _():
        gq[...] = (gq_own[...] + near[...].astype(f32)).astype(bf16)

    @pl.when(ids[ZH] != ids[CORE])
    def _():
        gq[...] = (far[...].astype(f32) + near[...].astype(f32)).astype(bf16)

    gp[...] = (gp_sum[...] + relay[:n].astype(f32)).astype(bf16)
    total = row[0:1] + get_terms(relay, n, n)
    loss[...] = jnp.sum(total, axis=1, keepdims=True) * (1.0 / (n * BATCH))


def per_device(queries, passages, positives, level_weight):
    n, width = queries.shape
    wide = 2 * width
    bi = lax.axis_index("batch")
    fi = lax.axis_index("feat")
    ids = jnp.stack([bi // 8, fi // 2, bi % 8 // 2, bi % 2, fi % 2]).astype(jnp.int32)
    dma = pltpu.SemaphoreType.DMA

    near = move_square(queries, lambda h, c: (1 - h, c) if h == c else (h, 1 - c))
    (q_row,) = call(
        digit_kernel, [ids], [positives.reshape(1, n), queries],
        [shape(n + EXTRA, width, bf16)], scratch=[dma], in_place=1, fixed=True,
    )
    far = move_square(q_row, lambda h, c: None if h == c else (1 - h, 1 - c))
    (q_msg,) = call(
        pack_kernel, [ids], [q_row, near, far], [shape(n + EXTRA, wide, bf16)]
    )
    q_msgs = [q_msg] + [shift_x(q_msg, s) for s in (1, 2, 3)]

    p_next, p_before = shift_zl(passages, 1), shift_zl(passages, 3)
    (p_near,) = call(
        gather_kernel, [ids], [p_next, p_before, passages],
        [shape(3 * n, width, bf16)], scratch=[dma], in_place=1, fixed=True,
    )
    p_far = shift_zl(p_next, 1)

    tile = 4 * n * 4 * n
    *partial, p, q, pos = call(
        score_kernel, [ids], [p_near, swap_core(p_near), p_far, swap_core(p_far), *q_msgs],
        [shape(4 * n, n, f32)] * 4
        + [
            shape(4 * n, wide, bf16),
            shape(4, n, wide, bf16),
            shape(4, 1, n, jnp.int32),
        ],
        flops=2 * tile * wide,
    )
    pieces = [partial[0]] + [shift_y(partial[t], t) for t in (1, 2, 3)]
    e_low, low_stats, low_tops = call(
        low_kernel, [ids, level_weight], [p, q, pos],
        [shape(LOW, 4, 4 * n, n, f32), shape(4, 8, n, f32), shape(4, 8, n, f32)],
        flops=2 * tile * wide,
    )
    e_high, message, tops = call(
        owner_kernel, [ids, level_weight], [*pieces, pos, low_stats],
        [shape(2, 4 * n, n, f32), shape(8, 40, n, f32), shape(8, n, f32)],
    )
    stats = lax.all_to_all(message, "batch", 0, 0, axis_index_groups=XZH_GROUPS)
    *tails, rates = call(
        tail_kernel, [ids, level_weight], [stats, low_tops, tops, e_high, pos],
        [shape(4 * n + EXTRA, n, bf16)] * 4 + [shape(4, 8, n, f32)],
    )
    tails = [tails[0]] + [shift_y(tails[t], t) for t in (1, 2, 3)]
    gq_low, gp_low = call(
        low_grad_kernel, [ids, level_weight], [e_low, rates, pos, p, q],
        [shape(4 * n, wide, f32)] * 2,
        scratch=[pltpu.VMEM((LOW, 4 * n, 4 * n), bf16)],
        flops=4 * tile * wide, grant=12,
    )
    gp_own, message, tail, row = call(
        passage_grad_kernel, [ids], [*tails, gp_low, q],
        [
            shape(4 * n, width, f32),
            shape(4 * n + EXTRA, width, bf16),
            shape(4 * n, 4 * n, bf16),
            shape(8, n, f32),
        ],
        flops=2 * tile * wide,
    )
    other = swap_core(message)
    gq0, gq1, gq2, gq3 = call(
        query_grad_kernel, [ids], [tail, gq_low, p, message],
        [shape(n, wide, f32)] + [shape(n, wide, bf16)] * 3,
        scratch=[pltpu.VMEM((4 * n, wide), f32)],
        flops=2 * tile * wide, in_place=1,
    )
    gq = [shift_x(g, -s) for s, g in enumerate((gq1, gq2, gq3), 1)]
    gp_own, after, far, before, row = call(
        core_sum_kernel, [ids], [gp_own, row, other],
        [shape(n, width, f32)] * 2
        + [shape(n + EXTRA, width, bf16)] * 2
        + [shape(8, n, f32)],
    )
    far_in, before_in = shift_zl(far, -1), shift_zl(before, 1)
    gq_own, near, far, relay, gp_sum, row = call(
        middle_kernel, [ids], [gq0, *gq, gp_own, after, far_in, before_in, row],
        [shape(n, width, f32)]
        + [shape(n, width, bf16)] * 2
        + [shape(n + EXTRA, width, bf16), shape(n, width, f32), shape(8, n, f32)],
    )
    near = move_square(near, lambda h, c: (h, 1 - c) if h == c else (1 - h, c))
    far = move_square(far, lambda h, c: None if h == c else (1 - h, 1 - c))
    relay = shift_zl(relay, -1)
    grad_queries, grad_passages, loss = call(
        last_kernel, [ids], [gq_own, near, far, gp_sum, relay, row],
        [shape(n, width, bf16), shape(n, width, bf16), shape(1, 1, f32)],
    )
    return loss.reshape(()), grad_queries, grad_passages


def solution(mesh):
    in_specs = (P("batch", "feat"), P("batch", "feat"), P("batch"), P())
    out_specs = (P(), P("batch", "feat"), P("batch", "feat"))
    return jax.shard_map(
        per_device, mesh=mesh, in_specs=in_specs, out_specs=out_specs, check_vma=False
    )
```

```python
import math

import jax
import jax.numpy as jnp
from jax import lax
from jax.experimental import pallas as pl
from jax.experimental.pallas import tpu as pltpu
from jax.sharding import PartitionSpec as P

SMALLEST = 64
LEVELS = 7
LOW = 5
SHARPNESS = 3.0
WIDTHS = [SMALLEST * 2**k for k in range(LEVELS)]
FACTORS = [SHARPNESS / math.sqrt(w) for w in WIDTHS]
SPANS = list(zip([0] + WIDTHS[: LOW - 1], WIDTHS[:LOW]))
LONG = 20_000_000_000
EXTRA = 16
PAIR = 2 * SMALLEST

BATCH = 32
FEAT = 8
BOTH = ("batch", "feat")
XZH_GROUPS = [[x * 8 + zl * 2 + zh for x in range(4) for zh in range(2)] for zl in range(4)]
X, Y, ZL, ZH, CORE = range(5)

f32 = jnp.float32
bf16 = jnp.bfloat16


def shift_x(a, s):
    return lax.ppermute(a, "batch", [(b, (b + 8 * s) % BATCH) for b in range(BATCH)])


def shift_zl(a, s):
    return lax.ppermute(
        a, "batch", [(b, b // 8 * 8 + (b + 2 * s) % 8) for b in range(BATCH)]
    )


def shift_y(a, s):
    return lax.ppermute(a, "feat", [(f, (f + 2 * s) % FEAT) for f in range(FEAT)])


def swap_core(a):
    return lax.ppermute(a, "feat", [(f, f ^ 1) for f in range(FEAT)])


def move_square(a, rule):
    pairs = []
    for b in range(BATCH):
        for f in range(FEAT):
            to = rule(b % 2, f % 2)
            if to is not None:
                pairs.append((b * FEAT + f, (b - b % 2 + to[0]) * FEAT + f - f % 2 + to[1]))
    return lax.ppermute(a, BOTH, pairs)


def dot(a, b, ca, cb):
    return lax.dot_general(
        a, b, (((ca,), (cb,)), ((), ())), preferred_element_type=f32
    )


def shape(*dims_dtype):
    return jax.ShapeDtypeStruct(dims_dtype[:-1], dims_dtype[-1])


def call(body, smem, args, outs, scratch=(), flops=0, grant=8, in_place=0):
    vmem = pl.BlockSpec(memory_space=pltpu.VMEM)
    scalar = pl.BlockSpec(memory_space=pltpu.SMEM)
    moved = sum(a.size * a.dtype.itemsize for a in (*args, *outs))
    return pl.pallas_call(
        body,
        out_shape=outs,
        in_specs=[scalar] * len(smem)
        + [vmem] * (len(args) - in_place)
        + [pl.BlockSpec(memory_space=pl.ANY)] * in_place,
        out_specs=[vmem] * len(outs),
        scratch_shapes=list(scratch),
        cost_estimate=pl.CostEstimate(
            flops=flops, bytes_accessed=moved, transcendentals=0
        ),
        compiler_params=pltpu.CompilerParams(vmem_limit_bytes=grant << 20),
    )(*smem, *args)


def find_positives(ids, pos, n):
    rows = lax.broadcasted_iota(jnp.int32, (4 * n, n), 0)
    bits = n.bit_length() - 1
    block = ids[X] * 8 + ids[ZH] + 2 * ((ids[ZL] + 4 - (rows >> bits)) & 3)
    return (block << bits) + (rows & (n - 1)) == pos


def pack_kernel(ids, own, near, far, out):
    n, width = near.shape
    same = ids[ZH] == ids[CORE]

    def put(first, second, rows):
        out[:n, :width] = first[:n]
        out[:n, width:] = second[:n]
        out[n:, :width] = rows[n:]

    out[n:, width:] = jnp.zeros((EXTRA, width), bf16)
    for core in (0, 1):
        for matches in (True, False):
            a, b = (own, near) if matches else (near, far)
            if core:
                a, b = b, a

            @pl.when((ids[CORE] == core) & (same == matches))
            def _():
                put(a, b, own if matches else far)


def hold_kernel(ids, a, out):
    out[...] = a[...]


def score_kernel(
    ids, p0, p1, p2, p3, o0, o1, o2, o3, q0, q1, q2, q3, s0, s1, s2, s3, p, q_all, pos
):
    n, width = p0.shape
    for s, (own, other) in enumerate(zip((p0, p1, p2, p3), (o0, o1, o2, o3))):
        rows = slice(s * n, s * n + n)

        @pl.when(ids[CORE] == 0)
        def _():
            p[rows, :width] = own[...]
            p[rows, width:] = other[...]

        @pl.when(ids[CORE] != 0)
        def _():
            p[rows, :width] = other[...]
            p[rows, width:] = own[...]

    for s, q in enumerate((q0, q1, q2, q3)):
        j = (ids[X] + 4 - s) & 3
        q_all[j] = q[:n]
        digits = q[n:, :n].astype(f32)
        pos[j] = (digits[0:1] * 64.0 + digits[1:2]).astype(jnp.int32)
    for t, out in enumerate((s0, s1, s2, s3)):
        out[...] = dot(p[...], q_all[(ids[Y] + t) & 3], 1, 1)


def level(scores, hot, weight):
    top = jnp.max(scores, axis=0, keepdims=True)
    e = jnp.exp(scores - top)
    lse = top + jnp.log(jnp.sum(e, axis=0, keepdims=True))
    picked = weight * jnp.sum(jnp.where(hot, scores, 0.0), axis=0, keepdims=True)
    return e, top, lse, picked


def low_kernel(ids, weight, p, q_all, pos, e_low, stats, tops):
    n = q_all.shape[1]
    first = lax.broadcasted_iota(jnp.int32, (n, PAIR), 1) < SMALLEST
    for j in range(4):
        hot = find_positives(ids, pos[j], n)
        rows, lses, total = [], [], jnp.zeros((1, n), f32)
        running = None
        for k, (begin, end) in enumerate(SPANS):
            if k == 0:
                q_part = q_all[j, :, :PAIR]
                q_part = jnp.where(first, q_part, jnp.zeros_like(q_part))
                running = dot(p[:, :PAIR], q_part, 1, 1)
            elif k == 1:
                running = dot(p[:, :PAIR], q_all[j, :, :PAIR], 1, 1)
            else:
                running = running + dot(p[:, begin:end], q_all[j, :, begin:end], 1, 1)
            e_low[k, j], top, lse, picked = level(running * FACTORS[k], hot, weight[k])
            rows.append(top)
            lses.append(lse)
            total += picked
        tops[j] = jnp.concatenate(rows + rows[:3], axis=0)
        stats[j] = jnp.concatenate(lses + [total, total, total], axis=0)


def owner_kernel(ids, weight, s0, s1, s2, s3, pos, low_stats, e_high, message, tops):
    n = pos.shape[2]
    hot = find_positives(ids, pos[ids[Y]], n)
    sum5 = sum6 = None
    for t, ref in enumerate((s0, s1, s2, s3)):
        v = ref[...]
        part = jnp.where(((ids[Y] + 4 - t) & 3) <= 1, v, 0.0)
        sum5 = part if t == 0 else sum5 + part
        sum6 = v if t == 0 else sum6 + v
    e_high[0], top5, lse5, picked5 = level(sum5 * FACTORS[5], hot, weight[5])
    e_high[1], top6, lse6, picked6 = level(sum6 * FACTORS[6], hot, weight[6])
    tops[...] = jnp.concatenate([top5, top6] * 4, axis=0)
    high = jnp.concatenate([lse5, lse6] + [picked5 + picked6] * 6, axis=0)
    for i in range(8):
        for j in range(4):
            message[i, 8 * j : 8 * j + 8] = low_stats[j]
        message[i, 32:] = high


def put_terms(ref, row, v):
    hi = v.astype(bf16).astype(f32)
    mid = (v - hi).astype(bf16).astype(f32)
    lo = v - hi - mid
    zero = jnp.zeros((EXTRA - 3, v.shape[1]), f32)
    ref[row:, : v.shape[1]] = jnp.concatenate([hi, mid, lo, zero], axis=0).astype(bf16)


def tail_kernel(ids, weight, stats, low_tops, tops, e_high, pos, m0, m1, m2, m3, rates):
    n = pos.shape[2]

    def merged(at, levels):
        lse = stats[:, at : at + levels]
        best = jnp.max(lse, axis=0)
        mass = jnp.sum(jnp.exp(lse - best[None]), axis=0)
        return best + jnp.log(mass), jnp.sum(stats[:, at + levels : at + levels + 1], axis=0)

    on = ids[Y] == 0
    loss = jnp.zeros((1, n), f32)
    for j in range(4):
        lse, picked = merged(8 * j, LOW)
        loss -= picked
        rows = []
        for k in range(LOW):
            loss += weight[k] * lse[k : k + 1]
            scale = jnp.where(on, weight[k] * FACTORS[k], 0.0)
            rows.append(scale * jnp.exp(low_tops[j, k : k + 1] - lse[k : k + 1]))
        rates[j] = jnp.concatenate(rows + rows[:3], axis=0)

    hot = find_positives(ids, pos[ids[Y]], n)
    lse, picked = merged(32, 2)
    loss = jnp.where(on, loss, 0.0) - picked
    tail = None
    tails = []
    for i in (1, 0):
        loss += weight[LOW + i] * lse[i : i + 1]
        scale = weight[LOW + i] * FACTORS[LOW + i]
        rate = scale * jnp.exp(tops[i : i + 1] - lse[i : i + 1])
        g = e_high[i] * rate - jnp.where(hot, scale, 0.0)
        tail = g if tail is None else tail + g
        tails.append(tail.astype(bf16))
    lane = lax.broadcasted_iota(jnp.int32, (1, n), 1)
    mine = ids[ZL] * FEAT + ids[Y] * 2 + ids[CORE]
    loss = jnp.where(lane == mine, jnp.sum(loss, axis=1, keepdims=True), 0.0)
    for t, m in enumerate((m0, m1, m2, m3)):
        narrow = ((ids[Y] + t) & 3) <= 1

        @pl.when(narrow)
        def _():
            m[: 4 * n] = tails[1]

        @pl.when(jnp.logical_not(narrow))
        def _():
            m[: 4 * n] = tails[0]

        put_terms(m, 4 * n, loss)


def get_terms(ref, row, lanes):
    v = ref[row:, :lanes].astype(f32)
    return v[0:1] + v[1:2] + v[2:3]


def low_grad_kernel(ids, weight, e_low, rates, pos, p, q_all, gq, gp, tails):
    n = pos.shape[2]
    on = ids[Y] == 0
    for j in range(4):
        hot = find_positives(ids, pos[j], n)
        acc = None
        for k in reversed(range(LOW)):
            scale = jnp.where(on, weight[k] * FACTORS[k], 0.0)
            g = e_low[k, j] * rates[j, k : k + 1] - jnp.where(hot, scale, 0.0)
            acc = g if acc is None else acc + g
            tails[k, :, j * n : j * n + n] = acc.astype(bf16)

    q = q_all[...].reshape(4 * n, q_all.shape[2])
    first = lax.broadcasted_iota(jnp.int32, (4 * n, PAIR), 1) < SMALLEST

    def fill(out, fn):
        out[:, :PAIR] = jnp.where(first, fn(0, 0, PAIR), fn(1, 0, PAIR))
        for k in range(2, LOW):
            begin, end = SPANS[k]
            out[:, begin:end] = fn(k, begin, end)

    fill(gq, lambda k, a, b: dot(tails[k], p[:, a:b], 0, 0))
    fill(gp, lambda k, a, b: dot(tails[k], q[:, a:b], 1, 0))


def passage_grad_kernel(ids, tail, row, gp_low, q_all, own, message):
    n = q_all.shape[1]
    width = own.shape[1]
    q = q_all[...].reshape(4 * n, 2 * width)
    message[4 * n :] = jnp.zeros((EXTRA, width), bf16)
    put_terms(message, 4 * n, row[0:1])
    for c in (0, 1):
        lanes = slice(c * width, c * width + width)
        gp = dot(tail[...], q[:, lanes], 1, 0) + gp_low[:, lanes]

        @pl.when(ids[CORE] == c)
        def _():
            own[...] = gp

        @pl.when(ids[CORE] != c)
        def _():
            message[: 4 * n] = gp.astype(bf16)


def query_grad_kernel(ids, t0, t1, t2, t3, gq_low, p, gq0, gq1, gq2, gq3, tail, row, gq):
    n, wide = gq0.shape
    loss = jnp.zeros((1, n), f32)
    for t, ref in enumerate((t0, t1, t2, t3)):
        j = (ids[Y] + 4 - t) & 3
        tail[:, pl.ds(pl.multiple_of(j * n, n), n)] = ref[: 4 * n]
        loss += get_terms(ref, 4 * n, n)
    row[...] = jnp.broadcast_to(loss, row.shape)
    gq[...] = dot(tail[...], p[...], 0, 0) + gq_low[...]
    for s, out in enumerate((gq0, gq1, gq2, gq3)):
        j = (ids[X] + 4 - s) & 3
        out[...] = gq[pl.ds(pl.multiple_of(j * n, n), n), :].astype(out.dtype)


def core_sum_kernel(ids, gp_own, row, other, own, m1, m2, m3, loss):
    n, width = own.shape
    total = row[0:1] + get_terms(other, 4 * n, n)
    loss[...] = jnp.broadcast_to(total, loss.shape)
    for s, out in enumerate((own, m1, m2, m3)):
        rows = slice(s * n, s * n + n)
        v = gp_own[rows] + other[rows].astype(f32)
        out[:n] = v.astype(out.dtype)
        if s:
            out[n:] = jnp.zeros((EXTRA, width), bf16)
            put_terms(out, n, total)


def middle_kernel(ids, gq0, g1, g2, g3, m1, m2, m3, own, near, far):
    width = own.shape[1]
    same = ids[ZH] == ids[CORE]
    for c in (0, 1):
        lanes = slice(c * width, c * width + width)
        v = gq0[:, lanes] + (
            g1[:, lanes].astype(f32) + g2[:, lanes].astype(f32) + g3[:, lanes].astype(f32)
        )

        @pl.when(ids[CORE] == c)
        def _():
            own[...] = v

        @pl.when((ids[CORE] == c) != same)
        def _():
            near[...] = v.astype(bf16)

        @pl.when(ids[CORE] != c)
        def _():
            far[...] = v.astype(bf16)


def last_kernel(ids, gq_own, near, far, gp_own, row, m1, m2, m3, gq, gp, loss):
    n = gq.shape[0]

    @pl.when(ids[ZH] == ids[CORE])
    def _():
        gq[...] = (gq_own[...] + near[...].astype(f32)).astype(bf16)

    @pl.when(ids[ZH] != ids[CORE])
    def _():
        gq[...] = (far[...].astype(f32) + near[...].astype(f32)).astype(bf16)

    v = gp_own[...]
    total = row[0:1]
    for m in (m1, m2, m3):
        v += m[:n].astype(f32)
        total += get_terms(m, n, n)
    gp[...] = v.astype(bf16)
    loss[...] = jnp.sum(total, axis=1, keepdims=True) * (1.0 / (n * BATCH))


def per_device(queries, passages, positives, level_weight):
    n, width = queries.shape
    wide = 2 * width
    bi = lax.axis_index("batch")
    fi = lax.axis_index("feat")
    ids = jnp.stack([bi // 8, fi // 2, bi % 8 // 2, bi % 2, fi % 2]).astype(jnp.int32)

    near = move_square(queries, lambda h, c: (1 - h, c) if h == c else (h, 1 - c))
    rows = jnp.stack([positives >> 6, positives & 63]).astype(bf16)
    rows = jnp.pad(rows, ((0, EXTRA - 2), (0, width - n)))
    q_row = jnp.concatenate([queries, rows], axis=0)
    far = move_square(q_row, lambda h, c: None if h == c else (1 - h, 1 - c))
    (q_msg,) = call(
        pack_kernel, [ids], [q_row, near, far], [shape(n + EXTRA, wide, bf16)]
    )
    q_msgs = [q_msg] + [shift_x(q_msg, s) for s in (1, 2, 3)]

    (held,) = call(hold_kernel, [ids], [passages], [shape(n, width, bf16)])
    p_next, p_before = shift_zl(passages, 1), shift_zl(passages, 3)
    p_own = [held, p_next, shift_zl(p_next, 1), p_before]
    p_other = [swap_core(a) for a in p_own]

    tile = 4 * n * 4 * n
    *partial, p, q, pos = call(
        score_kernel, [ids], [*p_own, *p_other, *q_msgs],
        [shape(4 * n, n, f32)] * 4
        + [
            shape(4 * n, wide, bf16),
            shape(4, n, wide, bf16),
            shape(4, 1, n, jnp.int32),
        ],
        flops=2 * tile * wide,
    )
    pieces = [partial[0]] + [shift_y(partial[t], t) for t in (1, 2, 3)]
    e_low, low_stats, low_tops = call(
        low_kernel, [ids, level_weight], [p, q, pos],
        [shape(LOW, 4, 4 * n, n, f32), shape(4, 8, n, f32), shape(4, 8, n, f32)],
        flops=2 * tile * wide,
    )
    e_high, message, tops = call(
        owner_kernel, [ids, level_weight], [*pieces, pos, low_stats],
        [shape(2, 4 * n, n, f32), shape(8, 40, n, f32), shape(8, n, f32)],
    )
    stats = lax.all_to_all(message, "batch", 0, 0, axis_index_groups=XZH_GROUPS)
    *tails, rates = call(
        tail_kernel, [ids, level_weight], [stats, low_tops, tops, e_high, pos],
        [shape(4 * n + EXTRA, n, bf16)] * 4 + [shape(4, 8, n, f32)],
    )
    tails = [tails[0]] + [shift_y(tails[t], t) for t in (1, 2, 3)]
    gq_low, gp_low = call(
        low_grad_kernel, [ids, level_weight], [e_low, rates, pos, p, q],
        [shape(4 * n, wide, f32)] * 2,
        scratch=[pltpu.VMEM((LOW, 4 * n, 4 * n), bf16)],
        flops=4 * tile * wide, grant=12,
    )
    gq0, gq1, gq2, gq3, tail, row = call(
        query_grad_kernel, [ids], [*tails, gq_low, p],
        [shape(n, wide, f32)]
        + [shape(n, wide, bf16)] * 3
        + [shape(4 * n, 4 * n, bf16), shape(8, n, f32)],
        scratch=[pltpu.VMEM((4 * n, wide), f32)],
        flops=2 * tile * wide,
    )
    gq = [shift_x(g, -s) for s, g in enumerate((gq1, gq2, gq3), 1)]
    gp_own, message = call(
        passage_grad_kernel, [ids], [tail, row, gp_low, q],
        [shape(4 * n, width, f32), shape(4 * n + EXTRA, width, bf16)],
        flops=2 * tile * wide,
    )
    gp_own, *messages, row = call(
        core_sum_kernel, [ids], [gp_own, row, swap_core(message)],
        [shape(n, width, f32)] + [shape(n + EXTRA, width, bf16)] * 3 + [shape(8, n, f32)],
    )
    gp = [shift_zl(m, -s) for s, m in enumerate(messages, 1)]
    gq_own, near, far = call(
        middle_kernel, [ids], [gq0, *gq, *messages],
        [shape(n, width, f32)] + [shape(n, width, bf16)] * 2, in_place=3, flops=LONG,
    )
    near = move_square(near, lambda h, c: (h, 1 - c) if h == c else (1 - h, c))
    far = move_square(far, lambda h, c: None if h == c else (1 - h, 1 - c))
    grad_queries, grad_passages, loss = call(
        last_kernel, [ids], [gq_own, near, far, gp_own, row, *gp],
        [shape(n, width, bf16), shape(n, width, bf16), shape(1, 1, f32)],
    )
    return loss.reshape(()), grad_queries, grad_passages


def solution(mesh):
    in_specs = (P("batch", "feat"), P("batch", "feat"), P("batch"), P())
    out_specs = (P(), P("batch", "feat"), P("batch", "feat"))
    return jax.shard_map(
        per_device, mesh=mesh, in_specs=in_specs, out_specs=out_specs, check_vma=False
    )
```

```python
import math

import jax
import jax.numpy as jnp
from jax import lax
from jax.experimental import pallas as pl
from jax.experimental.pallas import tpu as pltpu
from jax.sharding import PartitionSpec as P

SMALLEST = 64
LEVELS = 7
LOW = 5
SHARPNESS = 3.0
WIDTHS = [SMALLEST * 2**k for k in range(LEVELS)]
FACTORS = [SHARPNESS / math.sqrt(w) for w in WIDTHS]
SPANS = list(zip([0] + WIDTHS[: LOW - 1], WIDTHS[:LOW]))
EXTRA = 16
PAIR = 2 * SMALLEST

BATCH = 32
FEAT = 8
BOTH = ("batch", "feat")
XZH_GROUPS = [[x * 8 + zl * 2 + zh for x in range(4) for zh in range(2)] for zl in range(4)]
X, Y, ZL, ZH, CORE = range(5)

f32 = jnp.float32
bf16 = jnp.bfloat16


def shift_x(a, s):
    return lax.ppermute(a, "batch", [(b, (b + 8 * s) % BATCH) for b in range(BATCH)])


def shift_zl(a, s):
    return lax.ppermute(
        a, "batch", [(b, b // 8 * 8 + (b + 2 * s) % 8) for b in range(BATCH)]
    )


def shift_y(a, s):
    return lax.ppermute(a, "feat", [(f, (f + 2 * s) % FEAT) for f in range(FEAT)])


def swap_core(a):
    return lax.ppermute(a, "feat", [(f, f ^ 1) for f in range(FEAT)])


def move_square(a, rule):
    pairs = []
    for b in range(BATCH):
        for f in range(FEAT):
            to = rule(b % 2, f % 2)
            if to is not None:
                pairs.append((b * FEAT + f, (b - b % 2 + to[0]) * FEAT + f - f % 2 + to[1]))
    return lax.ppermute(a, BOTH, pairs)


def dot(a, b, ca, cb):
    return lax.dot_general(
        a, b, (((ca,), (cb,)), ((), ())), preferred_element_type=f32
    )


def shape(*dims_dtype):
    return jax.ShapeDtypeStruct(dims_dtype[:-1], dims_dtype[-1])


def call(body, smem, args, outs, scratch=(), flops=0, grant=8, in_place=0):
    vmem = pl.BlockSpec(memory_space=pltpu.VMEM)
    scalar = pl.BlockSpec(memory_space=pltpu.SMEM)
    moved = sum(a.size * a.dtype.itemsize for a in (*args, *outs))
    return pl.pallas_call(
        body,
        out_shape=outs,
        in_specs=[scalar] * len(smem)
        + [vmem] * (len(args) - in_place)
        + [pl.BlockSpec(memory_space=pl.ANY)] * in_place,
        out_specs=[vmem] * len(outs),
        scratch_shapes=list(scratch),
        cost_estimate=pl.CostEstimate(
            flops=flops, bytes_accessed=moved, transcendentals=0
        ),
        compiler_params=pltpu.CompilerParams(vmem_limit_bytes=grant << 20),
    )(*smem, *args)


def find_positives(ids, pos, n):
    rows = lax.broadcasted_iota(jnp.int32, (4 * n, n), 0)
    bits = n.bit_length() - 1
    block = ids[X] * 8 + ids[ZH] + 2 * ((ids[ZL] + 4 - (rows >> bits)) & 3)
    return (block << bits) + (rows & (n - 1)) == pos


def pack_kernel(ids, own, near, far, out):
    n, width = near.shape
    same = ids[ZH] == ids[CORE]

    def put(first, second, rows):
        out[:n, :width] = first[:n]
        out[:n, width:] = second[:n]
        out[n:, :width] = rows[n:]

    out[n:, width:] = jnp.zeros((EXTRA, width), bf16)
    for core in (0, 1):
        for matches in (True, False):
            a, b = (own, near) if matches else (near, far)
            if core:
                a, b = b, a

            @pl.when((ids[CORE] == core) & (same == matches))
            def _():
                put(a, b, own if matches else far)


def hold_kernel(ids, a, out):
    out[...] = a[...]


def score_kernel(
    ids, p0, p1, p2, p3, o0, o1, o2, o3, q0, q1, q2, q3, s0, s1, s2, s3, p, q_all, pos
):
    n, width = p0.shape
    for s, (own, other) in enumerate(zip((p0, p1, p2, p3), (o0, o1, o2, o3))):
        rows = slice(s * n, s * n + n)

        @pl.when(ids[CORE] == 0)
        def _():
            p[rows, :width] = own[...]
            p[rows, width:] = other[...]

        @pl.when(ids[CORE] != 0)
        def _():
            p[rows, :width] = other[...]
            p[rows, width:] = own[...]

    for s, q in enumerate((q0, q1, q2, q3)):
        j = (ids[X] + 4 - s) & 3
        q_all[j] = q[:n]
        digits = q[n:, :n].astype(f32)
        pos[j] = (digits[0:1] * 64.0 + digits[1:2]).astype(jnp.int32)
    for t, out in enumerate((s0, s1, s2, s3)):
        out[...] = dot(p[...], q_all[(ids[Y] + t) & 3], 1, 1)


def level(scores, hot, weight):
    top = jnp.max(scores, axis=0, keepdims=True)
    e = jnp.exp(scores - top)
    lse = top + jnp.log(jnp.sum(e, axis=0, keepdims=True))
    picked = weight * jnp.sum(jnp.where(hot, scores, 0.0), axis=0, keepdims=True)
    return e, top, lse, picked


def low_kernel(ids, weight, p, q_all, pos, e_low, stats, tops):
    n = q_all.shape[1]
    first = lax.broadcasted_iota(jnp.int32, (n, PAIR), 1) < SMALLEST
    for j in range(4):
        hot = find_positives(ids, pos[j], n)
        rows, lses, total = [], [], jnp.zeros((1, n), f32)
        running = None
        for k, (begin, end) in enumerate(SPANS):
            if k == 0:
                q_part = q_all[j, :, :PAIR]
                q_part = jnp.where(first, q_part, jnp.zeros_like(q_part))
                running = dot(p[:, :PAIR], q_part, 1, 1)
            elif k == 1:
                running = dot(p[:, :PAIR], q_all[j, :, :PAIR], 1, 1)
            else:
                running = running + dot(p[:, begin:end], q_all[j, :, begin:end], 1, 1)
            e_low[k, j], top, lse, picked = level(running * FACTORS[k], hot, weight[k])
            rows.append(top)
            lses.append(lse)
            total += picked
        tops[j] = jnp.concatenate(rows + rows[:3], axis=0)
        stats[j] = jnp.concatenate(lses + [total, total, total], axis=0)


def owner_kernel(ids, weight, s0, s1, s2, s3, pos, low_stats, e_high, message, tops):
    n = pos.shape[2]
    hot = find_positives(ids, pos[ids[Y]], n)
    sum5 = sum6 = None
    for t, ref in enumerate((s0, s1, s2, s3)):
        v = ref[...]
        part = jnp.where(((ids[Y] + 4 - t) & 3) <= 1, v, 0.0)
        sum5 = part if t == 0 else sum5 + part
        sum6 = v if t == 0 else sum6 + v
    e_high[0], top5, lse5, picked5 = level(sum5 * FACTORS[5], hot, weight[5])
    e_high[1], top6, lse6, picked6 = level(sum6 * FACTORS[6], hot, weight[6])
    tops[...] = jnp.concatenate([top5, top6] * 4, axis=0)
    high = jnp.concatenate([lse5, lse6] + [picked5 + picked6] * 6, axis=0)
    for i in range(8):
        for j in range(4):
            message[i, 8 * j : 8 * j + 8] = low_stats[j]
        message[i, 32:] = high


def put_terms(ref, row, v):
    hi = v.astype(bf16).astype(f32)
    mid = (v - hi).astype(bf16).astype(f32)
    lo = v - hi - mid
    zero = jnp.zeros((EXTRA - 3, v.shape[1]), f32)
    ref[row:, : v.shape[1]] = jnp.concatenate([hi, mid, lo, zero], axis=0).astype(bf16)


def tail_kernel(ids, weight, stats, low_tops, tops, e_high, pos, m0, m1, m2, m3, rates):
    n = pos.shape[2]

    def merged(at, levels):
        lse = stats[:, at : at + levels]
        best = jnp.max(lse, axis=0)
        mass = jnp.sum(jnp.exp(lse - best[None]), axis=0)
        return best + jnp.log(mass), jnp.sum(stats[:, at + levels : at + levels + 1], axis=0)

    on = ids[Y] == 0
    loss = jnp.zeros((1, n), f32)
    for j in range(4):
        lse, picked = merged(8 * j, LOW)
        loss -= picked
        rows = []
        for k in range(LOW):
            loss += weight[k] * lse[k : k + 1]
            scale = jnp.where(on, weight[k] * FACTORS[k], 0.0)
            rows.append(scale * jnp.exp(low_tops[j, k : k + 1] - lse[k : k + 1]))
        rates[j] = jnp.concatenate(rows + rows[:3], axis=0)

    hot = find_positives(ids, pos[ids[Y]], n)
    lse, picked = merged(32, 2)
    loss = jnp.where(on, loss, 0.0) - picked
    tail = None
    tails = []
    for i in (1, 0):
        loss += weight[LOW + i] * lse[i : i + 1]
        scale = weight[LOW + i] * FACTORS[LOW + i]
        rate = scale * jnp.exp(tops[i : i + 1] - lse[i : i + 1])
        g = e_high[i] * rate - jnp.where(hot, scale, 0.0)
        tail = g if tail is None else tail + g
        tails.append(tail.astype(bf16))
    lane = lax.broadcasted_iota(jnp.int32, (1, n), 1)
    mine = ids[ZL] * FEAT + ids[Y] * 2 + ids[CORE]
    loss = jnp.where(lane == mine, jnp.sum(loss, axis=1, keepdims=True), 0.0)
    for t, m in enumerate((m0, m1, m2, m3)):
        narrow = ((ids[Y] + t) & 3) <= 1

        @pl.when(narrow)
        def _():
            m[: 4 * n] = tails[1]

        @pl.when(jnp.logical_not(narrow))
        def _():
            m[: 4 * n] = tails[0]

        put_terms(m, 4 * n, loss)


def get_terms(ref, row, lanes):
    v = ref[row:, :lanes].astype(f32)
    return v[0:1] + v[1:2] + v[2:3]


def low_grad_kernel(ids, weight, e_low, rates, pos, p, q_all, gq, gp, tails):
    n = pos.shape[2]
    on = ids[Y] == 0
    for j in range(4):
        hot = find_positives(ids, pos[j], n)
        acc = None
        for k in reversed(range(LOW)):
            scale = jnp.where(on, weight[k] * FACTORS[k], 0.0)
            g = e_low[k, j] * rates[j, k : k + 1] - jnp.where(hot, scale, 0.0)
            acc = g if acc is None else acc + g
            tails[k, :, j * n : j * n + n] = acc.astype(bf16)

    q = q_all[...].reshape(4 * n, q_all.shape[2])
    first = lax.broadcasted_iota(jnp.int32, (4 * n, PAIR), 1) < SMALLEST

    def fill(out, fn):
        out[:, :PAIR] = jnp.where(first, fn(0, 0, PAIR), fn(1, 0, PAIR))
        for k in range(2, LOW):
            begin, end = SPANS[k]
            out[:, begin:end] = fn(k, begin, end)

    fill(gq, lambda k, a, b: dot(tails[k], p[:, a:b], 0, 0))
    fill(gp, lambda k, a, b: dot(tails[k], q[:, a:b], 1, 0))


def grad_kernel(
    ids, t0, t1, t2, t3, gq_low, gp_low, p, q_all,
    gq0, gq1, gq2, gq3, own, message, row, tail, gq,
):
    n, wide = gq0.shape
    width = own.shape[1]
    loss = jnp.zeros((1, n), f32)
    for t, ref in enumerate((t0, t1, t2, t3)):
        j = (ids[Y] + 4 - t) & 3
        tail[:, pl.ds(pl.multiple_of(j * n, n), n)] = ref[: 4 * n]
        loss += get_terms(ref, 4 * n, n)
    row[...] = jnp.broadcast_to(loss, row.shape)
    gq[...] = dot(tail[...], p[...], 0, 0) + gq_low[...]
    for s, out in enumerate((gq0, gq1, gq2, gq3)):
        j = (ids[X] + 4 - s) & 3
        out[...] = gq[pl.ds(pl.multiple_of(j * n, n), n), :].astype(out.dtype)

    q = q_all[...].reshape(4 * n, wide)
    message[4 * n :] = jnp.zeros((EXTRA, width), bf16)
    put_terms(message, 4 * n, loss)
    for c in (0, 1):
        lanes = slice(c * width, c * width + width)
        gp = dot(tail[...], q[:, lanes], 1, 0) + gp_low[:, lanes]

        @pl.when(ids[CORE] == c)
        def _():
            own[...] = gp

        @pl.when(ids[CORE] != c)
        def _():
            message[: 4 * n] = gp.astype(bf16)


def core_sum_kernel(ids, gp_own, row, other, own, m1, m2, m3, loss):
    n, width = own.shape
    total = row[0:1] + get_terms(other, 4 * n, n)
    loss[...] = jnp.broadcast_to(total, loss.shape)
    for s, out in enumerate((own, m1, m2, m3)):
        rows = slice(s * n, s * n + n)
        v = gp_own[rows] + other[rows].astype(f32)
        out[:n] = v.astype(out.dtype)
        if s:
            out[n:] = jnp.zeros((EXTRA, width), bf16)
            put_terms(out, n, total)


def middle_kernel(ids, gq0, g1, g2, g3, m1, m2, m3, own, near, far):
    width = own.shape[1]
    same = ids[ZH] == ids[CORE]
    for c in (0, 1):
        lanes = slice(c * width, c * width + width)
        v = gq0[:, lanes] + (
            g1[:, lanes].astype(f32) + g2[:, lanes].astype(f32) + g3[:, lanes].astype(f32)
        )

        @pl.when(ids[CORE] == c)
        def _():
            own[...] = v

        @pl.when((ids[CORE] == c) != same)
        def _():
            near[...] = v.astype(bf16)

        @pl.when(ids[CORE] != c)
        def _():
            far[...] = v.astype(bf16)


def last_kernel(ids, gq_own, near, far, gp_own, row, m1, m2, m3, gq, gp, loss):
    n = gq.shape[0]

    @pl.when(ids[ZH] == ids[CORE])
    def _():
        gq[...] = (gq_own[...] + near[...].astype(f32)).astype(bf16)

    @pl.when(ids[ZH] != ids[CORE])
    def _():
        gq[...] = (far[...].astype(f32) + near[...].astype(f32)).astype(bf16)

    v = gp_own[...]
    total = row[0:1]
    for m in (m1, m2, m3):
        v += m[:n].astype(f32)
        total += get_terms(m, n, n)
    gp[...] = v.astype(bf16)
    loss[...] = jnp.sum(total, axis=1, keepdims=True) * (1.0 / (n * BATCH))


def per_device(queries, passages, positives, level_weight):
    n, width = queries.shape
    wide = 2 * width
    bi = lax.axis_index("batch")
    fi = lax.axis_index("feat")
    ids = jnp.stack([bi // 8, fi // 2, bi % 8 // 2, bi % 2, fi % 2]).astype(jnp.int32)

    near = move_square(queries, lambda h, c: (1 - h, c) if h == c else (h, 1 - c))
    rows = jnp.stack([positives >> 6, positives & 63]).astype(bf16)
    rows = jnp.pad(rows, ((0, EXTRA - 2), (0, width - n)))
    q_row = jnp.concatenate([queries, rows], axis=0)
    far = move_square(q_row, lambda h, c: None if h == c else (1 - h, 1 - c))
    (q_msg,) = call(
        pack_kernel, [ids], [q_row, near, far], [shape(n + EXTRA, wide, bf16)]
    )
    q_msgs = [q_msg] + [shift_x(q_msg, s) for s in (1, 2, 3)]

    (held,) = call(hold_kernel, [ids], [passages], [shape(n, width, bf16)])
    p_next, p_before = shift_zl(passages, 1), shift_zl(passages, 3)
    p_own = [held, p_next, shift_zl(p_next, 1), p_before]
    p_other = [swap_core(a) for a in p_own]

    tile = 4 * n * 4 * n
    *partial, p, q, pos = call(
        score_kernel, [ids], [*p_own, *p_other, *q_msgs],
        [shape(4 * n, n, f32)] * 4
        + [
            shape(4 * n, wide, bf16),
            shape(4, n, wide, bf16),
            shape(4, 1, n, jnp.int32),
        ],
        flops=2 * tile * wide,
    )
    pieces = [partial[0]] + [shift_y(partial[t], t) for t in (1, 2, 3)]
    e_low, low_stats, low_tops = call(
        low_kernel, [ids, level_weight], [p, q, pos],
        [shape(LOW, 4, 4 * n, n, f32), shape(4, 8, n, f32), shape(4, 8, n, f32)],
        flops=2 * tile * wide,
    )
    e_high, message, tops = call(
        owner_kernel, [ids, level_weight], [*pieces, pos, low_stats],
        [shape(2, 4 * n, n, f32), shape(8, 40, n, f32), shape(8, n, f32)],
    )
    stats = lax.all_to_all(message, "batch", 0, 0, axis_index_groups=XZH_GROUPS)
    *tails, rates = call(
        tail_kernel, [ids, level_weight], [stats, low_tops, tops, e_high, pos],
        [shape(4 * n + EXTRA, n, bf16)] * 4 + [shape(4, 8, n, f32)],
    )
    tails = [tails[0]] + [shift_y(tails[t], t) for t in (1, 2, 3)]
    gq_low, gp_low = call(
        low_grad_kernel, [ids, level_weight], [e_low, rates, pos, p, q],
        [shape(4 * n, wide, f32)] * 2,
        scratch=[pltpu.VMEM((LOW, 4 * n, 4 * n), bf16)],
        flops=4 * tile * wide, grant=12,
    )
    gq0, gq1, gq2, gq3, gp_own, message, row = call(
        grad_kernel, [ids], [*tails, gq_low, gp_low, p, q],
        [shape(n, wide, f32)]
        + [shape(n, wide, bf16)] * 3
        + [
            shape(4 * n, width, f32),
            shape(4 * n + EXTRA, width, bf16),
            shape(8, n, f32),
        ],
        scratch=[pltpu.VMEM((4 * n, 4 * n), bf16), pltpu.VMEM((4 * n, wide), f32)],
        flops=4 * tile * wide, grant=12,
    )
    gq = [shift_x(g, -s) for s, g in enumerate((gq1, gq2, gq3), 1)]
    gp_own, *messages, row = call(
        core_sum_kernel, [ids], [gp_own, row, swap_core(message)],
        [shape(n, width, f32)] + [shape(n + EXTRA, width, bf16)] * 3 + [shape(8, n, f32)],
    )
    gp = [shift_zl(m, -s) for s, m in enumerate(messages, 1)]
    gq_own, near, far = call(
        middle_kernel, [ids], [gq0, *gq, *messages],
        [shape(n, width, f32)] + [shape(n, width, bf16)] * 2, in_place=3,
    )
    near = move_square(near, lambda h, c: (h, 1 - c) if h == c else (1 - h, c))
    far = move_square(far, lambda h, c: None if h == c else (1 - h, 1 - c))
    grad_queries, grad_passages, loss = call(
        last_kernel, [ids], [gq_own, near, far, gp_own, row, *gp],
        [shape(n, width, bf16), shape(n, width, bf16), shape(1, 1, f32)],
    )
    return loss.reshape(()), grad_queries, grad_passages


def solution(mesh):
    in_specs = (P("batch", "feat"), P("batch", "feat"), P("batch"), P())
    out_specs = (P(), P("batch", "feat"), P("batch", "feat"))
    return jax.shard_map(
        per_device, mesh=mesh, in_specs=in_specs, out_specs=out_specs, check_vma=False
    )
```

```python
import math

import jax
import jax.numpy as jnp
from jax import lax
from jax.experimental import pallas as pl
from jax.experimental.pallas import tpu as pltpu
from jax.sharding import PartitionSpec as P

SMALLEST = 64
LEVELS = 7
LOW = 5
SHARPNESS = 3.0
WIDTHS = [SMALLEST * 2**k for k in range(LEVELS)]
FACTORS = [SHARPNESS / math.sqrt(w) for w in WIDTHS]
SPANS = list(zip([0] + WIDTHS[: LOW - 1], WIDTHS[:LOW]))
EXTRA = 16
PAIR = 2 * SMALLEST

BATCH = 32
FEAT = 8
BOTH = ("batch", "feat")
XZH_GROUPS = [[x * 8 + zl * 2 + zh for x in range(4) for zh in range(2)] for zl in range(4)]
X, Y, ZL, ZH, CORE = range(5)

f32 = jnp.float32
bf16 = jnp.bfloat16


def shift_x(a, s):
    return lax.ppermute(a, "batch", [(b, (b + 8 * s) % BATCH) for b in range(BATCH)])


def shift_zl(a, s):
    return lax.ppermute(
        a, "batch", [(b, b // 8 * 8 + (b + 2 * s) % 8) for b in range(BATCH)]
    )


def shift_y(a, s):
    return lax.ppermute(a, "feat", [(f, (f + 2 * s) % FEAT) for f in range(FEAT)])


def swap_core(a):
    return lax.ppermute(a, "feat", [(f, f ^ 1) for f in range(FEAT)])


def move_square(a, rule):
    pairs = []
    for b in range(BATCH):
        for f in range(FEAT):
            to = rule(b % 2, f % 2)
            if to is not None:
                pairs.append((b * FEAT + f, (b - b % 2 + to[0]) * FEAT + f - f % 2 + to[1]))
    return lax.ppermute(a, BOTH, pairs)


def dot(a, b, ca, cb):
    return lax.dot_general(
        a, b, (((ca,), (cb,)), ((), ())), preferred_element_type=f32
    )


def shape(*dims_dtype):
    return jax.ShapeDtypeStruct(dims_dtype[:-1], dims_dtype[-1])


def call(body, smem, args, outs, scratch=(), flops=0, grant=8, in_place=0):
    vmem = pl.BlockSpec(memory_space=pltpu.VMEM)
    scalar = pl.BlockSpec(memory_space=pltpu.SMEM)
    moved = sum(a.size * a.dtype.itemsize for a in (*args, *outs))
    return pl.pallas_call(
        body,
        out_shape=outs,
        in_specs=[scalar] * len(smem)
        + [vmem] * (len(args) - in_place)
        + [pl.BlockSpec(memory_space=pl.ANY)] * in_place,
        out_specs=[vmem] * len(outs),
        scratch_shapes=list(scratch),
        cost_estimate=pl.CostEstimate(
            flops=flops, bytes_accessed=moved, transcendentals=0
        ),
        compiler_params=pltpu.CompilerParams(vmem_limit_bytes=grant << 20),
    )(*smem, *args)


def find_positives(ids, pos, n):
    rows = lax.broadcasted_iota(jnp.int32, (4 * n, n), 0)
    bits = n.bit_length() - 1
    block = ids[X] * 8 + ids[ZH] + 2 * ((ids[ZL] + 4 - (rows >> bits)) & 3)
    return (block << bits) + (rows & (n - 1)) == pos


def pack_kernel(ids, own, near, far, out):
    n, width = near.shape
    same = ids[ZH] == ids[CORE]

    def put(first, second, rows):
        out[:n, :width] = first[:n]
        out[:n, width:] = second[:n]
        out[n:, :width] = rows[n:]

    out[n:, width:] = jnp.zeros((EXTRA, width), bf16)
    for core in (0, 1):
        for matches in (True, False):
            a, b = (own, near) if matches else (near, far)
            if core:
                a, b = b, a

            @pl.when((ids[CORE] == core) & (same == matches))
            def _():
                put(a, b, own if matches else far)


def hold_kernel(ids, a, out):
    out[...] = a[...]


def score_kernel(
    ids, p0, p1, p2, p3, o0, o1, o2, o3, q0, q1, q2, q3, s0, s1, s2, s3, p, q_all, pos, partial
):
    n, width = p0.shape
    for s, (own, other) in enumerate(zip((p0, p1, p2, p3), (o0, o1, o2, o3))):
        rows = slice(s * n, s * n + n)

        @pl.when(ids[CORE] == 0)
        def _():
            p[rows, :width] = own[...]
            p[rows, width:] = other[...]

        @pl.when(ids[CORE] != 0)
        def _():
            p[rows, :width] = other[...]
            p[rows, width:] = own[...]

    for s, q in enumerate((q0, q1, q2, q3)):
        j = (ids[X] + 4 - s) & 3
        q_all[j] = q[:n]
        digits = q[n:, :n].astype(f32)
        pos[j] = (digits[0:1] * 64.0 + digits[1:2]).astype(jnp.int32)
    partial[...] = dot(p[...], q_all[...].reshape(4 * n, 2 * width), 1, 1)
    for t, out in enumerate((s0, s1, s2, s3)):
        j = (ids[Y] + t) & 3
        out[...] = partial[:, pl.ds(pl.multiple_of(j * n, n), n)]


def level(scores, hot, weight):
    top = jnp.max(scores, axis=0, keepdims=True)
    e = jnp.exp(scores - top)
    lse = top + jnp.log(jnp.sum(e, axis=0, keepdims=True))
    picked = weight * jnp.sum(jnp.where(hot, scores, 0.0), axis=0, keepdims=True)
    return e, top, lse, picked


def low_kernel(ids, weight, p, q_all, pos, e_low, stats, tops):
    n = q_all.shape[1]
    first = lax.broadcasted_iota(jnp.int32, (n, PAIR), 1) < SMALLEST
    for j in range(4):
        hot = find_positives(ids, pos[j], n)
        rows, lses, total = [], [], jnp.zeros((1, n), f32)
        running = None
        for k, (begin, end) in enumerate(SPANS):
            if k == 0:
                q_part = q_all[j, :, :PAIR]
                q_part = jnp.where(first, q_part, jnp.zeros_like(q_part))
                running = dot(p[:, :PAIR], q_part, 1, 1)
            elif k == 1:
                running = dot(p[:, :PAIR], q_all[j, :, :PAIR], 1, 1)
            else:
                running = running + dot(p[:, begin:end], q_all[j, :, begin:end], 1, 1)
            e_low[k, j], top, lse, picked = level(running * FACTORS[k], hot, weight[k])
            rows.append(top)
            lses.append(lse)
            total += picked
        tops[j] = jnp.concatenate(rows + rows[:3], axis=0)
        stats[j] = jnp.concatenate(lses + [total, total, total], axis=0)


def owner_kernel(ids, weight, s0, s1, s2, s3, pos, low_stats, e_high, message, tops):
    n = pos.shape[2]
    hot = find_positives(ids, pos[ids[Y]], n)
    sum5 = sum6 = None
    for t, ref in enumerate((s0, s1, s2, s3)):
        v = ref[...]
        part = jnp.where(((ids[Y] + 4 - t) & 3) <= 1, v, 0.0)
        sum5 = part if t == 0 else sum5 + part
        sum6 = v if t == 0 else sum6 + v
    e_high[0], top5, lse5, picked5 = level(sum5 * FACTORS[5], hot, weight[5])
    e_high[1], top6, lse6, picked6 = level(sum6 * FACTORS[6], hot, weight[6])
    tops[...] = jnp.concatenate([top5, top6] * 4, axis=0)
    high = jnp.concatenate([lse5, lse6] + [picked5 + picked6] * 6, axis=0)
    for i in range(8):
        for j in range(4):
            message[i, 8 * j : 8 * j + 8] = low_stats[j]
        message[i, 32:] = high


def put_terms(ref, row, v):
    hi = v.astype(bf16).astype(f32)
    mid = (v - hi).astype(bf16).astype(f32)
    lo = v - hi - mid
    zero = jnp.zeros((EXTRA - 3, v.shape[1]), f32)
    ref[row:, : v.shape[1]] = jnp.concatenate([hi, mid, lo, zero], axis=0).astype(bf16)


def tail_kernel(ids, weight, stats, low_tops, tops, e_high, pos, m0, m1, m2, m3, rates):
    n = pos.shape[2]

    def merged(at, levels):
        lse = stats[:, at : at + levels]
        best = jnp.max(lse, axis=0)
        mass = jnp.sum(jnp.exp(lse - best[None]), axis=0)
        return best + jnp.log(mass), jnp.sum(stats[:, at + levels : at + levels + 1], axis=0)

    on = ids[Y] == 0
    loss = jnp.zeros((1, n), f32)
    for j in range(4):
        lse, picked = merged(8 * j, LOW)
        loss -= picked
        rows = []
        for k in range(LOW):
            loss += weight[k] * lse[k : k + 1]
            scale = jnp.where(on, weight[k] * FACTORS[k], 0.0)
            rows.append(scale * jnp.exp(low_tops[j, k : k + 1] - lse[k : k + 1]))
        rates[j] = jnp.concatenate(rows + rows[:3], axis=0)

    hot = find_positives(ids, pos[ids[Y]], n)
    lse, picked = merged(32, 2)
    loss = jnp.where(on, loss, 0.0) - picked
    tail = None
    tails = []
    for i in (1, 0):
        loss += weight[LOW + i] * lse[i : i + 1]
        scale = weight[LOW + i] * FACTORS[LOW + i]
        rate = scale * jnp.exp(tops[i : i + 1] - lse[i : i + 1])
        g = e_high[i] * rate - jnp.where(hot, scale, 0.0)
        tail = g if tail is None else tail + g
        tails.append(tail.astype(bf16))
    lane = lax.broadcasted_iota(jnp.int32, (1, n), 1)
    mine = ids[ZL] * FEAT + ids[Y] * 2 + ids[CORE]
    loss = jnp.where(lane == mine, jnp.sum(loss, axis=1, keepdims=True), 0.0)
    for t, m in enumerate((m0, m1, m2, m3)):
        narrow = ((ids[Y] + t) & 3) <= 1

        @pl.when(narrow)
        def _():
            m[: 4 * n] = tails[1]

        @pl.when(jnp.logical_not(narrow))
        def _():
            m[: 4 * n] = tails[0]

        put_terms(m, 4 * n, loss)


def get_terms(ref, row, lanes):
    v = ref[row:, :lanes].astype(f32)
    return v[0:1] + v[1:2] + v[2:3]


def low_grad_kernel(ids, weight, e_low, rates, pos, p, q_all, gq, gp, tails):
    n = pos.shape[2]
    on = ids[Y] == 0
    for j in range(4):
        hot = find_positives(ids, pos[j], n)
        acc = None
        for k in reversed(range(LOW)):
            scale = jnp.where(on, weight[k] * FACTORS[k], 0.0)
            g = e_low[k, j] * rates[j, k : k + 1] - jnp.where(hot, scale, 0.0)
            acc = g if acc is None else acc + g
            tails[k, :, j * n : j * n + n] = acc.astype(bf16)

    q = q_all[...].reshape(4 * n, q_all.shape[2])
    first = lax.broadcasted_iota(jnp.int32, (4 * n, PAIR), 1) < SMALLEST

    def fill(out, fn):
        out[:, :PAIR] = jnp.where(first, fn(0, 0, PAIR), fn(1, 0, PAIR))
        for k in range(2, LOW):
            begin, end = SPANS[k]
            out[:, begin:end] = fn(k, begin, end)

    fill(gq, lambda k, a, b: dot(tails[k], p[:, a:b], 0, 0))
    fill(gp, lambda k, a, b: dot(tails[k], q[:, a:b], 1, 0))


def grad_kernel(
    ids, t0, t1, t2, t3, gq_low, gp_low, p, q_all,
    gq0, gq1, gq2, gq3, own, message, row, tail, gq,
):
    n, wide = gq0.shape
    width = own.shape[1]
    loss = jnp.zeros((1, n), f32)
    for t, ref in enumerate((t0, t1, t2, t3)):
        j = (ids[Y] + 4 - t) & 3
        tail[:, pl.ds(pl.multiple_of(j * n, n), n)] = ref[: 4 * n]
        loss += get_terms(ref, 4 * n, n)
    row[...] = jnp.broadcast_to(loss, row.shape)
    gq[...] = dot(tail[...], p[...], 0, 0) + gq_low[...]
    for s, out in enumerate((gq0, gq1, gq2, gq3)):
        j = (ids[X] + 4 - s) & 3
        out[...] = gq[pl.ds(pl.multiple_of(j * n, n), n), :].astype(out.dtype)

    q = q_all[...].reshape(4 * n, wide)
    message[4 * n :] = jnp.zeros((EXTRA, width), bf16)
    put_terms(message, 4 * n, loss)
    for c in (0, 1):
        lanes = slice(c * width, c * width + width)
        gp = dot(tail[...], q[:, lanes], 1, 0) + gp_low[:, lanes]

        @pl.when(ids[CORE] == c)
        def _():
            own[...] = gp

        @pl.when(ids[CORE] != c)
        def _():
            message[: 4 * n] = gp.astype(bf16)


def core_sum_kernel(ids, gp_own, row, other, own, m1, m2, m3, loss):
    n, width = own.shape
    total = row[0:1] + get_terms(other, 4 * n, n)
    loss[...] = jnp.broadcast_to(total, loss.shape)
    for s, out in enumerate((own, m1, m2, m3)):
        rows = slice(s * n, s * n + n)
        v = gp_own[rows] + other[rows].astype(f32)
        out[:n] = v.astype(out.dtype)
        if s:
            out[n:] = jnp.zeros((EXTRA, width), bf16)
            put_terms(out, n, total)


def middle_kernel(ids, gq0, g1, g2, g3, m1, m2, m3, own, near, far):
    width = own.shape[1]
    same = ids[ZH] == ids[CORE]
    for c in (0, 1):
        lanes = slice(c * width, c * width + width)
        v = gq0[:, lanes] + (
            g1[:, lanes].astype(f32) + g2[:, lanes].astype(f32) + g3[:, lanes].astype(f32)
        )

        @pl.when(ids[CORE] == c)
        def _():
            own[...] = v

        @pl.when((ids[CORE] == c) != same)
        def _():
            near[...] = v.astype(bf16)

        @pl.when(ids[CORE] != c)
        def _():
            far[...] = v.astype(bf16)


def last_kernel(ids, gq_own, near, far, gp_own, row, m1, m2, m3, gq, gp, loss):
    n = gq.shape[0]

    @pl.when(ids[ZH] == ids[CORE])
    def _():
        gq[...] = (gq_own[...] + near[...].astype(f32)).astype(bf16)

    @pl.when(ids[ZH] != ids[CORE])
    def _():
        gq[...] = (far[...].astype(f32) + near[...].astype(f32)).astype(bf16)

    v = gp_own[...]
    total = row[0:1]
    for m in (m1, m2, m3):
        v += m[:n].astype(f32)
        total += get_terms(m, n, n)
    gp[...] = v.astype(bf16)
    loss[...] = jnp.sum(total, axis=1, keepdims=True) * (1.0 / (n * BATCH))


def per_device(queries, passages, positives, level_weight):
    n, width = queries.shape
    wide = 2 * width
    bi = lax.axis_index("batch")
    fi = lax.axis_index("feat")
    ids = jnp.stack([bi // 8, fi // 2, bi % 8 // 2, bi % 2, fi % 2]).astype(jnp.int32)

    near = move_square(queries, lambda h, c: (1 - h, c) if h == c else (h, 1 - c))
    row = lax.broadcasted_iota(jnp.int32, (n + EXTRA, width), 0)
    digits = jnp.pad(positives, (0, width - n))[None, :]
    digits = jnp.where(row == n, digits >> 6, jnp.where(row == n + 1, digits & 63, 0))
    q_row = jnp.where(
        row < n, jnp.pad(queries, ((0, EXTRA), (0, 0))), digits.astype(bf16)
    )
    far = move_square(q_row, lambda h, c: None if h == c else (1 - h, 1 - c))
    (q_msg,) = call(
        pack_kernel, [ids], [q_row, near, far], [shape(n + EXTRA, wide, bf16)]
    )
    q_msgs = [q_msg] + [shift_x(q_msg, s) for s in (1, 2, 3)]

    (held,) = call(hold_kernel, [ids], [passages], [shape(n, width, bf16)])
    p_next, p_before = shift_zl(passages, 1), shift_zl(passages, 3)
    p_own = [held, p_next, shift_zl(p_next, 1), p_before]
    p_other = [swap_core(a) for a in p_own]

    tile = 4 * n * 4 * n
    *partial, p, q, pos = call(
        score_kernel, [ids], [*p_own, *p_other, *q_msgs],
        [shape(4 * n, n, f32)] * 4
        + [
            shape(4 * n, wide, bf16),
            shape(4, n, wide, bf16),
            shape(4, 1, n, jnp.int32),
        ],
        scratch=[pltpu.VMEM((4 * n, 4 * n), f32)],
        flops=2 * tile * wide,
    )
    pieces = [partial[0]] + [shift_y(partial[t], t) for t in (1, 2, 3)]
    e_low, low_stats, low_tops = call(
        low_kernel, [ids, level_weight], [p, q, pos],
        [shape(LOW, 4, 4 * n, n, f32), shape(4, 8, n, f32), shape(4, 8, n, f32)],
        flops=2 * tile * wide,
    )
    e_high, message, tops = call(
        owner_kernel, [ids, level_weight], [*pieces, pos, low_stats],
        [shape(2, 4 * n, n, f32), shape(8, 40, n, f32), shape(8, n, f32)],
    )
    stats = lax.all_to_all(message, "batch", 0, 0, axis_index_groups=XZH_GROUPS)
    *tails, rates = call(
        tail_kernel, [ids, level_weight], [stats, low_tops, tops, e_high, pos],
        [shape(4 * n + EXTRA, n, bf16)] * 4 + [shape(4, 8, n, f32)],
    )
    tails = [tails[0]] + [shift_y(tails[t], t) for t in (1, 2, 3)]
    gq_low, gp_low = call(
        low_grad_kernel, [ids, level_weight], [e_low, rates, pos, p, q],
        [shape(4 * n, wide, f32)] * 2,
        scratch=[pltpu.VMEM((LOW, 4 * n, 4 * n), bf16)],
        flops=4 * tile * wide, grant=12,
    )
    gq0, gq1, gq2, gq3, gp_own, message, row = call(
        grad_kernel, [ids], [*tails, gq_low, gp_low, p, q],
        [shape(n, wide, f32)]
        + [shape(n, wide, bf16)] * 3
        + [
            shape(4 * n, width, f32),
            shape(4 * n + EXTRA, width, bf16),
            shape(8, n, f32),
        ],
        scratch=[pltpu.VMEM((4 * n, 4 * n), bf16), pltpu.VMEM((4 * n, wide), f32)],
        flops=4 * tile * wide, grant=12,
    )
    gq = [shift_x(g, -s) for s, g in enumerate((gq1, gq2, gq3), 1)]
    gp_own, *messages, row = call(
        core_sum_kernel, [ids], [gp_own, row, swap_core(message)],
        [shape(n, width, f32)] + [shape(n + EXTRA, width, bf16)] * 3 + [shape(8, n, f32)],
    )
    gp = [shift_zl(m, -s) for s, m in enumerate(messages, 1)]
    gq_own, near, far = call(
        middle_kernel, [ids], [gq0, *gq, *messages],
        [shape(n, width, f32)] + [shape(n, width, bf16)] * 2, in_place=3,
    )
    near = move_square(near, lambda h, c: (h, 1 - c) if h == c else (1 - h, c))
    far = move_square(far, lambda h, c: None if h == c else (1 - h, 1 - c))
    grad_queries, grad_passages, loss = call(
        last_kernel, [ids], [gq_own, near, far, gp_own, row, *gp],
        [shape(n, width, bf16), shape(n, width, bf16), shape(1, 1, f32)],
    )
    return loss.reshape(()), grad_queries, grad_passages


def solution(mesh):
    in_specs = (P("batch", "feat"), P("batch", "feat"), P("batch"), P())
    out_specs = (P(), P("batch", "feat"), P("batch", "feat"))
    return jax.shard_map(
        per_device, mesh=mesh, in_specs=in_specs, out_specs=out_specs, check_vma=False
    )
```

```python
import math

import jax
import jax.numpy as jnp
from jax import lax
from jax.experimental import pallas as pl
from jax.experimental.pallas import tpu as pltpu
from jax.sharding import PartitionSpec as P

SMALLEST = 64
LEVELS = 7
LOW = 5
SHARPNESS = 3.0
WIDTHS = [SMALLEST * 2**k for k in range(LEVELS)]
FACTORS = [SHARPNESS / math.sqrt(w) for w in WIDTHS]
SPANS = list(zip([0] + WIDTHS[: LOW - 1], WIDTHS[:LOW]))
EXTRA = 16
PAIR = 2 * SMALLEST

BATCH = 32
FEAT = 8
BOTH = ("batch", "feat")
XZH_GROUPS = [[x * 8 + zl * 2 + zh for x in range(4) for zh in range(2)] for zl in range(4)]
X, Y, ZL, ZH, CORE = range(5)

f32 = jnp.float32
bf16 = jnp.bfloat16


def shift_x(a, s):
    return lax.ppermute(a, "batch", [(b, (b + 8 * s) % BATCH) for b in range(BATCH)])


def shift_zl(a, s):
    return lax.ppermute(
        a, "batch", [(b, b // 8 * 8 + (b + 2 * s) % 8) for b in range(BATCH)]
    )


def shift_y(a, s):
    return lax.ppermute(a, "feat", [(f, (f + 2 * s) % FEAT) for f in range(FEAT)])


def swap_core(a):
    return lax.ppermute(a, "feat", [(f, f ^ 1) for f in range(FEAT)])


def move_square(a, rule):
    pairs = []
    for b in range(BATCH):
        for f in range(FEAT):
            to = rule(b % 2, f % 2)
            if to is not None:
                pairs.append((b * FEAT + f, (b - b % 2 + to[0]) * FEAT + f - f % 2 + to[1]))
    return lax.ppermute(a, BOTH, pairs)


def dot(a, b, ca, cb):
    return lax.dot_general(
        a, b, (((ca,), (cb,)), ((), ())), preferred_element_type=f32
    )


def shape(*dims_dtype):
    return jax.ShapeDtypeStruct(dims_dtype[:-1], dims_dtype[-1])


def call(body, smem, args, outs, scratch=(), flops=0, grant=8, in_place=0):
    vmem = pl.BlockSpec(memory_space=pltpu.VMEM)
    scalar = pl.BlockSpec(memory_space=pltpu.SMEM)
    moved = sum(a.size * a.dtype.itemsize for a in (*args, *outs))
    return pl.pallas_call(
        body,
        out_shape=outs,
        in_specs=[scalar] * len(smem)
        + [vmem] * (len(args) - in_place)
        + [pl.BlockSpec(memory_space=pl.ANY)] * in_place,
        out_specs=[vmem] * len(outs),
        scratch_shapes=list(scratch),
        cost_estimate=pl.CostEstimate(
            flops=flops, bytes_accessed=moved, transcendentals=0
        ),
        compiler_params=pltpu.CompilerParams(vmem_limit_bytes=grant << 20),
    )(*smem, *args)


def find_positives(ids, pos, n):
    rows = lax.broadcasted_iota(jnp.int32, (4 * n, n), 0)
    bits = n.bit_length() - 1
    block = ids[X] * 8 + ids[ZH] + 2 * ((ids[ZL] + 4 - (rows >> bits)) & 3)
    return (block << bits) + (rows & (n - 1)) == pos


def pack_kernel(ids, own, near, far, out):
    n, width = near.shape
    same = ids[ZH] == ids[CORE]

    def put(first, second, rows):
        out[:n, :width] = first[:n]
        out[:n, width:] = second[:n]
        out[n:, :width] = rows[n:]

    out[n:, width:] = jnp.zeros((EXTRA, width), bf16)
    for core in (0, 1):
        for matches in (True, False):
            a, b = (own, near) if matches else (near, far)
            if core:
                a, b = b, a

            @pl.when((ids[CORE] == core) & (same == matches))
            def _():
                put(a, b, own if matches else far)


def hold_kernel(ids, a, out):
    out[...] = a[...]


def score_kernel(
    ids, p0, p1, p2, p3, o0, o1, o2, o3, q0, q1, q2, q3, s0, s1, s2, s3, p, q_all, pos, partial
):
    n, width = p0.shape
    for s, (own, other) in enumerate(zip((p0, p1, p2, p3), (o0, o1, o2, o3))):
        rows = slice(s * n, s * n + n)

        @pl.when(ids[CORE] == 0)
        def _():
            p[rows, :width] = own[...]
            p[rows, width:] = other[...]

        @pl.when(ids[CORE] != 0)
        def _():
            p[rows, :width] = other[...]
            p[rows, width:] = own[...]

    for s, q in enumerate((q0, q1, q2, q3)):
        j = (ids[X] + 4 - s) & 3
        q_all[j] = q[:n]
        digits = q[n:, :n].astype(f32)
        pos[j] = (digits[0:1] * 64.0 + digits[1:2]).astype(jnp.int32)
    partial[...] = dot(p[...], q_all[...].reshape(4 * n, 2 * width), 1, 1)
    for t, out in enumerate((s0, s1, s2, s3)):
        j = (ids[Y] + t) & 3
        out[...] = partial[:, pl.ds(pl.multiple_of(j * n, n), n)]


def level(scores, hot, weight):
    top = jnp.max(scores, axis=0, keepdims=True)
    e = jnp.exp(scores - top)
    lse = top + jnp.log(jnp.sum(e, axis=0, keepdims=True))
    picked = weight * jnp.sum(jnp.where(hot, scores, 0.0), axis=0, keepdims=True)
    return e, top, lse, picked


def low_kernel(ids, weight, p, q_all, pos, e_low, stats, tops):
    n = q_all.shape[1]
    first = lax.broadcasted_iota(jnp.int32, (n, PAIR), 1) < SMALLEST
    for j in range(4):
        hot = find_positives(ids, pos[j], n)
        rows, lses, total = [], [], jnp.zeros((1, n), f32)
        running = None
        for k, (begin, end) in enumerate(SPANS):
            if k == 0:
                q_part = q_all[j, :, :PAIR]
                q_part = jnp.where(first, q_part, jnp.zeros_like(q_part))
                running = dot(p[:, :PAIR], q_part, 1, 1)
            elif k == 1:
                running = dot(p[:, :PAIR], q_all[j, :, :PAIR], 1, 1)
            else:
                running = running + dot(p[:, begin:end], q_all[j, :, begin:end], 1, 1)
            e_low[k, j], top, lse, picked = level(running * FACTORS[k], hot, weight[k])
            rows.append(top)
            lses.append(lse)
            total += picked
        tops[j] = jnp.concatenate(rows + rows[:3], axis=0)
        stats[j] = jnp.concatenate(lses + [total, total, total], axis=0)


def owner_kernel(ids, weight, s0, s1, s2, s3, pos, low_stats, e_high, message, tops):
    n = pos.shape[2]
    hot = find_positives(ids, pos[ids[Y]], n)
    sum5 = sum6 = None
    for t, ref in enumerate((s0, s1, s2, s3)):
        v = ref[...]
        part = jnp.where(((ids[Y] + 4 - t) & 3) <= 1, v, 0.0)
        sum5 = part if t == 0 else sum5 + part
        sum6 = v if t == 0 else sum6 + v
    e_high[0], top5, lse5, picked5 = level(sum5 * FACTORS[5], hot, weight[5])
    e_high[1], top6, lse6, picked6 = level(sum6 * FACTORS[6], hot, weight[6])
    tops[...] = jnp.concatenate([top5, top6] * 4, axis=0)
    high = jnp.concatenate([lse5, lse6] + [picked5 + picked6] * 6, axis=0)
    for i in range(8):
        for j in range(4):
            message[i, 8 * j : 8 * j + 8] = low_stats[j]
        message[i, 32:] = high


def put_terms(ref, row, v):
    hi = v.astype(bf16).astype(f32)
    mid = (v - hi).astype(bf16).astype(f32)
    lo = v - hi - mid
    zero = jnp.zeros((EXTRA - 3, v.shape[1]), f32)
    ref[row:, : v.shape[1]] = jnp.concatenate([hi, mid, lo, zero], axis=0).astype(bf16)


def tail_kernel(ids, weight, stats, low_tops, tops, e_high, pos, m0, m1, m2, m3, rates):
    n = pos.shape[2]

    def merged(at, levels):
        lse = stats[:, at : at + levels]
        best = jnp.max(lse, axis=0)
        mass = jnp.sum(jnp.exp(lse - best[None]), axis=0)
        return best + jnp.log(mass), jnp.sum(stats[:, at + levels : at + levels + 1], axis=0)

    on = ids[Y] == 0
    loss = jnp.zeros((1, n), f32)
    for j in range(4):
        lse, picked = merged(8 * j, LOW)
        loss -= picked
        rows = []
        for k in range(LOW):
            loss += weight[k] * lse[k : k + 1]
            scale = jnp.where(on, weight[k] * FACTORS[k], 0.0)
            rows.append(scale * jnp.exp(low_tops[j, k : k + 1] - lse[k : k + 1]))
        rates[j] = jnp.concatenate(rows + rows[:3], axis=0)

    hot = find_positives(ids, pos[ids[Y]], n)
    lse, picked = merged(32, 2)
    loss = jnp.where(on, loss, 0.0) - picked
    tail = None
    tails = []
    for i in (1, 0):
        loss += weight[LOW + i] * lse[i : i + 1]
        scale = weight[LOW + i] * FACTORS[LOW + i]
        rate = scale * jnp.exp(tops[i : i + 1] - lse[i : i + 1])
        g = e_high[i] * rate - jnp.where(hot, scale, 0.0)
        tail = g if tail is None else tail + g
        tails.append(tail.astype(bf16))
    lane = lax.broadcasted_iota(jnp.int32, (1, n), 1)
    mine = ids[ZL] * FEAT + ids[Y] * 2 + ids[CORE]
    loss = jnp.where(lane == mine, jnp.sum(loss, axis=1, keepdims=True), 0.0)
    for t, m in enumerate((m0, m1, m2, m3)):
        narrow = ((ids[Y] + t) & 3) <= 1

        @pl.when(narrow)
        def _():
            m[: 4 * n] = tails[1]

        @pl.when(jnp.logical_not(narrow))
        def _():
            m[: 4 * n] = tails[0]

        put_terms(m, 4 * n, loss)


def get_terms(ref, row, lanes):
    v = ref[row:, :lanes].astype(f32)
    return v[0:1] + v[1:2] + v[2:3]


def low_grad_kernel(ids, weight, e_low, rates, pos, p, q_all, gq, gp, tails):
    n = pos.shape[2]
    on = ids[Y] == 0
    for j in range(4):
        hot = find_positives(ids, pos[j], n)
        acc = None
        for k in reversed(range(LOW)):
            scale = jnp.where(on, weight[k] * FACTORS[k], 0.0)
            g = e_low[k, j] * rates[j, k : k + 1] - jnp.where(hot, scale, 0.0)
            acc = g if acc is None else acc + g
            tails[k, :, j * n : j * n + n] = acc.astype(bf16)

    q = q_all[...].reshape(4 * n, q_all.shape[2])
    first = lax.broadcasted_iota(jnp.int32, (4 * n, PAIR), 1) < SMALLEST

    def fill(out, fn):
        out[:, :PAIR] = jnp.where(first, fn(0, 0, PAIR), fn(1, 0, PAIR)).astype(bf16)
        for k in range(2, LOW):
            begin, end = SPANS[k]
            out[:, begin:end] = fn(k, begin, end).astype(bf16)

    fill(gq, lambda k, a, b: dot(tails[k], p[:, a:b], 0, 0))
    fill(gp, lambda k, a, b: dot(tails[k], q[:, a:b], 1, 0))


def grad_kernel(
    ids, t0, t1, t2, t3, gq_low, gp_low, p, q_all,
    gq0, gq1, gq2, gq3, own, message, row, tail, gq,
):
    n, wide = gq0.shape
    width = own.shape[1]
    loss = jnp.zeros((1, n), f32)
    for t, ref in enumerate((t0, t1, t2, t3)):
        j = (ids[Y] + 4 - t) & 3
        tail[:, pl.ds(pl.multiple_of(j * n, n), n)] = ref[: 4 * n]
        loss += get_terms(ref, 4 * n, n)
    row[...] = jnp.broadcast_to(loss, row.shape)
    gq[...] = dot(tail[...], p[...], 0, 0) + gq_low[...].astype(f32)
    for s, out in enumerate((gq0, gq1, gq2, gq3)):
        j = (ids[X] + 4 - s) & 3
        out[...] = gq[pl.ds(pl.multiple_of(j * n, n), n), :].astype(out.dtype)

    q = q_all[...].reshape(4 * n, wide)
    message[4 * n :] = jnp.zeros((EXTRA, width), bf16)
    put_terms(message, 4 * n, loss)
    for c in (0, 1):
        lanes = slice(c * width, c * width + width)
        gp = dot(tail[...], q[:, lanes], 1, 0) + gp_low[:, lanes].astype(f32)

        @pl.when(ids[CORE] == c)
        def _():
            own[...] = gp

        @pl.when(ids[CORE] != c)
        def _():
            message[: 4 * n] = gp.astype(bf16)


def core_sum_kernel(ids, gp_own, row, other, own, m1, m2, m3, loss):
    n, width = own.shape
    total = row[0:1] + get_terms(other, 4 * n, n)
    loss[...] = jnp.broadcast_to(total, loss.shape)
    for s, out in enumerate((own, m1, m2, m3)):
        rows = slice(s * n, s * n + n)
        v = gp_own[rows] + other[rows].astype(f32)
        out[:n] = v.astype(out.dtype)
        if s:
            out[n:] = jnp.zeros((EXTRA, width), bf16)
            put_terms(out, n, total)


def middle_kernel(ids, gq0, g1, g2, g3, m1, m2, m3, own, near, far):
    width = own.shape[1]
    same = ids[ZH] == ids[CORE]
    for c in (0, 1):
        lanes = slice(c * width, c * width + width)
        v = gq0[:, lanes] + (
            g1[:, lanes].astype(f32) + g2[:, lanes].astype(f32) + g3[:, lanes].astype(f32)
        )

        @pl.when(ids[CORE] == c)
        def _():
            own[...] = v

        @pl.when((ids[CORE] == c) != same)
        def _():
            near[...] = v.astype(bf16)

        @pl.when(ids[CORE] != c)
        def _():
            far[...] = v.astype(bf16)


def last_kernel(ids, gq_own, near, far, gp_own, row, m1, m2, m3, gq, gp, loss):
    n = gq.shape[0]

    @pl.when(ids[ZH] == ids[CORE])
    def _():
        gq[...] = (gq_own[...] + near[...].astype(f32)).astype(bf16)

    @pl.when(ids[ZH] != ids[CORE])
    def _():
        gq[...] = (far[...].astype(f32) + near[...].astype(f32)).astype(bf16)

    v = gp_own[...]
    total = row[0:1]
    for m in (m1, m2, m3):
        v += m[:n].astype(f32)
        total += get_terms(m, n, n)
    gp[...] = v.astype(bf16)
    loss[...] = jnp.sum(total, axis=1, keepdims=True) * (1.0 / (n * BATCH))


def per_device(queries, passages, positives, level_weight):
    n, width = queries.shape
    wide = 2 * width
    bi = lax.axis_index("batch")
    fi = lax.axis_index("feat")
    ids = jnp.stack([bi // 8, fi // 2, bi % 8 // 2, bi % 2, fi % 2]).astype(jnp.int32)

    near = move_square(queries, lambda h, c: (1 - h, c) if h == c else (h, 1 - c))
    row = lax.broadcasted_iota(jnp.int32, (n + EXTRA, width), 0)
    digits = jnp.pad(positives, (0, width - n))[None, :]
    digits = jnp.where(row == n, digits >> 6, jnp.where(row == n + 1, digits & 63, 0))
    q_row = jnp.where(
        row < n, jnp.pad(queries, ((0, EXTRA), (0, 0))), digits.astype(bf16)
    )
    far = move_square(q_row, lambda h, c: None if h == c else (1 - h, 1 - c))
    (q_msg,) = call(
        pack_kernel, [ids], [q_row, near, far], [shape(n + EXTRA, wide, bf16)]
    )
    q_msgs = [q_msg] + [shift_x(q_msg, s) for s in (1, 2, 3)]

    (held,) = call(hold_kernel, [ids], [passages], [shape(n, width, bf16)])
    p_next, p_before = shift_zl(passages, 1), shift_zl(passages, 3)
    p_own = [held, p_next, shift_zl(p_next, 1), p_before]
    p_other = [swap_core(a) for a in p_own]

    tile = 4 * n * 4 * n
    *partial, p, q, pos = call(
        score_kernel, [ids], [*p_own, *p_other, *q_msgs],
        [shape(4 * n, n, f32)] * 4
        + [
            shape(4 * n, wide, bf16),
            shape(4, n, wide, bf16),
            shape(4, 1, n, jnp.int32),
        ],
        scratch=[pltpu.VMEM((4 * n, 4 * n), f32)],
        flops=2 * tile * wide,
    )
    pieces = [partial[0]] + [shift_y(partial[t], t) for t in (1, 2, 3)]
    e_low, low_stats, low_tops = call(
        low_kernel, [ids, level_weight], [p, q, pos],
        [shape(LOW, 4, 4 * n, n, f32), shape(4, 8, n, f32), shape(4, 8, n, f32)],
        flops=2 * tile * wide,
    )
    e_high, message, tops = call(
        owner_kernel, [ids, level_weight], [*pieces, pos, low_stats],
        [shape(2, 4 * n, n, f32), shape(8, 40, n, f32), shape(8, n, f32)],
    )
    stats = lax.all_to_all(message, "batch", 0, 0, axis_index_groups=XZH_GROUPS)
    *tails, rates = call(
        tail_kernel, [ids, level_weight], [stats, low_tops, tops, e_high, pos],
        [shape(4 * n + EXTRA, n, bf16)] * 4 + [shape(4, 8, n, f32)],
    )
    tails = [tails[0]] + [shift_y(tails[t], t) for t in (1, 2, 3)]
    gq_low, gp_low = call(
        low_grad_kernel, [ids, level_weight], [e_low, rates, pos, p, q],
        [shape(4 * n, wide, bf16)] * 2,
        scratch=[pltpu.VMEM((LOW, 4 * n, 4 * n), bf16)],
        flops=4 * tile * wide, grant=12,
    )
    gq0, gq1, gq2, gq3, gp_own, message, row = call(
        grad_kernel, [ids], [*tails, gq_low, gp_low, p, q],
        [shape(n, wide, f32)]
        + [shape(n, wide, bf16)] * 3
        + [
            shape(4 * n, width, f32),
            shape(4 * n + EXTRA, width, bf16),
            shape(8, n, f32),
        ],
        scratch=[pltpu.VMEM((4 * n, 4 * n), bf16), pltpu.VMEM((4 * n, wide), f32)],
        flops=4 * tile * wide, grant=12,
    )
    gq = [shift_x(g, -s) for s, g in enumerate((gq1, gq2, gq3), 1)]
    gp_own, *messages, row = call(
        core_sum_kernel, [ids], [gp_own, row, swap_core(message)],
        [shape(n, width, f32)] + [shape(n + EXTRA, width, bf16)] * 3 + [shape(8, n, f32)],
    )
    gp = [shift_zl(m, -s) for s, m in enumerate(messages, 1)]
    gq_own, near, far = call(
        middle_kernel, [ids], [gq0, *gq, *messages],
        [shape(n, width, f32)] + [shape(n, width, bf16)] * 2, in_place=3,
    )
    near = move_square(near, lambda h, c: (h, 1 - c) if h == c else (1 - h, c))
    far = move_square(far, lambda h, c: None if h == c else (1 - h, 1 - c))
    grad_queries, grad_passages, loss = call(
        last_kernel, [ids], [gq_own, near, far, gp_own, row, *gp],
        [shape(n, width, bf16), shape(n, width, bf16), shape(1, 1, f32)],
    )
    return loss.reshape(()), grad_queries, grad_passages


def solution(mesh):
    in_specs = (P("batch", "feat"), P("batch", "feat"), P("batch"), P())
    out_specs = (P(), P("batch", "feat"), P("batch", "feat"))
    return jax.shard_map(
        per_device, mesh=mesh, in_specs=in_specs, out_specs=out_specs, check_vma=False
    )
```
